256 devices in a mesh: lat: 16 (over y_hi, x, core), lon: 16 (over z, y_lo).
Axes of the slice: x: 4, y: 4 (y_hi: 2, y_lo: 2; y = y_hi * 2 + y_lo), z: 8, core: 2. Of those that a mesh axis runs over, the one named last changes fastest.
Arguments:
- tokens: bfloat16 [2, 96, 384, 512], P(None, 'lat', 'lon'), may hold values from -6 to 6
- cotangent: bfloat16 [2, 96, 384, 512], P(None, 'lat', 'lon'), may hold values from -6 to 6
- w_qkv: bfloat16 [512, 1536], replicated, may hold values from -6 to 6
- w_proj: bfloat16 [512, 512], replicated, may hold values from -0.25 to 0.25
- w_fc1: bfloat16 [512, 2048], replicated, may hold values from -0.25 to 0.25
- w_fc2: bfloat16 [2048, 512], replicated, may hold values from -0.125 to 0.125
Outputs:
- block_out: bfloat16 [2, 96, 384, 512], P(None, 'lat', 'lon')
- input_grad: bfloat16 [2, 96, 384, 512], P(None, 'lat', 'lon')
- weight_grads: float32 [24576, 128], P(('lat', 'lon'))
The draws below stay inside these ranges and needn't reach their ends.
All inputs are finite; a program needn't handle non-finite values.
Results may differ from the reference program's by a relative error of at most 0.017.
Values may be sent and summed in bfloat16 or wider, within the bound.
A program may use at most 128 MiB of HBM per device.

```python
import jax
import jax.numpy as jnp
from jax import lax

D = 512
H = 16
HD = 32
FF = 2048
LEVELS = 2
LAT = 96
LON = 384
TOKENS = 73728


def draw_w_qkv(key, part):
    key = jax.random.fold_in(key, 7)
    base = jax.random.truncated_normal(key, -4.0, 4.0, (D, 3 * D), jnp.float32) * D ** (-0.5)
    return base.astype(jnp.bfloat16)


def levels(own_key, shape, split, least, top_value):
    def one(position, parts):
        steps = jax.random.uniform(jax.random.fold_in(jax.random.fold_in(own_key, 6), position), (parts,), jnp.float32, least / len(split), top_value / len(split))
        return jnp.repeat(jnp.exp(steps), shape[position] // parts).reshape((-1,) + (1,) * (len(shape) - position - 1))

    gain = one(*split[0])
    for cut in split[1:]:
        gain = gain * one(*cut)
    return gain


def noise(own_key, dims, spread, reach, split=(), kind=jnp.bfloat16):
    entries = spread * jax.random.normal(own_key, dims, jnp.float32)
    if split:
        entries = entries * levels(own_key, dims, split, -0.22, 0.18)
    return jnp.clip(entries, -reach, reach).astype(kind)


def setup_inputs(seed: int = 0) -> dict:
    key_list = jax.random.split(jax.random.key(seed), 7)
    return {
        "tokens": noise(key_list[0], (LEVELS, LAT, LON, D), 1.0, 6.0, ((1, 16), (2, 16))),
        "cotangent": noise(key_list[1], (LEVELS, LAT, LON, D), 1.0, 6.0, ((1, 16), (2, 16))),
        "w_qkv": draw_w_qkv(jax.random.fold_in(key_list[6], 71), 0),
        "w_proj": noise(key_list[3], (D, D), D ** -0.5, 0.25),
        "w_fc1": noise(key_list[4], (D, FF), D ** -0.5, 0.25),
        "w_fc2": noise(key_list[5], (FF, D), FF ** -0.5, 0.125),
    }


epsilon = 1e-05
neg_fill = -1e+30
inv_root_two = 0.7071067811865476
inv_root_tau = 0.3989422804014327

def normalize(values):
    centre = values - lax.optimization_barrier(jnp.mean(values, axis=-1, keepdims=True))
    inv_std = lax.rsqrt(lax.optimization_barrier(jnp.mean(centre * centre, axis=-1, keepdims=True)) + epsilon)
    return (centre * inv_std, inv_std)

def norm_back(upstream, normed, inv_std):
    mean_up = lax.optimization_barrier(jnp.mean(upstream, axis=-1, keepdims=True))
    mean_dot = lax.optimization_barrier(jnp.mean(upstream * normed, axis=-1, keepdims=True))
    return inv_std * (upstream - mean_up - normed * mean_dot)

def gelu_value(hidden):
    return 0.5 * hidden * (1.0 + lax.erf(hidden * inv_root_two))

def gelu_slope(hidden):
    return 0.5 * (1.0 + lax.erf(hidden * inv_root_two)) + hidden * inv_root_tau * jnp.exp(-0.5 * hidden * hidden)

def to_windows(grid_arr):
    level_count, row_count, col_count, features = grid_arr.shape
    split_grid = grid_arr.reshape(level_count, row_count // 6, 6, col_count // 12, 12, features)
    return split_grid.transpose(1, 3, 0, 2, 4, 5).reshape(row_count // 6 * (col_count // 12), level_count * 72, features)

def from_windows(windowed, grid_shape):
    level_count, row_count, col_count = grid_shape
    features = windowed.shape[-1]
    split_grid = windowed.reshape(row_count // 6, col_count // 12, level_count, 6, 12, features)
    return split_grid.transpose(2, 0, 3, 1, 4, 5).reshape(level_count, row_count, col_count, features)

def as_f32(values):
    return values.astype(jnp.float32)

def attend_forward(normed_w, allowed, w_qkv, w_proj):
    win_count, window_len, features = normed_w.shape
    projected = jnp.einsum('wsd,de->wse', as_f32(normed_w), as_f32(w_qkv))
    queries = (projected[..., :D] * HD ** (-0.5)).astype(jnp.bfloat16).reshape(win_count, window_len, H, HD)
    key_heads = projected[..., D:2 * D].astype(jnp.bfloat16).reshape(win_count, window_len, H, HD)
    value_heads = projected[..., 2 * D:].astype(jnp.bfloat16).reshape(win_count, window_len, H, HD)
    scores = jnp.einsum('wqhe,wkhe->whqk', as_f32(queries), as_f32(key_heads))
    scores = jnp.where(allowed[:, None], scores, neg_fill)
    row_max = lax.optimization_barrier(jnp.max(scores, axis=-1, keepdims=True))
    exp_scores = jnp.exp(scores - row_max)
    attn_probs = exp_scores / lax.optimization_barrier(jnp.sum(exp_scores, axis=-1, keepdims=True))
    attn_round = attn_probs.astype(jnp.bfloat16)
    context = jnp.einsum('whqk,wkhe->wqhe', as_f32(attn_round), as_f32(value_heads))
    context = context.astype(jnp.bfloat16).reshape(win_count, window_len, D)
    branch_w = jnp.einsum('wsd,de->wse', as_f32(context), as_f32(w_proj)).astype(jnp.bfloat16)
    return (branch_w, (queries, key_heads, value_heads, attn_probs, attn_round, context))

def attend_backward(grad_w, normed_w, saved_fwd, w_qkv, w_proj):
    queries, key_heads, value_heads, attn_probs, attn_round, context = saved_fwd
    win_count, window_len = (queries.shape[0], queries.shape[1])
    grad_proj = jnp.einsum('wsd,wse->de', as_f32(context), as_f32(grad_w))
    grad_context = jnp.einsum('wse,de->wsd', as_f32(grad_w), as_f32(w_proj)).astype(jnp.bfloat16)
    grad_context = grad_context.reshape(win_count, window_len, H, HD)
    grad_probs = jnp.einsum('wqhe,wkhe->whqk', as_f32(grad_context), as_f32(value_heads))
    grad_values = jnp.einsum('whqk,wqhe->wkhe', as_f32(attn_round), as_f32(grad_context)).astype(jnp.bfloat16)
    grad_scores = attn_probs * (grad_probs - lax.optimization_barrier(jnp.sum(grad_probs * attn_probs, axis=-1, keepdims=True)))
    grad_scores = grad_scores.astype(jnp.bfloat16)
    grad_queries = (jnp.einsum('whqk,wkhe->wqhe', as_f32(grad_scores), as_f32(key_heads)) * HD ** (-0.5)).astype(jnp.bfloat16)
    grad_keys = jnp.einsum('whqk,wqhe->wkhe', as_f32(grad_scores), as_f32(queries)).astype(jnp.bfloat16)
    grad_mixed = jnp.concatenate([grad_queries, grad_keys, grad_values], axis=2).reshape(win_count, window_len, 3 * D)
    grad_qkv = jnp.einsum('wsd,wse->de', as_f32(normed_w), as_f32(grad_mixed))
    grad_normed = jnp.einsum('wse,de->wsd', as_f32(grad_mixed), as_f32(w_qkv)).astype(jnp.bfloat16)
    return (grad_normed, grad_qkv, grad_proj)

def feed_forward(residual, grad_out, w_fc1, w_fc2):
    resid32 = residual.astype(jnp.float32)
    normed, inv_std = normalize(resid32)
    normed_b = normed.astype(jnp.bfloat16)
    hidden = jnp.dot(normed_b, w_fc1, preferred_element_type=jnp.float32)
    active = gelu_value(hidden).astype(jnp.bfloat16)
    output = (resid32 + jnp.dot(active, w_fc2, preferred_element_type=jnp.float32)).astype(jnp.bfloat16)
    grad_act = jnp.dot(grad_out, w_fc2.T, preferred_element_type=jnp.float32)
    grad_hidden = (grad_act * gelu_slope(hidden)).astype(jnp.bfloat16)
    grad_fc2t = jnp.dot(grad_out.T, active, preferred_element_type=jnp.float32)
    grad_fc1 = jnp.dot(normed_b.T, grad_hidden, preferred_element_type=jnp.float32)
    grad_normed = jnp.dot(grad_hidden, w_fc1.T, preferred_element_type=jnp.float32)
    grad_resid = (grad_out.astype(jnp.float32) + norm_back(grad_normed, normed, inv_std)).astype(jnp.bfloat16)
    return (output, grad_resid, grad_fc1, grad_fc2t)

def block_pass(inputs, grad_out, beyond, w_qkv, w_proj, w_fc1, w_fc2):
    level_count, row_count, col_count, features = inputs.shape
    grid_shape = (level_count, row_count, col_count)
    side_grid = jnp.broadcast_to(beyond.astype(jnp.int32)[None, :, None, None], (level_count, row_count, col_count, 1))
    side_win = to_windows(side_grid)[..., 0]
    allowed = side_win[:, :, None] == side_win[:, None, :]
    inputs32 = inputs.astype(jnp.float32)
    normed1, inv_std1 = normalize(inputs32)
    windows_in = to_windows(normed1.astype(jnp.bfloat16))
    branch_w, saved_fwd = attend_forward(windows_in, allowed, w_qkv, w_proj)
    branch = from_windows(branch_w, grid_shape)
    residual = (inputs32 + branch.astype(jnp.float32)).astype(jnp.bfloat16)
    output, grad_resid, grad_fc1, grad_fc2t = feed_forward(residual.reshape(-1, features), grad_out.reshape(-1, features), w_fc1, w_fc2)
    grad_resid = grad_resid.reshape(inputs.shape)
    grad_norm_w, grad_qkv, grad_proj = attend_backward(to_windows(grad_resid), windows_in, saved_fwd, w_qkv, w_proj)
    grad_norm = from_windows(grad_norm_w, grid_shape)
    grad_in = (grad_resid.astype(jnp.float32) + norm_back(grad_norm.astype(jnp.float32), normed1, inv_std1)).astype(jnp.bfloat16)
    grads = jnp.concatenate([grad_qkv, grad_proj, grad_fc1, grad_fc2t], axis=1)
    return (output.reshape(inputs.shape), grad_in, grads)

def reference(tokens, cotangent, w_qkv, w_proj, w_fc1, w_fc2):
    rolled_x = jnp.roll(tokens, (-3, -6), axis=(1, 2))
    rolled_g = jnp.roll(cotangent, (-3, -6), axis=(1, 2))
    band_count = LAT // 6
    bands_x = rolled_x.reshape(LEVELS, band_count, 6, LON, D).transpose(1, 0, 2, 3, 4)
    bands_g = rolled_g.reshape(LEVELS, band_count, 6, LON, D).transpose(1, 0, 2, 3, 4)
    band_ids = jnp.arange(band_count, dtype=jnp.int32)

    def band_step(grad_total, band_item):
        band_x, band_g, band_id = band_item
        row_ids = band_id * 6 + jnp.arange(6, dtype=jnp.int32)
        output, grad_in, grads = block_pass(band_x, band_g, row_ids >= LAT - 3, w_qkv, w_proj, w_fc1, w_fc2)
        return (grad_total + grads, (output, grad_in))
    grad_start = jnp.zeros((D, 4 * D + 2 * FF), jnp.float32)
    grad_total, stacked = lax.scan(band_step, grad_start, (bands_x, bands_g, band_ids))
    out_bands, gin_bands = stacked
    block_out = out_bands.transpose(1, 0, 2, 3, 4).reshape(LEVELS, LAT, LON, D)
    input_grad = gin_bands.transpose(1, 0, 2, 3, 4).reshape(LEVELS, LAT, LON, D)
    block_out = jnp.roll(block_out, (3, 6), axis=(1, 2))
    input_grad = jnp.roll(input_grad, (3, 6), axis=(1, 2))
    weight_grads = (grad_total * TOKENS ** (-0.5)).reshape(-1, 128)
    return (block_out, input_grad, weight_grads)
```

```python
import jax
import jax.numpy as jnp
from jax import lax
from jax.experimental import pallas as pl
from jax.experimental.pallas import tpu as pltpu
from jax.sharding import PartitionSpec as P

MESH = pl.DeviceIdType.MESH
H = 16
D = 512
NT = 288
F32 = jnp.float32
BF16 = jnp.bfloat16

epsilon = 1e-05
neg_fill = -1e30
inv_root_two = 0.7071067811865476
inv_root_tau = 0.3989422804014327
grad_scale = 73728 ** (-0.5)


class Place:
    def __init__(self):
        lat, lon = lax.axis_index("lat"), lax.axis_index("lon")
        self.core = lax.rem(lat, 2)
        self.x = lax.rem(lax.div(lat, 2), 4)
        self.y = lax.div(lat, 8) * 2 + lax.rem(lon, 2)
        self.z = lax.div(lon, 2)

    def shifted(self, axis=None, by=0):
        x, y, z, core = self.x, self.y, self.z, self.core
        if axis == "x":
            x = lax.rem(x + by, 4)
        elif axis == "y":
            y = lax.rem(y + by, 4)
        elif axis == "z":
            z = lax.rem(z + by, 8)
        elif axis == "core":
            core = 1 - core
        return (lax.div(y, 2) * 8 + x * 2 + core, z * 2 + lax.rem(y, 2))


SIZES = {"x": 4, "y": 4, "z": 8}
ORDERS = (("x", "y", "z"), ("y", "x", "z"), ("z", "x", "y"))


def row_order(place, order, own_core):
    p = lax.broadcasted_iota(jnp.int32, (256, 1), 0)
    r = p & 1
    rest = p >> 1
    off = {}
    for axis in reversed(order):
        bits = 3 if axis == "z" else 2
        off[axis] = rest & (SIZES[axis] - 1)
        rest = rest >> bits
    x = (off["x"] + place.x) & 3
    y = (off["y"] + place.y) & 3
    z = (off["z"] + place.z) & 7
    core = place.core if own_core else 1 - place.core
    row = ((((((y >> 1) * 4 + x) * 2 + core) * 8 + z) * 2 + (y & 1)) * 2) + r
    columns = lax.broadcasted_iota(jnp.int32, (256, D), 1)
    return jnp.where(columns == row, 1.0, 0.0).astype(BF16)


def dot(a, b, ca=1, cb=0):
    return lax.dot_general(a, b, (((ca,), (cb,)), ((), ())), preferred_element_type=F32)


class Copies:
    def __init__(self, send_sems, recv_sems):
        self.send_sems, self.recv_sems, self.used, self.started = send_sems, recv_sems, 0, []

    def send(self, src, dst, target):
        k = self.used
        self.used += 1
        copy = pltpu.make_async_remote_copy(
            src_ref=src,
            dst_ref=dst,
            send_sem=self.send_sems.at[k],
            recv_sem=self.recv_sems.at[k],
            device_id=target,
            device_id_type=MESH,
        )
        copy.start()
        self.started.append(copy)
        return copy

    def drain(self):
        for copy in self.started:
            copy.wait_send()


def add_into(acc, rows, cols, arrived, step=16):
    start, count = rows
    c0, cn = cols
    step = min(step, count)

    @pl.loop(0, count // step)
    def _(i):
        here = pl.ds(pl.multiple_of(start + i * step, step), step)
        there = pl.ds(pl.multiple_of(i * step, step), step)
        acc[here, c0 : c0 + cn] += arrived[there, :].astype(F32)


def cast_from(acc, rows, cols, out, step=16):
    start, count = rows
    c0, cn = cols
    step = min(step, count)

    @pl.loop(0, count // step)
    def _(i):
        here = pl.ds(pl.multiple_of(start + i * step, step), step)
        there = pl.ds(pl.multiple_of(i * step, step), step)
        out[there, :] = acc[here, c0 : c0 + cn].astype(BF16)


def sum_part(place, copies, part, width, bufs, acc, sent0, arrive0, emit):
    order = ORDERS[part]
    first, second, third = order
    n = SIZES[first]
    rows = 256 // n
    half = width // 2
    yield
    sent0.wait_recv()
    add_into(acc, (0, 256), (0, width), arrive0)
    ring_send, ring_recv = bufs["ring_send"], bufs["ring_recv"]
    for s in range(n // 2):
        kp, km = n // 2 - s, (n // 2 + s) % n
        if s == 0:
            plus_cols, minus_cols = (0, half), (half, half)
        else:
            plus_cols = minus_cols = (0, width)
        pend = []
        for way, chunk, cols, by in ((0, kp, plus_cols, 1), (1, km, minus_cols, n - 1)):
            span = (s * rows, rows)
            out = ring_send.at[way, pl.ds(s * rows, rows), pl.ds(0, cols[1])]
            inn = ring_recv.at[way, pl.ds(s * rows, rows), pl.ds(0, cols[1])]
            cast_from(acc, (chunk * rows, rows), cols, out)
            pend.append((copies.send(out, inn, place.shifted(first, by)), inn, cols))
        yield
        for way, (copy, inn, cols) in enumerate(pend):
            chunk = kp - 1 if way == 0 else (km + 1) % n
            copy.wait_recv()
            add_into(acc, (chunk * rows, rows), cols, inn)
    n2 = 4
    rows2 = rows // n2
    pend = []
    for j in range(1, n2):
        inn = bufs["mid_recv"].at[pl.ds((j - 1) * rows2, rows2)]
        if rows2 >= 16:
            out = bufs["mid_send"].at[pl.ds((j - 1) * rows2, rows2)]
            cast_from(acc, (j * rows2, rows2), (0, width), out)
        else:
            out = acc.at[pl.ds(j * rows2, rows2)]
        pend.append((copies.send(out, inn, place.shifted(second, j)), inn))
    yield
    total = acc[0:rows2, :]
    for copy, inn in pend:
        copy.wait_recv()
        total = total + inn[...].astype(F32)
    n3 = SIZES[third]
    tiles = width // 128
    last_send, last_recv = bufs["last_send"], bufs["last_recv"]
    for c in range(tiles):
        last_send[pl.ds(c, 2 * n3, stride=tiles), :] = total[:, c * 128 : (c + 1) * 128]
    pend = []
    for j in range(1, n3):
        out = last_send.at[pl.ds(j * 2 * tiles, 2 * tiles)]
        inn = last_recv.at[pl.ds((j - 1) * 2 * tiles, 2 * tiles)]
        pend.append((copies.send(out, inn, place.shifted(third, j)), inn))
    yield
    done = last_send[0 : 2 * tiles, :]
    for copy, inn in pend:
        copy.wait_recv()
        done = done + inn[...]
    done = done * grad_scale
    for r in range(2):
        for local, whole, count in emit:
            bufs["out"][r * 48 + whole : r * 48 + whole + count, :] = done[
                r * tiles + local : r * tiles + local + count, :
            ]


def part_scratch(width):
    out = []
    for order in ORDERS:
        n = SIZES[order[0]]
        rows = 256 // n
        n3 = SIZES[order[2]]
        tiles = width // 128
        wide = rows // 4 >= 16
        out.append(
            dict(
                ring_send=pltpu.VMEM((2, n // 2 * rows, width), BF16),
                ring_recv=pltpu.VMEM((2, n // 2 * rows, width), BF16),
                mid_send=pltpu.VMEM((3 * rows // 4, width), BF16) if wide else pltpu.VMEM((8, 128), F32),
                mid_recv=pltpu.VMEM((3 * rows // 4, width), BF16 if wide else F32),
                last_send=pltpu.VMEM((n3 * 2 * tiles, 128), F32),
                last_recv=pltpu.VMEM(((n3 - 1) * 2 * tiles, 128), F32),
            )
        )
    return out


def batch_scratch(width):
    return dict(
        send0=pltpu.VMEM((3, 256, width), BF16),
        recv0=pltpu.VMEM((3, 256, width), BF16),
        acc=pltpu.VMEM((3, 256, width), F32),
        parts=part_scratch(width),
    )


def greet(place):
    barrier = pltpu.get_barrier_semaphore()
    peers = [place.shifted("core")]
    for axis in ("x", "y", "z"):
        peers += [place.shifted(axis, by) for by in range(1, SIZES[axis])]
    for peer in peers:
        pl.semaphore_signal(barrier, inc=1, device_id=peer, device_id_type=MESH)
    pl.semaphore_wait(barrier, len(peers))


LATE = (
    (("qkv", 0, 512, 0),),
    (("qkv", 512, 512, 4),),
    (("qkv", 1024, 512, 8),),
)
EARLY = (
    (("fc1", 0, 1536, 16),),
    (("fc1", 1536, 512, 28), ("fc2", 0, 1024, 32)),
    (("fc2", 1024, 1024, 40), ("proj", 0, 512, 12)),
)


def start_batch(place, copies, split, width, scr, out_ref, pairs, orders_ref, lhs_ref):
    gens = []
    for part in range(3):
        acc = scr["acc"].at[part]
        send0 = scr["send0"].at[part]
        recv0 = scr["recv0"].at[part]
        for own in (0, 1):
            at = 0
            for name, begin, count, _ in split[part]:
                left, right = pairs[name]
                lhs_ref[...] = dot(orders_ref[2 * part + own], left[...], 1, 1).astype(BF16)
                base = at

                @pl.loop(0, count // 256)
                def _(i):
                    src = pl.ds(pl.multiple_of(begin + i * 256, 256), 256)
                    dst = pl.ds(pl.multiple_of(base + i * 256, 256), 256)
                    value = dot(lhs_ref[...], right[:, src])
                    if own:
                        acc[:, dst] = value
                    else:
                        send0[:, dst] = value.astype(BF16)

                at += count
            if not own:
                copy = copies.send(send0, recv0, place.shifted("core"))
        emit, at = [], 0
        for _, _, count, whole in split[part]:
            emit.append((at // 128, whole, count // 128))
            at += count
        bufs = dict(scr["parts"][part], out=out_ref)
        gens.append(sum_part(place, copies, part, width, bufs, acc, copy, recv0, emit))
    return gens


def tick(gens):
    left = []
    for gen in gens:
        try:
            next(gen)
            left.append(gen)
        except StopIteration:
            pass
    return left


def grads_kernel(n1, gm, ctx, gr, n2, gh, ct, act, out_ref, early, late, orders_ref, lhs_ref, send_sems, recv_sems):
    place = Place()
    copies = Copies(send_sems, recv_sems)
    greet(place)
    for part, order in enumerate(ORDERS):
        for own in (0, 1):
            orders_ref[2 * part + own] = row_order(place, order, own)
    pairs = dict(qkv=(n1, gm), proj=(ctx, gr), fc1=(n2, gh), fc2=(ct, act))
    gens = start_batch(place, copies, EARLY, 1536, early, out_ref, pairs, orders_ref, lhs_ref)
    gens = tick(gens)
    gens = tick(gens)
    gens += start_batch(place, copies, LATE, 512, late, out_ref, pairs, orders_ref, lhs_ref)
    while gens:
        gens = tick(gens)
    copies.drain()


def grads_call(*operands):
    vmem = pl.BlockSpec(memory_space=pltpu.VMEM)
    return pl.pallas_call(
        grads_kernel,
        out_shape=jax.ShapeDtypeStruct((96, 128), F32),
        in_specs=[vmem] * 8,
        out_specs=vmem,
        scratch_shapes=[
            batch_scratch(1536),
            batch_scratch(512),
            pltpu.VMEM((6, 256, D), BF16),
            pltpu.VMEM((256, NT), BF16),
            pltpu.SemaphoreType.DMA((100,)),
            pltpu.SemaphoreType.DMA((100,)),
        ],
        compiler_params=pltpu.CompilerParams(
            collective_id=0, has_side_effects=True, vmem_limit_bytes=56 * 1024 * 1024
        ),
    )(*operands)


def passed_along(value, axis, steps):
    count = lax.axis_size(axis)
    pairs = [(source, (source + steps) % count) for source in range(count)]
    return lax.ppermute(value, axis, pairs)


def normalize(values):
    centre = values - jnp.mean(values, axis=-1, keepdims=True)
    inv_std = lax.rsqrt(jnp.mean(centre * centre, axis=-1, keepdims=True) + epsilon)
    return (centre * inv_std, inv_std)


def norm_back(upstream, normed, inv_std):
    mean_up = jnp.mean(upstream, axis=-1, keepdims=True)
    mean_dot = jnp.mean(upstream * normed, axis=-1, keepdims=True)
    return inv_std * (upstream - mean_up - normed * mean_dot)


def gelu_value(hidden):
    return 0.5 * hidden * (1.0 + lax.erf(hidden * inv_root_two))


def gelu_slope(hidden):
    return 0.5 * (1.0 + lax.erf(hidden * inv_root_two)) + hidden * inv_root_tau * jnp.exp(
        -0.5 * hidden * hidden
    )


def to_windows(grid_arr):
    level_count, row_count, col_count, features = grid_arr.shape
    split_grid = grid_arr.reshape(level_count, row_count // 6, 6, col_count // 12, 12, features)
    return split_grid.transpose(1, 3, 0, 2, 4, 5).reshape(
        row_count // 6 * (col_count // 12), level_count * 72, features
    )


def from_windows(windowed, grid_shape):
    level_count, row_count, col_count = grid_shape
    features = windowed.shape[-1]
    split_grid = windowed.reshape(row_count // 6, col_count // 12, level_count, 6, 12, features)
    return split_grid.transpose(2, 0, 3, 1, 4, 5).reshape(
        level_count, row_count, col_count, features
    )


def roll_lat(grid_arr, direction):
    if direction > 0:
        sending = grid_arr[..., :3, :, :]
    else:
        sending = grid_arr[..., -3:, :, :]
    arrived = passed_along(sending, "lat", -direction)
    if direction > 0:
        return jnp.concatenate([grid_arr[..., 3:, :, :], arrived], axis=-3)
    return jnp.concatenate([arrived, grid_arr[..., :-3, :, :]], axis=-3)


def roll_lon(grid_arr, direction):
    if direction > 0:
        sending = grid_arr[..., :6, :]
    else:
        sending = grid_arr[..., -6:, :]
    arrived = passed_along(sending, "lon", -direction)
    if direction > 0:
        return jnp.concatenate([grid_arr[..., 6:, :], arrived], axis=-2)
    return jnp.concatenate([arrived, grid_arr[..., :-6, :]], axis=-2)


def roll_in(grid_arr):
    return roll_lon(roll_lat(grid_arr, 1), 1)


def roll_out(grid_arr):
    return roll_lat(roll_lon(grid_arr, -1), -1)


def attend_forward(normed_w, allowed, w_qkv, w_proj):
    win_count, window_len, features = normed_w.shape
    head_size = features // H
    projected = jnp.einsum("wsd,de->wse", normed_w, w_qkv, preferred_element_type=jnp.float32)
    queries = (
        (projected[..., :features] * head_size ** (-0.5))
        .astype(jnp.bfloat16)
        .reshape(win_count, window_len, H, head_size)
    )
    key_heads = (
        projected[..., features : 2 * features]
        .astype(jnp.bfloat16)
        .reshape(win_count, window_len, H, head_size)
    )
    value_heads = (
        projected[..., 2 * features :]
        .astype(jnp.bfloat16)
        .reshape(win_count, window_len, H, head_size)
    )
    scores = jnp.einsum("wqhe,wkhe->whqk", queries, key_heads, preferred_element_type=jnp.float32)
    scores = jnp.where(allowed[:, None], scores, neg_fill)
    row_max = jnp.max(scores, axis=-1, keepdims=True)
    exp_scores = jnp.exp(scores - row_max)
    attn_probs = exp_scores / jnp.sum(exp_scores, axis=-1, keepdims=True)
    attn_round = attn_probs.astype(jnp.bfloat16)
    context = jnp.einsum(
        "whqk,wkhe->wqhe", attn_round, value_heads, preferred_element_type=jnp.float32
    )
    context = context.astype(jnp.bfloat16).reshape(win_count, window_len, features)
    branch_w = jnp.einsum(
        "wsd,de->wse", context, w_proj, preferred_element_type=jnp.float32
    ).astype(jnp.bfloat16)
    return (branch_w, (queries, key_heads, value_heads, attn_probs, attn_round, context))


def attend_backward(grad_w, normed_w, saved_fwd, w_qkv, w_proj):
    queries, key_heads, value_heads, attn_probs, attn_round, context = saved_fwd
    win_count, window_len, heads_n, head_size = queries.shape
    grad_context = jnp.einsum(
        "wse,de->wsd", grad_w, w_proj, preferred_element_type=jnp.float32
    ).astype(jnp.bfloat16)
    grad_context = grad_context.reshape(win_count, window_len, heads_n, head_size)
    grad_probs = jnp.einsum(
        "wqhe,wkhe->whqk", grad_context, value_heads, preferred_element_type=jnp.float32
    )
    grad_values = jnp.einsum(
        "whqk,wqhe->wkhe", attn_round, grad_context, preferred_element_type=jnp.float32
    ).astype(jnp.bfloat16)
    grad_scores = attn_probs * (
        grad_probs - jnp.sum(grad_probs * attn_probs, axis=-1, keepdims=True)
    )
    grad_scores = grad_scores.astype(jnp.bfloat16)
    grad_queries = jnp.einsum(
        "whqk,wkhe->wqhe", grad_scores, key_heads, preferred_element_type=jnp.float32
    )
    grad_queries = (grad_queries * head_size ** (-0.5)).astype(jnp.bfloat16)
    grad_keys = jnp.einsum(
        "whqk,wqhe->wkhe", grad_scores, queries, preferred_element_type=jnp.float32
    ).astype(jnp.bfloat16)
    grad_mixed = jnp.concatenate([grad_queries, grad_keys, grad_values], axis=2).reshape(
        win_count, window_len, 3 * heads_n * head_size
    )
    grad_normed = jnp.einsum(
        "wse,de->wsd", grad_mixed, w_qkv, preferred_element_type=jnp.float32
    ).astype(jnp.bfloat16)
    return (grad_normed, grad_mixed)


def feed_forward(residual, grad_out, w_fc1, w_fc2):
    resid32 = residual.astype(jnp.float32)
    normed, inv_std = normalize(resid32)
    normed_b = normed.astype(jnp.bfloat16)
    hidden = jnp.dot(normed_b, w_fc1, preferred_element_type=jnp.float32)
    active = gelu_value(hidden).astype(jnp.bfloat16)
    output = (resid32 + jnp.dot(active, w_fc2, preferred_element_type=jnp.float32)).astype(
        jnp.bfloat16
    )
    grad_act = jnp.einsum("rd,fd->rf", grad_out, w_fc2, preferred_element_type=jnp.float32)
    grad_hidden = (grad_act * gelu_slope(hidden)).astype(jnp.bfloat16)
    grad_normed = jnp.einsum("rf,df->rd", grad_hidden, w_fc1, preferred_element_type=jnp.float32)
    grad_resid = (grad_out.astype(jnp.float32) + norm_back(grad_normed, normed, inv_std)).astype(
        jnp.bfloat16
    )
    return (output, grad_resid, normed_b, grad_hidden, active)


def on_device(tokens, cotangent, w_qkv, w_proj, w_fc1, w_fc2):
    level_count, row_count, col_count, features = tokens.shape
    lat_count = lax.axis_size("lat")
    total_tokens = level_count * row_count * col_count * lat_count * lax.axis_size("lon")
    grid_shape = (level_count, row_count, col_count)
    row_ids = lax.axis_index("lat") * row_count + jnp.arange(row_count, dtype=jnp.int32)
    beyond = (row_ids >= row_count * lat_count - 3).astype(jnp.int32)
    side_grid = jnp.broadcast_to(
        beyond[None, :, None, None], (level_count, row_count, col_count, 1)
    )
    side_win = to_windows(side_grid)[..., 0]
    allowed = side_win[:, :, None] == side_win[:, None, :]
    inputs, grad_out = (tokens, cotangent)
    inputs32 = inputs.astype(jnp.float32)
    normed1, inv_std1 = normalize(inputs32)
    normed1_b = normed1.astype(jnp.bfloat16)
    attn_input = roll_in(normed1_b)
    windows_in = to_windows(attn_input)
    branch_w, saved_fwd = attend_forward(windows_in, allowed, w_qkv, w_proj)
    branch = from_windows(branch_w, grid_shape)
    branch = roll_out(branch)
    residual = (inputs32 + branch.astype(jnp.float32)).astype(jnp.bfloat16)
    output, grad_resid, normed2_b, grad_hidden, active = feed_forward(
        residual.reshape(-1, features), grad_out.reshape(-1, features), w_fc1, w_fc2
    )
    grad_resid = grad_resid.reshape(level_count, row_count, col_count, features)
    grad_branch = roll_in(grad_resid)
    grad_branch_w = to_windows(grad_branch)
    grad_norm_w, grad_mixed = attend_backward(
        grad_branch_w, windows_in, saved_fwd, w_qkv, w_proj
    )
    grad_norm = from_windows(grad_norm_w, grid_shape)
    grad_norm = roll_out(grad_norm)
    grad_in = (
        grad_resid.astype(jnp.float32) + norm_back(grad_norm.astype(jnp.float32), normed1, inv_std1)
    ).astype(jnp.bfloat16)
    output = output.reshape(level_count, row_count, col_count, features)
    flat = lambda v: v.reshape(NT, -1)
    weight_grads = grads_call(
        flat(windows_in), flat(grad_mixed), flat(saved_fwd[5]), flat(grad_branch_w),
        normed2_b, grad_hidden, flat(grad_out), active,
    )
    return (output, grad_in, weight_grads)


def solution(mesh):
    return jax.shard_map(
        on_device,
        mesh=mesh,
        in_specs=(P(None, "lat", "lon", None), P(None, "lat", "lon", None), P(), P(), P(), P()),
        out_specs=(
            P(None, "lat", "lon", None),
            P(None, "lat", "lon", None),
            P(("lat", "lon"), None),
        ),
        check_vma=False,
    )
```

```python
import jax
import jax.numpy as jnp
from jax import lax
from jax.experimental import pallas as pl
from jax.experimental.pallas import tpu as pltpu
from jax.sharding import PartitionSpec as P

MESH = pl.DeviceIdType.MESH
H = 16
D = 512
NT = 288
F32 = jnp.float32
BF16 = jnp.bfloat16

epsilon = 1e-05
neg_fill = -1e30
inv_root_two = 0.7071067811865476
inv_root_tau = 0.3989422804014327
grad_scale = 73728 ** (-0.5)


class Place:
    def __init__(self):
        lat, lon = lax.axis_index("lat"), lax.axis_index("lon")
        self.lat, self.lon = lat, lon
        self.core = lax.rem(lat, 2)
        self.x = lax.rem(lax.div(lat, 2), 4)
        self.y = lax.div(lat, 8) * 2 + lax.rem(lon, 2)
        self.z = lax.div(lon, 2)

    def shifted(self, axis=None, by=0):
        x, y, z, core = self.x, self.y, self.z, self.core
        if axis == "x":
            x = lax.rem(x + by, 4)
        elif axis == "y":
            y = lax.rem(y + by, 4)
        elif axis == "z":
            z = lax.rem(z + by, 8)
        elif axis == "core":
            core = 1 - core
        return (lax.div(y, 2) * 8 + x * 2 + core, z * 2 + lax.rem(y, 2))

    def neighbour(self, by_lat, by_lon):
        return (lax.rem(self.lat + by_lat, 16), lax.rem(self.lon + by_lon, 16))


SIZES = {"x": 4, "y": 4, "z": 8}
ORDERS = (("x", "y", "z"), ("y", "x", "z"), ("z", "x", "y"))


def row_order(place, order, own_core):
    p = lax.broadcasted_iota(jnp.int32, (256, 1), 0)
    r = p & 1
    rest = p >> 1
    off = {}
    for axis in reversed(order):
        bits = 3 if axis == "z" else 2
        off[axis] = rest & (SIZES[axis] - 1)
        rest = rest >> bits
    x = (off["x"] + place.x) & 3
    y = (off["y"] + place.y) & 3
    z = (off["z"] + place.z) & 7
    core = place.core if own_core else 1 - place.core
    row = ((((((y >> 1) * 4 + x) * 2 + core) * 8 + z) * 2 + (y & 1)) * 2) + r
    columns = lax.broadcasted_iota(jnp.int32, (256, D), 1)
    return jnp.where(columns == row, 1.0, 0.0).astype(BF16)


def dot(a, b, ca=1, cb=0):
    return lax.dot_general(a, b, (((ca,), (cb,)), ((), ())), preferred_element_type=F32)


class Copies:
    def __init__(self, send_sems, recv_sems):
        self.send_sems, self.recv_sems, self.used, self.started = send_sems, recv_sems, 0, []

    def send(self, src, dst, target):
        k = self.used
        self.used += 1
        copy = pltpu.make_async_remote_copy(
            src_ref=src,
            dst_ref=dst,
            send_sem=self.send_sems.at[k],
            recv_sem=self.recv_sems.at[k],
            device_id=target,
            device_id_type=MESH,
        )
        copy.start()
        self.started.append(copy)
        return copy

    def drain(self):
        for copy in self.started:
            copy.wait_send()


def add_into(acc, rows, cols, arrived, step=16):
    start, count = rows
    c0, cn = cols
    step = min(step, count)

    @pl.loop(0, count // step)
    def _(i):
        here = pl.ds(pl.multiple_of(start + i * step, step), step)
        there = pl.ds(pl.multiple_of(i * step, step), step)
        acc[here, c0 : c0 + cn] += arrived[there, :].astype(F32)


def cast_from(acc, rows, cols, out, step=16):
    start, count = rows
    c0, cn = cols
    step = min(step, count)

    @pl.loop(0, count // step)
    def _(i):
        here = pl.ds(pl.multiple_of(start + i * step, step), step)
        there = pl.ds(pl.multiple_of(i * step, step), step)
        out[there, :] = acc[here, c0 : c0 + cn].astype(BF16)


def sum_part(place, copies, part, width, bufs, acc, sent0, arrive0, emit):
    order = ORDERS[part]
    first, second, third = order
    n = SIZES[first]
    rows = 256 // n
    half = width // 2
    yield
    sent0.wait_recv()
    add_into(acc, (0, 256), (0, width), arrive0)
    ring_send, ring_recv = bufs["ring_send"], bufs["ring_recv"]
    for s in range(n // 2):
        kp, km = n // 2 - s, (n // 2 + s) % n
        if s == 0:
            plus_cols, minus_cols = (0, half), (half, half)
        else:
            plus_cols = minus_cols = (0, width)
        pend = []
        for way, chunk, cols, by in ((0, kp, plus_cols, 1), (1, km, minus_cols, n - 1)):
            span = (s * rows, rows)
            out = ring_send.at[way, pl.ds(s * rows, rows), pl.ds(0, cols[1])]
            inn = ring_recv.at[way, pl.ds(s * rows, rows), pl.ds(0, cols[1])]
            cast_from(acc, (chunk * rows, rows), cols, out)
            pend.append((copies.send(out, inn, place.shifted(first, by)), inn, cols))
        yield
        for way, (copy, inn, cols) in enumerate(pend):
            chunk = kp - 1 if way == 0 else (km + 1) % n
            copy.wait_recv()
            add_into(acc, (chunk * rows, rows), cols, inn)
    n2 = 4
    rows2 = rows // n2
    pend = []
    for j in range(1, n2):
        inn = bufs["mid_recv"].at[pl.ds((j - 1) * rows2, rows2)]
        if rows2 >= 16:
            out = bufs["mid_send"].at[pl.ds((j - 1) * rows2, rows2)]
            cast_from(acc, (j * rows2, rows2), (0, width), out)
        else:
            out = acc.at[pl.ds(j * rows2, rows2)]
        pend.append((copies.send(out, inn, place.shifted(second, j)), inn))
    yield
    total = acc[0:rows2, :]
    for copy, inn in pend:
        copy.wait_recv()
        total = total + inn[...].astype(F32)
    n3 = SIZES[third]
    tiles = width // 128
    last_send, last_recv = bufs["last_send"], bufs["last_recv"]
    for c in range(tiles):
        last_send[pl.ds(c, 2 * n3, stride=tiles), :] = total[:, c * 128 : (c + 1) * 128]
    pend = []
    for j in range(1, n3):
        out = last_send.at[pl.ds(j * 2 * tiles, 2 * tiles)]
        inn = last_recv.at[pl.ds((j - 1) * 2 * tiles, 2 * tiles)]
        pend.append((copies.send(out, inn, place.shifted(third, j)), inn))
    yield
    done = last_send[0 : 2 * tiles, :]
    for copy, inn in pend:
        copy.wait_recv()
        done = done + inn[...]
    done = done * grad_scale
    for r in range(2):
        for local, whole, count in emit:
            bufs["out"][r * 48 + whole : r * 48 + whole + count, :] = done[
                r * tiles + local : r * tiles + local + count, :
            ]


def part_scratch(width):
    out = []
    for order in ORDERS:
        n = SIZES[order[0]]
        rows = 256 // n
        n3 = SIZES[order[2]]
        tiles = width // 128
        wide = rows // 4 >= 16
        out.append(
            dict(
                ring_send=pltpu.VMEM((2, n // 2 * rows, width), BF16),
                ring_recv=pltpu.VMEM((2, n // 2 * rows, width), BF16),
                mid_send=pltpu.VMEM((3 * rows // 4, width), BF16) if wide else pltpu.VMEM((8, 128), F32),
                mid_recv=pltpu.VMEM((3 * rows // 4, width), BF16 if wide else F32),
                last_send=pltpu.VMEM((n3 * 2 * tiles, 128), F32),
                last_recv=pltpu.VMEM(((n3 - 1) * 2 * tiles, 128), F32),
            )
        )
    return out


def batch_scratch(width):
    return dict(
        send0=pltpu.VMEM((3, 256, width), BF16),
        recv0=pltpu.VMEM((3, 256, width), BF16),
        acc=pltpu.VMEM((3, 256, width), F32),
        parts=part_scratch(width),
    )


def greet(place):
    barrier = pltpu.get_barrier_semaphore()
    peers = [place.shifted("core")]
    for axis in ("x", "y", "z"):
        peers += [place.shifted(axis, by) for by in range(1, SIZES[axis])]
    for by in (1, 15):
        peers += [place.neighbour(by, 0), place.neighbour(0, by), place.neighbour(by, by)]
    for peer in peers:
        pl.semaphore_signal(barrier, inc=1, device_id=peer, device_id_type=MESH)
    pl.semaphore_wait(barrier, len(peers))


LATE = (
    (("qkv", 0, 512, 0),),
    (("qkv", 512, 512, 4),),
    (("qkv", 1024, 512, 8),),
)
EARLY = (
    (("fc1", 0, 1536, 16),),
    (("fc1", 1536, 512, 28), ("fc2", 0, 1024, 32)),
    (("fc2", 1024, 1024, 40), ("proj", 0, 512, 12)),
)


def start_batch(place, copies, split, width, scr, out_ref, pairs, orders_ref, lhs_ref):
    gens = []
    for part in range(3):
        acc = scr["acc"].at[part]
        send0 = scr["send0"].at[part]
        recv0 = scr["recv0"].at[part]
        for own in (0, 1):
            at = 0
            for name, begin, count, _ in split[part]:
                left, right = pairs[name]
                lhs_ref[...] = dot(orders_ref[2 * part + own], left[...], 1, 1).astype(BF16)
                base = at

                @pl.loop(0, count // 256)
                def _(i):
                    src = pl.ds(pl.multiple_of(begin + i * 256, 256), 256)
                    dst = pl.ds(pl.multiple_of(base + i * 256, 256), 256)
                    value = dot(lhs_ref[...], right[:, src])
                    if own:
                        acc[:, dst] = value
                    else:
                        send0[:, dst] = value.astype(BF16)

                at += count
            if not own:
                copy = copies.send(send0, recv0, place.shifted("core"))
        emit, at = [], 0
        for _, _, count, whole in split[part]:
            emit.append((at // 128, whole, count // 128))
            at += count
        bufs = dict(scr["parts"][part], out=out_ref)
        gens.append(sum_part(place, copies, part, width, bufs, acc, copy, recv0, emit))
    return gens


def tick(gens):
    left = []
    for gen in gens:
        try:
            next(gen)
            left.append(gen)
        except StopIteration:
            pass
    return left


PACKED = 320
SECTIONS = ((112, 112, 1, 0), (224, 48, 0, 1), (272, 48, 1, 1))


def token_of(s):
    big = s < 224
    second = ((s >= 112) & (s < 224)) | (s >= 272)
    u = jnp.where(big, s - jnp.where(s >= 112, 112, 0), s - jnp.where(s >= 272, 272, 224))
    low = jnp.where(second, 0, 3)
    wide = big & (u < 72)
    u2 = jnp.where(big, u - 72, u)
    lev_w = (u >= 36).astype(jnp.int32)
    m_w = u - 36 * lev_w
    row_w = (m_w >= 12).astype(jnp.int32) + (m_w >= 24).astype(jnp.int32)
    col_w = 6 + m_w - 12 * row_w
    lev_n = (u2 >= 18).astype(jnp.int32)
    m_n = u2 - 18 * lev_n
    row_n = (m_n >= 6).astype(jnp.int32) + (m_n >= 12).astype(jnp.int32)
    col_n = jnp.where(big, 18, 0) + m_n - 6 * row_n
    lev = jnp.where(wide, lev_w, lev_n)
    row = jnp.where(wide, row_w, row_n) + low
    col = jnp.where(wide, col_w, col_n)
    empty = u >= jnp.where(big, 108, 36)
    return jnp.where(empty, -1, lev * 144 + row * 24 + col)


def packed_of(w):
    at = jnp.where(w < 72, w, w + 40)
    at = jnp.where(w >= 144, w - 72, at)
    at = jnp.where(w >= 180, w + 44, at)
    at = jnp.where(w >= 216, w - 32, at)
    return jnp.where(w >= 252, w + 20, at)


def iota(shape, dim):
    return lax.broadcasted_iota(jnp.int32, shape, dim)


def ones_at(same):
    return jnp.where(same, 1.0, 0.0).astype(BF16)


def pack_matrix():
    return ones_at(token_of(iota((PACKED, 1), 0)) == iota((PACKED, NT), 1))


def unpack_matrix():
    return ones_at(token_of(iota((1, PACKED), 1)) == iota((NT, PACKED), 0))


def window_matrix():
    return ones_at(packed_of(iota((NT, 1), 0)) == iota((NT, PACKED), 1))


def unwindow_matrix():
    return ones_at(packed_of(iota((1, NT), 1)) == iota((PACKED, NT), 0))


def normalize(values):
    centre = values - jnp.mean(values, axis=-1, keepdims=True)
    inv_std = lax.rsqrt(jnp.mean(centre * centre, axis=-1, keepdims=True) + epsilon)
    return centre * inv_std, inv_std


def norm_back(upstream, normed, inv_std):
    mean_up = jnp.mean(upstream, axis=-1, keepdims=True)
    mean_dot = jnp.mean(upstream * normed, axis=-1, keepdims=True)
    return inv_std * (upstream - mean_up - normed * mean_dot)


def head_stack(value):
    lane = iota((144, 128), 1)
    zero = jnp.zeros_like(value)
    return jnp.concatenate([jnp.where((lane >> 5) == j, value, zero) for j in range(4)], axis=0)


def head_merge(value):
    lane = iota((144, 128), 1) >> 5
    out = value[432:576]
    for j in range(3):
        out = jnp.where(lane == j, value[144 * j : 144 * j + 144], out)
    return out


def block_kernel(
    x_ref, c_ref, wqkv_hbm, wproj_hbm, wfc1_hbm, wfc2_hbm,
    out_ref, gin_ref, wg_ref,
    early, late, orders_ref, lhs_ref, wqkv, wproj, wfc1, wfc2,
    packs, arrived, maps_p, maps_w, act_ref, gh_ref, qkv, gm, probs, bias, ctx, gctx, f32s, b16s, cols,
    send_sems, recv_sems, weight_sems,
):
    place = Place()
    copies = Copies(send_sems, recv_sems)
    loads = [
        pltpu.make_async_copy(src, dst, weight_sems.at[i])
        for i, (src, dst) in enumerate(((wqkv_hbm, wqkv), (wproj_hbm, wproj), (wfc1_hbm, wfc1), (wfc2_hbm, wfc2)))
    ]
    for load in loads:
        load.start()

    maps_p[0] = pack_matrix()
    greet(place)
    halos = []
    for i, ref in enumerate((x_ref, c_ref)):
        packs[i] = dot(maps_p[0], ref[...]).astype(BF16)
        halos.append(
            [
                copies.send(
                    packs.at[i, pl.ds(at, count)],
                    arrived.at[i, pl.ds(at, count)],
                    place.neighbour(16 - a if a else 0, 16 - b if b else 0),
                )
                for at, count, a, b in SECTIONS
            ]
        )
        arrived[i, 0:112] = packs[i, 0:112]
    maps_w[0] = window_matrix()
    maps_p[1] = unwindow_matrix()
    maps_w[1] = unpack_matrix()
    for part, order in enumerate(ORDERS):
        for own in (0, 1):
            orders_ref[2 * part + own] = row_order(place, order, own)
    last_band = place.lat == 15
    apart = ((iota((144, 144), 0) >= 72) != (iota((144, 144), 1) >= 72)) & last_band
    bias[...] = jnp.where(apart, neg_fill, 0.0)

    def return_home(slot, value):
        packs[slot] = dot(maps_p[1], value).astype(BF16)
        sent = [
            copies.send(
                packs.at[slot, pl.ds(at, count)],
                arrived.at[slot, pl.ds(at, count)],
                place.neighbour(a, b),
            )
            for at, count, a, b in SECTIONS
        ]
        arrived[slot, 0:112] = packs[slot, 0:112]
        return sent

    def arrive_home(slot, sent, ref):
        for copy in sent:
            copy.wait_recv()
        ref[...] = dot(maps_w[1], arrived[slot]).astype(BF16)

    X, N1, N2, G1 = 0, 1, 2, 3
    N1B, N2B, COT, GR = 0, 1, 2, 3
    R1, R2 = 0, 1

    for copy in halos[0]:
        copy.wait_recv()
    x = dot(maps_w[0], arrived[0])
    f32s[X] = x
    normed, inv_std = normalize(x)
    f32s[N1] = normed
    cols[R1] = inv_std
    b16s[N1B] = normed.astype(BF16)
    loads[0].wait()
    for i in range(3):
        part = dot(b16s[N1B], wqkv[:, 512 * i : 512 * i + 512])
        if i == 0:
            part = part * 32 ** (-0.5)
        qkv[:, 512 * i : 512 * i + 512] = part.astype(BF16)

    def group(i, which):
        w, g = lax.div(i, 4), lax.rem(i, 4)
        return pl.ds(pl.multiple_of(w * 144, 144), 144), pl.ds(pl.multiple_of(which * 512 + g * 128, 128), 128)

    @pl.loop(0, 8)
    def _(i):
        rows, lanes = group(i, 0)
        q = head_stack(qkv[rows, lanes])
        scores = dot(q, qkv[group(i, 1)], 1, 1)
        added = jnp.concatenate([bias[...]] * 4, axis=0)
        scores = scores + added
        raised = jnp.exp(scores - jnp.max(scores, axis=-1, keepdims=True))
        p = raised * (1.0 / jnp.sum(raised, axis=-1, keepdims=True))
        probs[i] = p
        ctx[rows, lanes] = head_merge(dot(p.astype(BF16), qkv[group(i, 2)])).astype(BF16)

    loads[1].wait()
    branch = dot(ctx[...], wproj[...]).astype(BF16)
    residual = (f32s[X] + branch.astype(F32)).astype(BF16)
    resid32 = residual.astype(F32)
    f32s[X] = resid32
    normed, inv_std = normalize(resid32)
    f32s[N2] = normed
    cols[R2] = inv_std
    b16s[N2B] = normed.astype(BF16)

    for copy in halos[1]:
        copy.wait_recv()
    b16s[COT] = dot(maps_w[0], arrived[1]).astype(BF16)
    loads[2].wait()
    loads[3].wait()

    @pl.loop(0, 8)
    def _(t):
        tile = pl.ds(pl.multiple_of(t * 256, 256), 256)
        hidden = dot(b16s[N2B], wfc1[:, tile])
        upper = 0.5 * (1.0 + lax.erf(hidden * inv_root_two))
        act_ref[:, tile] = (hidden * upper).astype(BF16)
        slope = upper + hidden * inv_root_tau * jnp.exp(-0.5 * hidden * hidden)
        gh_ref[:, tile] = (dot(b16s[COT], wfc2[tile, :], 1, 1) * slope).astype(BF16)

    grad_n2 = dot(gh_ref[...], wfc1[...], 1, 1)
    grad_resid = (b16s[COT].astype(F32) + norm_back(grad_n2, f32s[N2], cols[R2])).astype(BF16)
    b16s[GR] = grad_resid

    pairs = dict(
        qkv=(b16s.at[N1B], gm),
        proj=(ctx, b16s.at[GR]),
        fc1=(b16s.at[N2B], gh_ref),
        fc2=(b16s.at[COT], act_ref),
    )
    gens = start_batch(place, copies, EARLY, 1536, early, wg_ref, pairs, orders_ref, lhs_ref)

    block_out = (f32s[X] + dot(act_ref[...], wfc2[...])).astype(BF16)
    out_sent = return_home(2, block_out)
    gctx[...] = dot(b16s[GR], wproj[...], 1, 1).astype(BF16)

    for i in range(8):
        gens = tick(gens)
        w, g = i // 4, i % 4
        rows = slice(144 * w, 144 * w + 144)
        lanes = [slice(512 * j + 128 * g, 512 * j + 128 * g + 128) for j in range(3)]
        grad = head_stack(gctx[rows, lanes[0]])
        p = probs[i]
        grad_p = dot(grad, qkv[rows, lanes[2]], 1, 1)
        grad_s = (p * (grad_p - jnp.sum(grad_p * p, axis=-1, keepdims=True))).astype(BF16)
        gm[rows, lanes[2]] = dot(p.astype(BF16), grad, 0, 0).astype(BF16)
        gm[rows, lanes[0]] = (head_merge(dot(grad_s, qkv[rows, lanes[1]])) * 32 ** (-0.5)).astype(BF16)
        gm[rows, lanes[1]] = dot(grad_s, head_stack(qkv[rows, lanes[0]]), 0, 0).astype(BF16)

    gens += start_batch(place, copies, LATE, 512, late, wg_ref, pairs, orders_ref, lhs_ref)
    gens = tick(gens)
    grad_n1 = dot(gm[...], wqkv[...], 1, 1).astype(BF16).astype(F32)
    grad_in = b16s[GR].astype(F32) + norm_back(grad_n1, f32s[N1], cols[R1])
    in_sent = return_home(3, grad_in.astype(BF16))
    gens = tick(gens)
    arrive_home(2, out_sent, out_ref)
    gens = tick(gens)
    arrive_home(3, in_sent, gin_ref)
    while gens:
        gens = tick(gens)
    copies.drain()


def on_device(tokens, cotangent, w_qkv, w_proj, w_fc1, w_fc2):
    vmem = pl.BlockSpec(memory_space=pltpu.VMEM)
    hbm = pl.BlockSpec(memory_space=pl.ANY)
    out, gin, wg = pl.pallas_call(
        block_kernel,
        out_shape=(
            jax.ShapeDtypeStruct((NT, D), BF16),
            jax.ShapeDtypeStruct((NT, D), BF16),
            jax.ShapeDtypeStruct((96, 128), F32),
        ),
        in_specs=[vmem, vmem, hbm, hbm, hbm, hbm],
        out_specs=(vmem, vmem, vmem),
        scratch_shapes=[
            batch_scratch(1536),
            batch_scratch(512),
            pltpu.VMEM((6, 256, D), BF16),
            pltpu.VMEM((256, NT), BF16),
            pltpu.VMEM((D, 3 * D), BF16),
            pltpu.VMEM((D, D), BF16),
            pltpu.VMEM((D, 4 * D), BF16),
            pltpu.VMEM((4 * D, D), BF16),
            pltpu.VMEM((4, PACKED, D), BF16),
            pltpu.VMEM((4, PACKED, D), BF16),
            pltpu.VMEM((2, PACKED, NT), BF16),
            pltpu.VMEM((2, NT, PACKED), BF16),
            pltpu.VMEM((NT, 4 * D), BF16),
            pltpu.VMEM((NT, 4 * D), BF16),
            pltpu.VMEM((NT, 3 * D), BF16),
            pltpu.VMEM((NT, 3 * D), BF16),
            pltpu.VMEM((8, 576, 144), F32),
            pltpu.VMEM((144, 144), F32),
            pltpu.VMEM((NT, D), BF16),
            pltpu.VMEM((NT, D), BF16),
            pltpu.VMEM((3, NT, D), F32),
            pltpu.VMEM((4, NT, D), BF16),
            pltpu.VMEM((2, NT, 1), F32),
            pltpu.SemaphoreType.DMA((120,)),
            pltpu.SemaphoreType.DMA((120,)),
            pltpu.SemaphoreType.DMA((4,)),
        ],
        compiler_params=pltpu.CompilerParams(
            collective_id=0, has_side_effects=True, vmem_limit_bytes=60 * 1024 * 1024
        ),
    )(tokens.reshape(NT, D), cotangent.reshape(NT, D), w_qkv, w_proj, w_fc1, w_fc2)
    return out.reshape(tokens.shape), gin.reshape(tokens.shape), wg


def solution(mesh):
    return jax.shard_map(
        on_device,
        mesh=mesh,
        in_specs=(P(None, "lat", "lon", None), P(None, "lat", "lon", None), P(), P(), P(), P()),
        out_specs=(
            P(None, "lat", "lon", None),
            P(None, "lat", "lon", None),
            P(("lat", "lon"), None),
        ),
        check_vma=False,
    )
```

```python
import jax
import jax.numpy as jnp
from jax import lax
from jax.experimental import pallas as pl
from jax.experimental.pallas import tpu as pltpu
from jax.sharding import PartitionSpec as P

MESH = pl.DeviceIdType.MESH
H = 16
D = 512
NT = 288
F32 = jnp.float32
BF16 = jnp.bfloat16

epsilon = 1e-05
neg_fill = -1e30
inv_root_two = 0.7071067811865476
inv_root_tau = 0.3989422804014327
grad_scale = 73728 ** (-0.5)


class Place:
    def __init__(self):
        lat, lon = lax.axis_index("lat"), lax.axis_index("lon")
        self.lat, self.lon = lat, lon
        self.core = lax.rem(lat, 2)
        self.x = lax.rem(lax.div(lat, 2), 4)
        self.y = lax.div(lat, 8) * 2 + lax.rem(lon, 2)
        self.z = lax.div(lon, 2)

    def shifted(self, axis=None, by=0):
        x, y, z, core = self.x, self.y, self.z, self.core
        if axis == "x":
            x = lax.rem(x + by, 4)
        elif axis == "y":
            y = lax.rem(y + by, 4)
        elif axis == "z":
            z = lax.rem(z + by, 8)
        elif axis == "core":
            core = 1 - core
        return (lax.div(y, 2) * 8 + x * 2 + core, z * 2 + lax.rem(y, 2))

    def neighbour(self, by_lat, by_lon):
        return (lax.rem(self.lat + by_lat, 16), lax.rem(self.lon + by_lon, 16))


SIZES = {"x": 4, "y": 4, "z": 8}
ORDERS = (("x", "y", "z"), ("y", "x", "z"), ("z", "x", "y"))


def row_order(place, order):
    p = lax.broadcasted_iota(jnp.int32, (256, 1), 0)
    r = p & 1
    rest = p >> 1
    off = {}
    for axis in reversed(order):
        bits = 3 if axis == "z" else 2
        off[axis] = rest & (SIZES[axis] - 1)
        rest = rest >> bits
    x = (off["x"] + place.x) & 3
    y = (off["y"] + place.y) & 3
    z = (off["z"] + place.z) & 7
    row = ((((((y >> 1) * 4 + x) * 2 + place.core) * 8 + z) * 2 + (y & 1)) * 2) + r
    columns = lax.broadcasted_iota(jnp.int32, (256, D), 1)
    return jnp.where(columns == row, 1.0, 0.0).astype(BF16)


def dot(a, b, ca=1, cb=0):
    return lax.dot_general(a, b, (((ca,), (cb,)), ((), ())), preferred_element_type=F32)


class Copies:
    def __init__(self, send_sems, recv_sems):
        self.send_sems, self.recv_sems, self.used, self.started = send_sems, recv_sems, 0, []

    def send(self, src, dst, target):
        k = self.used
        self.used += 1
        copy = pltpu.make_async_remote_copy(
            src_ref=src,
            dst_ref=dst,
            send_sem=self.send_sems.at[k],
            recv_sem=self.recv_sems.at[k],
            device_id=target,
            device_id_type=MESH,
        )
        copy.start()
        self.started.append(copy)
        return copy

    def drain(self):
        for copy in self.started:
            copy.wait_send()


class Part:
    def __init__(self, place, copies, part, width, scr, emit, out_ref):
        self.place, self.copies, self.scr, self.width = place, copies, scr, width
        self.first, self.second, self.third = ORDERS[part]
        self.n1, self.n2, self.n3 = (SIZES[a] for a in ORDERS[part])
        self.rows1 = 256 // self.n1
        self.rows2 = self.rows1 // self.n2
        self.emit, self.out_ref = emit, out_ref
        self.pending = []

    def multiply(self, lhs, rhs, src, at, count):
        value = dot(lhs[...], rhs[:, src : src + count])
        self.scr["own"][:, at : at + count] = value[: self.rows1]
        self.scr["send1"][:, at : at + count] = value[self.rows1 :].astype(BF16)

    def send_first(self, at, count):
        r = self.rows1
        for j in range(1, self.n1):
            here = (pl.ds((j - 1) * r, r), pl.ds(at, count))
            self.pending.append(
                self.copies.send(
                    self.scr["send1"].at[here], self.scr["recv1"].at[here], self.place.shifted(self.first, j)
                )
            )

    def arrive(self):
        for copy in self.pending:
            copy.wait_recv()
        self.pending = []

    def second_step(self):
        self.arrive()
        scr, r1, r = self.scr, self.rows1, self.rows2
        whole = None
        if r < 16:
            whole = scr["own"][...]
            for i in range(self.n1 - 1):
                whole = whole + scr["recv1"][i * r1 : i * r1 + r1].astype(F32)
        for j in (2, 1, 3, 0):
            rows = slice(j * r, j * r + r)
            if r < 16:
                total = whole[rows]
            else:
                total = scr["own"][rows]
                for i in range(self.n1 - 1):
                    total = total + scr["recv1"][i * r1 + j * r : i * r1 + j * r + r].astype(F32)
            if j == 0:
                scr["own"][rows] = total
            else:
                here = pl.ds((j - 1) * r, r)
                scr["send2"][(j - 1) * r : j * r] = total.astype(scr["send2"].dtype)
                self.pending.append(
                    self.copies.send(
                        scr["send2"].at[here], scr["recv2"].at[here], self.place.shifted(self.second, j)
                    )
                )

    def third_step(self):
        self.arrive()
        scr, r = self.scr, self.rows2
        total = scr["own"][0:r]
        for i in range(self.n2 - 1):
            total = total + scr["recv2"][i * r : i * r + r].astype(F32)
        slots = scr["wide3"].shape[0] // (2 * self.n3)
        for c in range(self.width // 128):
            scr["wide3"][pl.ds(c, 2 * self.n3, stride=slots), :] = total[:, c * 128 : (c + 1) * 128]
        each = 2 * slots
        scr["send3"][...] = scr["wide3"][each:].astype(BF16)
        for j in range(1, self.n3):
            here = pl.ds((j - 1) * each, each)
            self.pending.append(
                self.copies.send(scr["send3"].at[here], scr["recv3"].at[here], self.place.shifted(self.third, j))
            )

    def finish(self):
        self.arrive()
        scr = self.scr
        slots = scr["wide3"].shape[0] // (2 * self.n3)
        each = 2 * slots
        total = scr["wide3"][0:each]
        for i in range(self.n3 - 1):
            total = total + scr["recv3"][i * each : (i + 1) * each].astype(F32)
        total = total * grad_scale
        for r in range(2):
            for local, whole, count in self.emit:
                self.out_ref[r * 48 + whole : r * 48 + whole + count, :] = total[
                    r * slots + local : r * slots + local + count, :
                ]


def part_scratch(part, width):
    n1, n2, n3 = (SIZES[a] for a in ORDERS[part])
    r1 = 256 // n1
    r2 = r1 // n2
    slots = -(-(width // 128) // 8) * 8
    mid = BF16 if r2 >= 16 else F32
    return dict(
        own=pltpu.VMEM((r1, width), F32),
        send1=pltpu.VMEM((256 - r1, width), BF16),
        recv1=pltpu.VMEM((256 - r1, width), BF16),
        send2=pltpu.VMEM((r1 - r2, width), mid),
        recv2=pltpu.VMEM((r1 - r2, width), mid),
        wide3=pltpu.VMEM((2 * n3 * slots, 128), F32),
        send3=pltpu.VMEM((2 * (n3 - 1) * slots, 128), BF16),
        recv3=pltpu.VMEM((2 * (n3 - 1) * slots, 128), BF16),
    )


EARLY = (2048, 2048, 512)
LATE = (640, 640, 256)
EARLY_OUT = (((0, 16, 16),), ((0, 32, 16),), ((0, 12, 4),))
LATE_OUT = (((0, 0, 4), (4, 8, 1)), ((0, 4, 4), (4, 9, 1)), ((0, 10, 2),))


def greet(place):
    barrier = pltpu.get_barrier_semaphore()
    peers = [place.shifted("core")]
    for axis in ("x", "y", "z"):
        peers += [place.shifted(axis, by) for by in range(1, SIZES[axis])]
    for by in (1, 15):
        peers += [place.neighbour(by, 0), place.neighbour(0, by), place.neighbour(by, by)]
    for peer in peers:
        pl.semaphore_signal(barrier, inc=1, device_id=peer, device_id_type=MESH)
    return lambda: pl.semaphore_wait(barrier, len(peers))


PACKED = 320
SECTIONS = ((112, 112, 1, 0), (224, 48, 0, 1), (272, 48, 1, 1))


def token_of(s):
    big = s < 224
    second = ((s >= 112) & (s < 224)) | (s >= 272)
    u = jnp.where(big, s - jnp.where(s >= 112, 112, 0), s - jnp.where(s >= 272, 272, 224))
    low = jnp.where(second, 0, 3)
    wide = big & (u < 72)
    u2 = jnp.where(big, u - 72, u)
    lev_w = (u >= 36).astype(jnp.int32)
    m_w = u - 36 * lev_w
    row_w = (m_w >= 12).astype(jnp.int32) + (m_w >= 24).astype(jnp.int32)
    col_w = 6 + m_w - 12 * row_w
    lev_n = (u2 >= 18).astype(jnp.int32)
    m_n = u2 - 18 * lev_n
    row_n = (m_n >= 6).astype(jnp.int32) + (m_n >= 12).astype(jnp.int32)
    col_n = jnp.where(big, 18, 0) + m_n - 6 * row_n
    lev = jnp.where(wide, lev_w, lev_n)
    row = jnp.where(wide, row_w, row_n) + low
    col = jnp.where(wide, col_w, col_n)
    empty = u >= jnp.where(big, 108, 36)
    return jnp.where(empty, -1, lev * 144 + row * 24 + col)


def packed_of(w):
    at = jnp.where(w < 72, w, w + 40)
    at = jnp.where(w >= 144, w - 72, at)
    at = jnp.where(w >= 180, w + 44, at)
    at = jnp.where(w >= 216, w - 32, at)
    return jnp.where(w >= 252, w + 20, at)


def iota(shape, dim):
    return lax.broadcasted_iota(jnp.int32, shape, dim)


def ones_at(same):
    return jnp.where(same, 1.0, 0.0).astype(BF16)


def pack_matrix():
    return ones_at(token_of(iota((PACKED, 1), 0)) == iota((PACKED, NT), 1))


def unpack_matrix():
    return ones_at(token_of(iota((1, PACKED), 1)) == iota((NT, PACKED), 0))


def window_matrix():
    return ones_at(packed_of(iota((NT, 1), 0)) == iota((NT, PACKED), 1))


def unwindow_matrix():
    return ones_at(packed_of(iota((1, NT), 1)) == iota((PACKED, NT), 0))


def normalize(values):
    centre = values - jnp.mean(values, axis=-1, keepdims=True)
    inv_std = lax.rsqrt(jnp.mean(centre * centre, axis=-1, keepdims=True) + epsilon)
    return centre * inv_std, inv_std


def norm_back(upstream, normed, inv_std):
    mean_up = jnp.mean(upstream, axis=-1, keepdims=True)
    mean_dot = jnp.mean(upstream * normed, axis=-1, keepdims=True)
    return inv_std * (upstream - mean_up - normed * mean_dot)


def head_stack(value):
    lane = iota((144, 128), 1)
    zero = jnp.zeros_like(value)
    return jnp.concatenate([jnp.where((lane >> 5) == j, value, zero) for j in range(4)], axis=0)


def head_merge(value):
    lane = iota((144, 128), 1) >> 5
    out = value[432:576]
    for j in range(3):
        out = jnp.where(lane == j, value[144 * j : 144 * j + 144], out)
    return out


OWN, SIB = slice(0, NT), slice(NT, 2 * NT)


def block_kernel(
    x_ref, c_ref, wqkv_hbm, wproj_hbm, wfc1_hbm, wfc2_hbm,
    out_ref, gin_ref, wg_ref,
    early, late, orders_ref, wqkv, wproj, wfc1, wfc2,
    packs, arrived, maps_p, maps_w, act, gh, n1b, n2b, cot, ctx, gr, gm,
    lhs_n1, lhs_n2, lhs_cot, lhs_ctx, qkv, probs, bias, gctx, f32s, cols,
    send_sems, recv_sems, weight_sems,
):
    place = Place()
    copies = Copies(send_sems, recv_sems)
    met = greet(place)
    loads = [
        pltpu.make_async_copy(src, dst, weight_sems.at[i])
        for i, (src, dst) in enumerate(((wqkv_hbm, wqkv), (wproj_hbm, wproj), (wfc1_hbm, wfc1), (wfc2_hbm, wfc2)))
    ]
    for load in loads:
        load.start()
    X, N1, N2 = 0, 1, 2
    R1, R2 = 0, 1

    def share(ref, at=0, count=None):
        here = pl.ds(at, ref.shape[1] if count is None else count)
        return copies.send(ref.at[pl.ds(0, NT), here], ref.at[pl.ds(NT, NT), here], place.shifted("core"))

    early = [
        Part(place, copies, i, width, scr, emit, wg_ref) for i, (width, scr, emit) in enumerate(zip(EARLY, early, EARLY_OUT))
    ]
    late = [
        Part(place, copies, i, width, scr, emit, wg_ref) for i, (width, scr, emit) in enumerate(zip(LATE, late, LATE_OUT))
    ]

    maps_p[0] = pack_matrix()
    packs[0] = dot(maps_p[0], x_ref[...]).astype(BF16)
    packs[1] = dot(maps_p[0], c_ref[...]).astype(BF16)
    maps_w[0] = window_matrix()
    maps_p[1] = unwindow_matrix()
    maps_w[1] = unpack_matrix()
    for part, order in enumerate(ORDERS):
        orders_ref[part] = row_order(place, order)
    apart = ((iota((144, 144), 0) >= 72) != (iota((144, 144), 1) >= 72)) & (place.lat == 15)
    bias[...] = jnp.where(apart, neg_fill, 0.0)
    met()
    halos = []
    for i in range(2):
        halos.append(
            [
                copies.send(
                    packs.at[i, pl.ds(at, count)],
                    arrived.at[i, pl.ds(at, count)],
                    place.neighbour(16 - a if a else 0, 16 - b if b else 0),
                )
                for at, count, a, b in SECTIONS
            ]
        )
        arrived[i, 0:112] = packs[i, 0:112]

    def return_home(slot, value):
        packs[slot] = dot(maps_p[1], value).astype(BF16)
        sent = [
            copies.send(
                packs.at[slot, pl.ds(at, count)],
                arrived.at[slot, pl.ds(at, count)],
                place.neighbour(a, b),
            )
            for at, count, a, b in SECTIONS
        ]
        arrived[slot, 0:112] = packs[slot, 0:112]
        return sent

    def arrive_home(slot, sent, ref):
        for copy in sent:
            copy.wait_recv()
        ref[...] = dot(maps_w[1], arrived[slot]).astype(BF16)

    for copy in halos[0]:
        copy.wait_recv()
    x = dot(maps_w[0], arrived[0])
    f32s[X] = x
    normed, inv_std = normalize(x)
    f32s[N1] = normed
    cols[R1] = inv_std
    n1b[OWN] = normed.astype(BF16)
    shared_n1 = share(n1b)
    loads[0].wait()
    for i in range(3):
        part = dot(n1b[OWN], wqkv[:, 512 * i : 512 * i + 512])
        if i == 0:
            part = part * 32 ** (-0.5)
        qkv[:, 512 * i : 512 * i + 512] = part.astype(BF16)

    def group(w, g):
        rows = slice(144 * w, 144 * w + 144)
        return rows, [slice(512 * j + 128 * g, 512 * j + 128 * g + 128) for j in range(3)]

    for w in range(2):
        for g in range(4):
            rows, (lq, lk, lv) = group(w, g)
            scores = dot(head_stack(qkv[rows, lq]), qkv[rows, lk], 1, 1)
            scores = scores + jnp.concatenate([bias[...]] * 4, axis=0)
            raised = jnp.exp(scores - jnp.max(scores, axis=-1, keepdims=True))
            p = raised * (1.0 / jnp.sum(raised, axis=-1, keepdims=True))
            probs[4 * w + g] = p
            ctx[rows, lq] = head_merge(dot(p.astype(BF16), qkv[rows, lv])).astype(BF16)

    shared_ctx = share(ctx)
    loads[1].wait()
    branch = dot(ctx[OWN], wproj[...]).astype(BF16)
    residual = (f32s[X] + branch.astype(F32)).astype(BF16)
    resid32 = residual.astype(F32)
    f32s[X] = resid32
    normed, inv_std = normalize(resid32)
    f32s[N2] = normed
    cols[R2] = inv_std
    n2b[OWN] = normed.astype(BF16)
    shared_n2 = share(n2b)

    for copy in halos[1]:
        copy.wait_recv()
    cot[OWN] = dot(maps_w[0], arrived[1]).astype(BF16)
    shared_cot = share(cot)
    loads[2].wait()
    loads[3].wait()
    shared_ff = []

    def forward_tile(t):
        tile = slice(512 * t, 512 * t + 512)
        hidden = dot(n2b[OWN], wfc1[:, tile])
        upper = 0.5 * (1.0 + lax.erf(hidden * inv_root_two))
        act[OWN, tile] = (hidden * upper).astype(BF16)
        slope = upper + hidden * inv_root_tau * jnp.exp(-0.5 * hidden * hidden)
        gh[OWN, tile] = (dot(cot[OWN], wfc2[tile, :], 1, 1) * slope).astype(BF16)
        shared_ff.append((share(act, 512 * t, 512), share(gh, 512 * t, 512)))

    def half(h):
        for pair in shared_ff[2 * h : 2 * h + 2]:
            for copy in pair:
                copy.wait_recv()
        for part, lhs, rhs in ((0, lhs_n2, gh), (1, lhs_cot, act)):
            early[part].multiply(lhs, rhs, 1024 * h, 1024 * h, 1024)
            early[part].send_first(1024 * h, 1024)

    for t in range(3):
        forward_tile(t)
    shared_n2.wait_recv()
    shared_cot.wait_recv()
    lhs_n2[...] = dot(orders_ref[0], n2b[...], 1, 1).astype(BF16)
    lhs_cot[...] = dot(orders_ref[1], cot[...], 1, 1).astype(BF16)
    half(0)
    forward_tile(3)
    grad_n2 = dot(gh[OWN], wfc1[...], 1, 1)
    grad_resid = (cot[OWN].astype(F32) + norm_back(grad_n2, f32s[N2], cols[R2])).astype(BF16)
    gr[OWN] = grad_resid
    shared_gr = share(gr)
    half(1)
    shared_ctx.wait_recv()
    lhs_ctx[...] = dot(orders_ref[2], ctx[...], 1, 1).astype(BF16)
    shared_gr.wait_recv()
    early[2].multiply(lhs_ctx, gr, 0, 0, 512)
    early[2].send_first(0, 512)

    block_out = (f32s[X] + dot(act[OWN], wfc2[...])).astype(BF16)
    out_sent = return_home(2, block_out)
    gctx[...] = dot(gr[OWN], wproj[...], 1, 1).astype(BF16)

    shared_n1.wait_recv()
    for i in range(3):
        lhs_n1[i] = dot(orders_ref[i], n1b[...], 1, 1).astype(BF16)
    shared_gm = []
    for g in range(4):
        for w in range(2):
            rows, (lq, lk, lv) = group(w, g)
            grad = head_stack(gctx[rows, lq])
            p = probs[4 * w + g]
            grad_p = dot(grad, qkv[rows, lv], 1, 1)
            grad_s = (p * (grad_p - jnp.sum(grad_p * p, axis=-1, keepdims=True))).astype(BF16)
            gm[rows, lv] = dot(p.astype(BF16), grad, 0, 0).astype(BF16)
            gm[rows, lq] = (head_merge(dot(grad_s, qkv[rows, lk])) * 32 ** (-0.5)).astype(BF16)
            gm[rows, lk] = dot(grad_s, head_stack(qkv[rows, lq]), 0, 0).astype(BF16)
        if g % 2:
            shared_gm += [share(gm, 512 * j + 128 * (g - 1), 256) for j in range(3)]

    for part in early:
        part.second_step()
    for copy in shared_gm:
        copy.wait_recv()
    for i in range(2):
        late[i].multiply(lhs_n1.at[i], gm, 512 * i, 0, 512)
        late[i].multiply(lhs_n1.at[i], gm, 1024 + 128 * i, 512, 128)
        late[i].send_first(0, 640)
    late[2].multiply(lhs_n1.at[2], gm, 1280, 0, 256)
    late[2].send_first(0, 256)
    grad_n1 = dot(gm[OWN], wqkv[...], 1, 1).astype(BF16).astype(F32)
    grad_in = gr[OWN].astype(F32) + norm_back(grad_n1, f32s[N1], cols[R1])
    in_sent = return_home(3, grad_in.astype(BF16))
    for part in early:
        part.third_step()
    for part in late:
        part.second_step()
    arrive_home(2, out_sent, out_ref)
    arrive_home(3, in_sent, gin_ref)
    for part in late:
        part.third_step()
    for part in early:
        part.finish()
    for part in late:
        part.finish()
    copies.drain()


def on_device(tokens, cotangent, w_qkv, w_proj, w_fc1, w_fc2):
    vmem = pl.BlockSpec(memory_space=pltpu.VMEM)
    hbm = pl.BlockSpec(memory_space=pl.ANY)
    both = 2 * NT
    out, gin, wg = pl.pallas_call(
        block_kernel,
        out_shape=(
            jax.ShapeDtypeStruct((NT, D), BF16),
            jax.ShapeDtypeStruct((NT, D), BF16),
            jax.ShapeDtypeStruct((96, 128), F32),
        ),
        in_specs=[vmem, vmem, hbm, hbm, hbm, hbm],
        out_specs=(vmem, vmem, vmem),
        scratch_shapes=[
            [part_scratch(i, w) for i, w in enumerate(EARLY)],
            [part_scratch(i, w) for i, w in enumerate(LATE)],
            pltpu.VMEM((3, 256, D), BF16),
            pltpu.VMEM((D, 3 * D), BF16),
            pltpu.VMEM((D, D), BF16),
            pltpu.VMEM((D, 4 * D), BF16),
            pltpu.VMEM((4 * D, D), BF16),
            pltpu.VMEM((4, PACKED, D), BF16),
            pltpu.VMEM((4, PACKED, D), BF16),
            pltpu.VMEM((2, PACKED, NT), BF16),
            pltpu.VMEM((2, NT, PACKED), BF16),
            pltpu.VMEM((both, 4 * D), BF16),
            pltpu.VMEM((both, 4 * D), BF16),
            pltpu.VMEM((both, D), BF16),
            pltpu.VMEM((both, D), BF16),
            pltpu.VMEM((both, D), BF16),
            pltpu.VMEM((both, D), BF16),
            pltpu.VMEM((both, D), BF16),
            pltpu.VMEM((both, 3 * D), BF16),
            pltpu.VMEM((3, 256, both), BF16),
            pltpu.VMEM((256, both), BF16),
            pltpu.VMEM((256, both), BF16),
            pltpu.VMEM((256, both), BF16),
            pltpu.VMEM((NT, 3 * D), BF16),
            pltpu.VMEM((8, 576, 144), F32),
            pltpu.VMEM((144, 144), F32),
            pltpu.VMEM((NT, D), BF16),
            pltpu.VMEM((3, NT, D), F32),
            pltpu.VMEM((2, NT, 1), F32),
            pltpu.SemaphoreType.DMA((120,)),
            pltpu.SemaphoreType.DMA((120,)),
            pltpu.SemaphoreType.DMA((4,)),
        ],
        compiler_params=pltpu.CompilerParams(
            collective_id=0, has_side_effects=True, vmem_limit_bytes=60 * 1024 * 1024
        ),
    )(tokens.reshape(NT, D), cotangent.reshape(NT, D), w_qkv, w_proj, w_fc1, w_fc2)
    return out.reshape(tokens.shape), gin.reshape(tokens.shape), wg


def solution(mesh):
    return jax.shard_map(
        on_device,
        mesh=mesh,
        in_specs=(P(None, "lat", "lon", None), P(None, "lat", "lon", None), P(), P(), P(), P()),
        out_specs=(
            P(None, "lat", "lon", None),
            P(None, "lat", "lon", None),
            P(("lat", "lon"), None),
        ),
        check_vma=False,
    )
```

```python
import jax
import jax.numpy as jnp
from jax import lax
from jax.experimental import pallas as pl
from jax.experimental.pallas import tpu as pltpu
from jax.sharding import PartitionSpec as P

MESH = pl.DeviceIdType.MESH
H = 16
D = 512
NT = 288
F32 = jnp.float32
BF16 = jnp.bfloat16

epsilon = 1e-05
neg_fill = -1e30
inv_root_two = 0.7071067811865476
inv_root_tau = 0.3989422804014327
grad_scale = 73728 ** (-0.5)


class Place:
    def __init__(self):
        lat, lon = lax.axis_index("lat"), lax.axis_index("lon")
        self.lat, self.lon = lat, lon
        self.core = lax.rem(lat, 2)
        self.x = lax.rem(lax.div(lat, 2), 4)
        self.y = lax.div(lat, 8) * 2 + lax.rem(lon, 2)
        self.z = lax.div(lon, 2)

    def shifted(self, axis=None, by=0):
        x, y, z, core = self.x, self.y, self.z, self.core
        if axis == "x":
            x = lax.rem(x + by, 4)
        elif axis == "y":
            y = lax.rem(y + by, 4)
        elif axis == "z":
            z = lax.rem(z + by, 8)
        elif axis == "core":
            core = 1 - core
        return (lax.div(y, 2) * 8 + x * 2 + core, z * 2 + lax.rem(y, 2))

    def neighbour(self, by_lat, by_lon):
        return (lax.rem(self.lat + by_lat, 16), lax.rem(self.lon + by_lon, 16))


SIZES = {"x": 4, "y": 4, "z": 8}
ORDERS = (("x", "y", "z"), ("y", "x", "z"), ("z", "x", "y"))


def row_order(place, order):
    p = lax.broadcasted_iota(jnp.int32, (256, 1), 0)
    r = p & 1
    rest = p >> 1
    off = {}
    for axis in reversed(order):
        bits = 3 if axis == "z" else 2
        off[axis] = rest & (SIZES[axis] - 1)
        rest = rest >> bits
    x = (off["x"] + place.x) & 3
    y = (off["y"] + place.y) & 3
    z = (off["z"] + place.z) & 7
    row = ((((((y >> 1) * 4 + x) * 2 + place.core) * 8 + z) * 2 + (y & 1)) * 2) + r
    columns = lax.broadcasted_iota(jnp.int32, (256, D), 1)
    return jnp.where(columns == row, 1.0, 0.0).astype(BF16)


def dot(a, b, ca=1, cb=0):
    return lax.dot_general(a, b, (((ca,), (cb,)), ((), ())), preferred_element_type=F32)


class Copies:
    def __init__(self, send_sems, recv_sems):
        self.send_sems, self.recv_sems, self.used, self.started = send_sems, recv_sems, 0, []

    def send(self, src, dst, target):
        k = self.used
        self.used += 1
        copy = pltpu.make_async_remote_copy(
            src_ref=src,
            dst_ref=dst,
            send_sem=self.send_sems.at[k],
            recv_sem=self.recv_sems.at[k],
            device_id=target,
            device_id_type=MESH,
        )
        copy.start()
        self.started.append(copy)
        return copy

    def drain(self):
        for copy in self.started:
            copy.wait_send()


class Part:
    def __init__(self, place, copies, part, width, scr, emit, out_ref):
        self.place, self.copies, self.scr, self.width = place, copies, scr, width
        self.first, self.second, self.third = ORDERS[part]
        self.n1, self.n2, self.n3 = (SIZES[a] for a in ORDERS[part])
        self.rows1 = 256 // self.n1
        self.rows2 = self.rows1 // self.n2
        self.emit, self.out_ref = emit, out_ref
        self.pending = []

    def multiply(self, lhs, rhs, src, at, count):
        value = dot(lhs[...], rhs[:, src : src + count])
        self.scr["own"][:, at : at + count] = value[: self.rows1]
        self.scr["send1"][:, at : at + count] = value[self.rows1 :].astype(BF16)

    def send_first(self, at, count):
        r = self.rows1
        for j in range(1, self.n1):
            here = (pl.ds((j - 1) * r, r), pl.ds(at, count))
            self.pending.append(
                self.copies.send(
                    self.scr["send1"].at[here], self.scr["recv1"].at[here], self.place.shifted(self.first, j)
                )
            )

    def arrive(self):
        for copy in self.pending:
            copy.wait_recv()
        self.pending = []

    def second_step(self):
        self.arrive()
        scr, r1, r = self.scr, self.rows1, self.rows2
        whole = None
        if r < 16:
            whole = scr["own"][...]
            for i in range(self.n1 - 1):
                whole = whole + scr["recv1"][i * r1 : i * r1 + r1].astype(F32)
        for j in (2, 1, 3, 0):
            rows = slice(j * r, j * r + r)
            if r < 16:
                total = whole[rows]
            else:
                total = scr["own"][rows]
                for i in range(self.n1 - 1):
                    total = total + scr["recv1"][i * r1 + j * r : i * r1 + j * r + r].astype(F32)
            if j == 0:
                scr["own"][rows] = total
            else:
                here = pl.ds((j - 1) * r, r)
                scr["send2"][(j - 1) * r : j * r] = total.astype(scr["send2"].dtype)
                self.pending.append(
                    self.copies.send(
                        scr["send2"].at[here], scr["recv2"].at[here], self.place.shifted(self.second, j)
                    )
                )

    def third_step(self):
        self.arrive()
        scr, r = self.scr, self.rows2
        total = scr["own"][0:r]
        for i in range(self.n2 - 1):
            total = total + scr["recv2"][i * r : i * r + r].astype(F32)
        slots = scr["wide3"].shape[0] // (2 * self.n3)
        for c in range(self.width // 128):
            scr["wide3"][pl.ds(c, 2 * self.n3, stride=slots), :] = total[:, c * 128 : (c + 1) * 128]
        each = 2 * slots
        scr["send3"][...] = scr["wide3"][each:].astype(BF16)
        for j in range(1, self.n3):
            here = pl.ds((j - 1) * each, each)
            self.pending.append(
                self.copies.send(scr["send3"].at[here], scr["recv3"].at[here], self.place.shifted(self.third, j))
            )

    def finish(self):
        self.arrive()
        scr = self.scr
        slots = scr["wide3"].shape[0] // (2 * self.n3)
        each = 2 * slots
        total = scr["wide3"][0:each]
        for i in range(self.n3 - 1):
            total = total + scr["recv3"][i * each : (i + 1) * each].astype(F32)
        total = total * grad_scale
        for r in range(2):
            for local, whole, count in self.emit:
                self.out_ref[r * 48 + whole : r * 48 + whole + count, :] = total[
                    r * slots + local : r * slots + local + count, :
                ]


def part_scratch(part, width):
    n1, n2, n3 = (SIZES[a] for a in ORDERS[part])
    r1 = 256 // n1
    r2 = r1 // n2
    slots = -(-(width // 128) // 8) * 8
    mid = BF16 if r2 >= 16 else F32
    return dict(
        own=pltpu.VMEM((r1, width), F32),
        send1=pltpu.VMEM((256 - r1, width), BF16),
        recv1=pltpu.VMEM((256 - r1, width), BF16),
        send2=pltpu.VMEM((r1 - r2, width), mid),
        recv2=pltpu.VMEM((r1 - r2, width), mid),
        wide3=pltpu.VMEM((2 * n3 * slots, 128), F32),
        send3=pltpu.VMEM((2 * (n3 - 1) * slots, 128), BF16),
        recv3=pltpu.VMEM((2 * (n3 - 1) * slots, 128), BF16),
    )


EARLY = (2048, 2048, 512)
LATE = (768, 768)
EARLY_OUT = (((0, 16, 16),), ((0, 32, 16),), ((0, 12, 4),))
LATE_OUT = (((0, 0, 2), (2, 8, 1), (3, 2, 2), (5, 10, 1)), ((0, 4, 2), (2, 9, 1), (3, 6, 2), (5, 11, 1)))


def greet(place):
    barrier = pltpu.get_barrier_semaphore()
    peers = [place.shifted("core")]
    for axis in ("x", "y", "z"):
        peers += [place.shifted(axis, by) for by in range(1, SIZES[axis])]
    for by in (1, 15):
        peers += [place.neighbour(by, 0), place.neighbour(0, by), place.neighbour(by, by)]
    for peer in peers:
        pl.semaphore_signal(barrier, inc=1, device_id=peer, device_id_type=MESH)
    return lambda: pl.semaphore_wait(barrier, len(peers))


PACKED = 320
SECTIONS = ((112, 112, 1, 0), (224, 48, 0, 1), (272, 48, 1, 1))


def token_of(s):
    big = s < 224
    second = ((s >= 112) & (s < 224)) | (s >= 272)
    u = jnp.where(big, s - jnp.where(s >= 112, 112, 0), s - jnp.where(s >= 272, 272, 224))
    low = jnp.where(second, 0, 3)
    wide = big & (u < 72)
    u2 = jnp.where(big, u - 72, u)
    lev_w = (u >= 36).astype(jnp.int32)
    m_w = u - 36 * lev_w
    row_w = (m_w >= 12).astype(jnp.int32) + (m_w >= 24).astype(jnp.int32)
    col_w = 6 + m_w - 12 * row_w
    lev_n = (u2 >= 18).astype(jnp.int32)
    m_n = u2 - 18 * lev_n
    row_n = (m_n >= 6).astype(jnp.int32) + (m_n >= 12).astype(jnp.int32)
    col_n = jnp.where(big, 18, 0) + m_n - 6 * row_n
    lev = jnp.where(wide, lev_w, lev_n)
    row = jnp.where(wide, row_w, row_n) + low
    col = jnp.where(wide, col_w, col_n)
    empty = u >= jnp.where(big, 108, 36)
    return jnp.where(empty, -1, lev * 144 + row * 24 + col)


def packed_of(w):
    at = jnp.where(w < 72, w, w + 40)
    at = jnp.where(w >= 144, w - 72, at)
    at = jnp.where(w >= 180, w + 44, at)
    at = jnp.where(w >= 216, w - 32, at)
    return jnp.where(w >= 252, w + 20, at)


def iota(shape, dim):
    return lax.broadcasted_iota(jnp.int32, shape, dim)


def ones_at(same):
    return jnp.where(same, 1.0, 0.0).astype(BF16)


def pack_matrix():
    return ones_at(token_of(iota((PACKED, 1), 0)) == iota((PACKED, NT), 1))


def unpack_matrix():
    return ones_at(token_of(iota((1, PACKED), 1)) == iota((NT, PACKED), 0))


def window_matrix():
    return ones_at(packed_of(iota((NT, 1), 0)) == iota((NT, PACKED), 1))


def unwindow_matrix():
    return ones_at(packed_of(iota((1, NT), 1)) == iota((PACKED, NT), 0))


def normalize(values):
    centre = values - jnp.mean(values, axis=-1, keepdims=True)
    inv_std = lax.rsqrt(jnp.mean(centre * centre, axis=-1, keepdims=True) + epsilon)
    return centre * inv_std, inv_std


def norm_back(upstream, normed, inv_std):
    mean_up = jnp.mean(upstream, axis=-1, keepdims=True)
    mean_dot = jnp.mean(upstream * normed, axis=-1, keepdims=True)
    return inv_std * (upstream - mean_up - normed * mean_dot)


def head_stack(value):
    lane = iota((144, 128), 1)
    zero = jnp.zeros_like(value)
    return jnp.concatenate([jnp.where((lane >> 5) == j, value, zero) for j in range(4)], axis=0)


def head_merge(value):
    lane = iota((144, 128), 1) >> 5
    out = value[432:576]
    for j in range(3):
        out = jnp.where(lane == j, value[144 * j : 144 * j + 144], out)
    return out


OWN, SIB = slice(0, NT), slice(NT, 2 * NT)


def block_kernel(
    x_ref, c_ref, wqkv_hbm, wproj_hbm, wfc1_hbm, wfc2_hbm,
    out_ref, gin_ref, wg_ref,
    early, late, orders_ref, wqkv, wproj, wfc1, wfc2,
    packs, arrived, maps_p, maps_w, act, gh, n1b, n2b, cot, ctx, gr, gm,
    lhs_n1, lhs_n2, lhs_cot, lhs_ctx, qkv, probs, bias, gctx, f32s, cols,
    send_sems, recv_sems, weight_sems,
):
    place = Place()
    copies = Copies(send_sems, recv_sems)
    met = greet(place)
    loads = [
        pltpu.make_async_copy(src, dst, weight_sems.at[i])
        for i, (src, dst) in enumerate(((wqkv_hbm, wqkv), (wproj_hbm, wproj), (wfc1_hbm, wfc1), (wfc2_hbm, wfc2)))
    ]
    for load in loads:
        load.start()
    X, N1, N2 = 0, 1, 2
    R1, R2 = 0, 1

    def share(ref, at=0, count=None):
        here = pl.ds(at, ref.shape[1] if count is None else count)
        return copies.send(ref.at[pl.ds(0, NT), here], ref.at[pl.ds(NT, NT), here], place.shifted("core"))

    early = [
        Part(place, copies, i, width, scr, emit, wg_ref) for i, (width, scr, emit) in enumerate(zip(EARLY, early, EARLY_OUT))
    ]
    late = [
        Part(place, copies, i, width, scr, emit, wg_ref) for i, (width, scr, emit) in enumerate(zip(LATE, late, LATE_OUT))
    ]

    maps_p[0] = pack_matrix()
    packs[0] = dot(maps_p[0], x_ref[...]).astype(BF16)
    packs[1] = dot(maps_p[0], c_ref[...]).astype(BF16)
    maps_w[0] = window_matrix()
    maps_p[1] = unwindow_matrix()
    maps_w[1] = unpack_matrix()
    for part, order in enumerate(ORDERS):
        orders_ref[part] = row_order(place, order)
    apart = ((iota((144, 144), 0) >= 72) != (iota((144, 144), 1) >= 72)) & (place.lat == 15)
    bias[...] = jnp.where(apart, neg_fill, 0.0)
    met()
    halos = []
    for i in range(2):
        halos.append(
            [
                copies.send(
                    packs.at[i, pl.ds(at, count)],
                    arrived.at[i, pl.ds(at, count)],
                    place.neighbour(16 - a if a else 0, 16 - b if b else 0),
                )
                for at, count, a, b in SECTIONS
            ]
        )
        arrived[i, 0:112] = packs[i, 0:112]

    def return_home(slot, value):
        packs[slot] = dot(maps_p[1], value).astype(BF16)
        sent = [
            copies.send(
                packs.at[slot, pl.ds(at, count)],
                arrived.at[slot, pl.ds(at, count)],
                place.neighbour(a, b),
            )
            for at, count, a, b in SECTIONS
        ]
        arrived[slot, 0:112] = packs[slot, 0:112]
        return sent

    def arrive_home(slot, sent, ref):
        for copy in sent:
            copy.wait_recv()
        ref[...] = dot(maps_w[1], arrived[slot]).astype(BF16)

    for copy in halos[0]:
        copy.wait_recv()
    x = dot(maps_w[0], arrived[0])
    f32s[X] = x
    normed, inv_std = normalize(x)
    f32s[N1] = normed
    cols[R1] = inv_std
    n1b[OWN] = normed.astype(BF16)
    shared_n1 = share(n1b)
    loads[0].wait()
    for i in range(3):
        part = dot(n1b[OWN], wqkv[:, 512 * i : 512 * i + 512])
        if i == 0:
            part = part * 32 ** (-0.5)
        qkv[:, 512 * i : 512 * i + 512] = part.astype(BF16)

    def group(w, g):
        rows = slice(144 * w, 144 * w + 144)
        return rows, [slice(512 * j + 128 * g, 512 * j + 128 * g + 128) for j in range(3)]

    for w in range(2):
        for g in range(4):
            rows, (lq, lk, lv) = group(w, g)
            scores = dot(head_stack(qkv[rows, lq]), qkv[rows, lk], 1, 1)
            scores = scores + jnp.concatenate([bias[...]] * 4, axis=0)
            raised = jnp.exp(scores - jnp.max(scores, axis=-1, keepdims=True))
            p = raised * (1.0 / jnp.sum(raised, axis=-1, keepdims=True))
            probs[4 * w + g] = p
            ctx[rows, lq] = head_merge(dot(p.astype(BF16), qkv[rows, lv])).astype(BF16)

    shared_ctx = share(ctx)
    loads[1].wait()
    branch = dot(ctx[OWN], wproj[...]).astype(BF16)
    residual = (f32s[X] + branch.astype(F32)).astype(BF16)
    resid32 = residual.astype(F32)
    f32s[X] = resid32
    normed, inv_std = normalize(resid32)
    f32s[N2] = normed
    cols[R2] = inv_std
    n2b[OWN] = normed.astype(BF16)
    shared_n2 = share(n2b)

    for copy in halos[1]:
        copy.wait_recv()
    cot[OWN] = dot(maps_w[0], arrived[1]).astype(BF16)
    shared_cot = share(cot)
    loads[2].wait()
    loads[3].wait()
    shared_ff = []

    def forward_tile(t):
        tile = slice(512 * t, 512 * t + 512)
        hidden = dot(n2b[OWN], wfc1[:, tile])
        upper = 0.5 * (1.0 + lax.erf(hidden * inv_root_two))
        act[OWN, tile] = (hidden * upper).astype(BF16)
        slope = upper + hidden * inv_root_tau * jnp.exp(-0.5 * hidden * hidden)
        gh[OWN, tile] = (dot(cot[OWN], wfc2[tile, :], 1, 1) * slope).astype(BF16)
        shared_ff.append((share(act, 512 * t, 512), share(gh, 512 * t, 512)))

    def quarter(t):
        for copy in shared_ff[t]:
            copy.wait_recv()
        for part, lhs, rhs in ((0, lhs_n2, gh), (1, lhs_cot, act)):
            early[part].multiply(lhs, rhs, 512 * t, 512 * t, 512)
            early[part].send_first(512 * t, 512)

    forward_tile(0)
    forward_tile(1)
    shared_n2.wait_recv()
    shared_cot.wait_recv()
    lhs_n2[...] = dot(orders_ref[0], n2b[...], 1, 1).astype(BF16)
    lhs_cot[...] = dot(orders_ref[1], cot[...], 1, 1).astype(BF16)
    quarter(0)
    forward_tile(2)
    quarter(1)
    forward_tile(3)
    quarter(2)
    grad_n2 = dot(gh[OWN], wfc1[...], 1, 1)
    grad_resid = (cot[OWN].astype(F32) + norm_back(grad_n2, f32s[N2], cols[R2])).astype(BF16)
    gr[OWN] = grad_resid
    shared_gr = share(gr)
    quarter(3)
    block_out = (f32s[X] + dot(act[OWN], wfc2[...])).astype(BF16)
    out_sent = return_home(2, block_out)
    gctx[...] = dot(gr[OWN], wproj[...], 1, 1).astype(BF16)
    shared_ctx.wait_recv()
    lhs_ctx[...] = dot(orders_ref[2], ctx[...], 1, 1).astype(BF16)
    shared_gr.wait_recv()
    early[2].multiply(lhs_ctx, gr, 0, 0, 512)
    early[2].send_first(0, 512)

    shared_n1.wait_recv()
    for i in range(2):
        lhs_n1[i] = dot(orders_ref[i], n1b[...], 1, 1).astype(BF16)

    def late_half(h, shared):
        for copy in shared:
            copy.wait_recv()
        for i in range(2):
            late[i].multiply(lhs_n1.at[i], gm, 512 * i + 256 * h, 384 * h, 256)
            late[i].multiply(lhs_n1.at[i], gm, 1024 + 256 * h + 128 * i, 384 * h + 256, 128)
            late[i].send_first(384 * h, 384)

    shared_gm = []
    for g in range(4):
        for w in range(2):
            rows, (lq, lk, lv) = group(w, g)
            grad = head_stack(gctx[rows, lq])
            p = probs[4 * w + g]
            grad_p = dot(grad, qkv[rows, lv], 1, 1)
            grad_s = (p * (grad_p - jnp.sum(grad_p * p, axis=-1, keepdims=True))).astype(BF16)
            gm[rows, lv] = dot(p.astype(BF16), grad, 0, 0).astype(BF16)
            gm[rows, lq] = (head_merge(dot(grad_s, qkv[rows, lk])) * 32 ** (-0.5)).astype(BF16)
            gm[rows, lk] = dot(grad_s, head_stack(qkv[rows, lq]), 0, 0).astype(BF16)
        if g == 1:
            shared_gm.append([share(gm, 512 * j, 256) for j in range(3)])
        if g == 2:
            late_half(0, shared_gm[0])
        if g >= 2:
            shared_gm.append([share(gm, 512 * j + 128 * g, 128) for j in range(3)])

    grad_n1 = dot(gm[OWN], wqkv[...], 1, 1).astype(BF16)
    late_half(1, shared_gm[1] + shared_gm[2])
    for part in early:
        part.second_step()
    grad_in = gr[OWN].astype(F32) + norm_back(grad_n1.astype(F32), f32s[N1], cols[R1])
    in_sent = return_home(3, grad_in.astype(BF16))
    arrive_home(2, out_sent, out_ref)
    for part in late:
        part.second_step()
    for part in early:
        part.third_step()
    arrive_home(3, in_sent, gin_ref)
    for part in late:
        part.third_step()
    for part in early:
        part.finish()
    for part in late:
        part.finish()
    copies.drain()


def on_device(tokens, cotangent, w_qkv, w_proj, w_fc1, w_fc2):
    vmem = pl.BlockSpec(memory_space=pltpu.VMEM)
    hbm = pl.BlockSpec(memory_space=pl.ANY)
    both = 2 * NT
    out, gin, wg = pl.pallas_call(
        block_kernel,
        out_shape=(
            jax.ShapeDtypeStruct((NT, D), BF16),
            jax.ShapeDtypeStruct((NT, D), BF16),
            jax.ShapeDtypeStruct((96, 128), F32),
        ),
        in_specs=[vmem, vmem, hbm, hbm, hbm, hbm],
        out_specs=(vmem, vmem, vmem),
        scratch_shapes=[
            [part_scratch(i, w) for i, w in enumerate(EARLY)],
            [part_scratch(i, w) for i, w in enumerate(LATE)],
            pltpu.VMEM((3, 256, D), BF16),
            pltpu.VMEM((D, 3 * D), BF16),
            pltpu.VMEM((D, D), BF16),
            pltpu.VMEM((D, 4 * D), BF16),
            pltpu.VMEM((4 * D, D), BF16),
            pltpu.VMEM((4, PACKED, D), BF16),
            pltpu.VMEM((4, PACKED, D), BF16),
            pltpu.VMEM((2, PACKED, NT), BF16),
            pltpu.VMEM((2, NT, PACKED), BF16),
            pltpu.VMEM((both, 4 * D), BF16),
            pltpu.VMEM((both, 4 * D), BF16),
            pltpu.VMEM((both, D), BF16),
            pltpu.VMEM((both, D), BF16),
            pltpu.VMEM((both, D), BF16),
            pltpu.VMEM((both, D), BF16),
            pltpu.VMEM((both, D), BF16),
            pltpu.VMEM((both, 3 * D), BF16),
            pltpu.VMEM((3, 256, both), BF16),
            pltpu.VMEM((256, both), BF16),
            pltpu.VMEM((256, both), BF16),
            pltpu.VMEM((256, both), BF16),
            pltpu.VMEM((NT, 3 * D), BF16),
            pltpu.VMEM((8, 576, 144), F32),
            pltpu.VMEM((144, 144), F32),
            pltpu.VMEM((NT, D), BF16),
            pltpu.VMEM((3, NT, D), F32),
            pltpu.VMEM((2, NT, 1), F32),
            pltpu.SemaphoreType.DMA((128,)),
            pltpu.SemaphoreType.DMA((128,)),
            pltpu.SemaphoreType.DMA((4,)),
        ],
        compiler_params=pltpu.CompilerParams(
            collective_id=0, has_side_effects=True, vmem_limit_bytes=60 * 1024 * 1024
        ),
    )(tokens.reshape(NT, D), cotangent.reshape(NT, D), w_qkv, w_proj, w_fc1, w_fc2)
    return out.reshape(tokens.shape), gin.reshape(tokens.shape), wg


def solution(mesh):
    return jax.shard_map(
        on_device,
        mesh=mesh,
        in_specs=(P(None, "lat", "lon", None), P(None, "lat", "lon", None), P(), P(), P(), P()),
        out_specs=(
            P(None, "lat", "lon", None),
            P(None, "lat", "lon", None),
            P(("lat", "lon"), None),
        ),
        check_vma=False,
    )
```

```python
import jax
import jax.numpy as jnp
from jax import lax
from jax.experimental import pallas as pl
from jax.experimental.pallas import tpu as pltpu
from jax.sharding import PartitionSpec as P

MESH = pl.DeviceIdType.MESH
H = 16
D = 512
NT = 288
F32 = jnp.float32
BF16 = jnp.bfloat16

epsilon = 1e-05
neg_fill = -1e30
inv_root_two = 0.7071067811865476
inv_root_tau = 0.3989422804014327
grad_scale = 73728 ** (-0.5)


class Place:
    def __init__(self):
        lat, lon = lax.axis_index("lat"), lax.axis_index("lon")
        self.lat, self.lon = lat, lon
        self.core = lax.rem(lat, 2)
        self.x = lax.rem(lax.div(lat, 2), 4)
        self.y = lax.div(lat, 8) * 2 + lax.rem(lon, 2)
        self.z = lax.div(lon, 2)

    def shifted(self, axis=None, by=0):
        x, y, z, core = self.x, self.y, self.z, self.core
        if axis == "x":
            x = lax.rem(x + by, 4)
        elif axis == "y":
            y = lax.rem(y + by, 4)
        elif axis == "z":
            z = lax.rem(z + by, 8)
        elif axis == "core":
            core = 1 - core
        return (lax.div(y, 2) * 8 + x * 2 + core, z * 2 + lax.rem(y, 2))

    def neighbour(self, by_lat, by_lon):
        return (lax.rem(self.lat + by_lat, 16), lax.rem(self.lon + by_lon, 16))


SIZES = {"x": 4, "y": 4, "z": 8}
ORDERS = (("x", "y", "z"), ("y", "x", "z"), ("z", "x", "y"))


def row_order(place, order):
    p = lax.broadcasted_iota(jnp.int32, (256, 1), 0)
    r = p & 1
    rest = p >> 1
    off = {}
    for axis in reversed(order):
        bits = 3 if axis == "z" else 2
        off[axis] = rest & (SIZES[axis] - 1)
        rest = rest >> bits
    x = (off["x"] + place.x) & 3
    y = (off["y"] + place.y) & 3
    z = (off["z"] + place.z) & 7
    row = ((((((y >> 1) * 4 + x) * 2 + place.core) * 8 + z) * 2 + (y & 1)) * 2) + r
    columns = lax.broadcasted_iota(jnp.int32, (256, D), 1)
    return jnp.where(columns == row, 1.0, 0.0).astype(BF16)


def dot(a, b, ca=1, cb=0):
    return lax.dot_general(a, b, (((ca,), (cb,)), ((), ())), preferred_element_type=F32)


class Copies:
    def __init__(self, send_sems, recv_sems):
        self.send_sems, self.recv_sems, self.used, self.started = send_sems, recv_sems, 0, []

    def send(self, src, dst, target):
        k = self.used
        self.used += 1
        copy = pltpu.make_async_remote_copy(
            src_ref=src,
            dst_ref=dst,
            send_sem=self.send_sems.at[k],
            recv_sem=self.recv_sems.at[k],
            device_id=target,
            device_id_type=MESH,
        )
        copy.start()
        self.started.append(copy)
        return copy

    def left(self, copy):
        copy.wait_send()
        self.started.remove(copy)

    def drain(self):
        for copy in self.started:
            copy.wait_send()


class Part:
    def __init__(self, place, copies, part, width, scr, emit, out_ref):
        self.place, self.copies, self.scr, self.width = place, copies, scr, width
        self.first, self.second, self.third = ORDERS[part]
        self.n1, self.n2, self.n3 = (SIZES[a] for a in ORDERS[part])
        self.rows1 = 256 // self.n1
        self.rows2 = self.rows1 // self.n2
        self.emit, self.out_ref = emit, out_ref
        self.pending = []

    def multiply(self, lhs, rhs, src, at, count):
        value = dot(lhs[...], rhs[:, src : src + count])
        self.scr["own"][:, at : at + count] = value[: self.rows1]
        self.scr["send1"][:, at : at + count] = value[self.rows1 :].astype(BF16)

    def send_first(self, at, count):
        r = self.rows1
        for j in range(1, self.n1):
            here = (pl.ds((j - 1) * r, r), pl.ds(at, count))
            self.pending.append(
                self.copies.send(
                    self.scr["send1"].at[here], self.scr["recv1"].at[here], self.place.shifted(self.first, j)
                )
            )

    def arrive(self):
        for copy in self.pending:
            copy.wait_recv()
        self.pending = []

    def second_step(self):
        self.arrive()
        scr, r1, r = self.scr, self.rows1, self.rows2
        whole = None
        if r < 16:
            whole = scr["own"][...]
            for i in range(self.n1 - 1):
                whole = whole + scr["recv1"][i * r1 : i * r1 + r1].astype(F32)
        for j in (2, 1, 3, 0):
            rows = slice(j * r, j * r + r)
            if r < 16:
                total = whole[rows]
            else:
                total = scr["own"][rows]
                for i in range(self.n1 - 1):
                    total = total + scr["recv1"][i * r1 + j * r : i * r1 + j * r + r].astype(F32)
            if j == 0:
                scr["own"][rows] = total
            else:
                here = pl.ds((j - 1) * r, r)
                scr["send2"][(j - 1) * r : j * r] = total.astype(scr["send2"].dtype)
                self.pending.append(
                    self.copies.send(
                        scr["send2"].at[here], scr["recv2"].at[here], self.place.shifted(self.second, j)
                    )
                )

    def third_step(self):
        self.arrive()
        scr, r = self.scr, self.rows2
        total = scr["own"][0:r]
        for i in range(self.n2 - 1):
            total = total + scr["recv2"][i * r : i * r + r].astype(F32)
        slots = scr["wide3"].shape[0] // (2 * self.n3)
        for c in range(self.width // 128):
            scr["wide3"][pl.ds(c, 2 * self.n3, stride=slots), :] = total[:, c * 128 : (c + 1) * 128]
        each = 2 * slots
        scr["send3"][...] = scr["wide3"][each:].astype(BF16)
        for j in range(1, self.n3):
            here = pl.ds((j - 1) * each, each)
            self.pending.append(
                self.copies.send(scr["send3"].at[here], scr["recv3"].at[here], self.place.shifted(self.third, j))
            )

    def finish(self):
        self.arrive()
        scr = self.scr
        slots = scr["wide3"].shape[0] // (2 * self.n3)
        each = 2 * slots
        total = scr["wide3"][0:each]
        for i in range(self.n3 - 1):
            total = total + scr["recv3"][i * each : (i + 1) * each].astype(F32)
        total = total * grad_scale
        for r in range(2):
            for local, whole, count in self.emit:
                self.out_ref[r * 48 + whole : r * 48 + whole + count, :] = total[
                    r * slots + local : r * slots + local + count, :
                ]


def part_scratch(part, width):
    n1, n2, n3 = (SIZES[a] for a in ORDERS[part])
    r1 = 256 // n1
    r2 = r1 // n2
    slots = -(-(width // 128) // 8) * 8
    mid = BF16 if r2 >= 16 else F32
    return dict(
        own=pltpu.VMEM((r1, width), F32),
        send1=pltpu.VMEM((256 - r1, width), BF16),
        recv1=pltpu.VMEM((256 - r1, width), BF16),
        send2=pltpu.VMEM((r1 - r2, width), mid),
        recv2=pltpu.VMEM((r1 - r2, width), mid),
        wide3=pltpu.VMEM((2 * n3 * slots, 128), F32),
        send3=pltpu.VMEM((2 * (n3 - 1) * slots, 128), BF16),
        recv3=pltpu.VMEM((2 * (n3 - 1) * slots, 128), BF16),
    )


EARLY = (2048, 2048, 512)
LATE = (768, 768)
EARLY_OUT = (((0, 16, 16),), ((0, 32, 16),), ((0, 12, 4),))
LATE_OUT = (((0, 0, 2), (2, 8, 1), (3, 2, 2), (5, 10, 1)), ((0, 4, 2), (2, 9, 1), (3, 6, 2), (5, 11, 1)))


def greet(place):
    barrier = pltpu.get_barrier_semaphore()
    peers = [place.shifted("core")]
    for axis in ("x", "y", "z"):
        peers += [place.shifted(axis, by) for by in range(1, SIZES[axis])]
    for by in (1, 15):
        peers += [place.neighbour(by, 0), place.neighbour(0, by), place.neighbour(by, by)]
    for peer in peers:
        pl.semaphore_signal(barrier, inc=1, device_id=peer, device_id_type=MESH)
    return lambda: pl.semaphore_wait(barrier, len(peers))


PACKED = 320
SECTIONS = ((112, 112, 1, 0), (224, 48, 0, 1), (272, 48, 1, 1))


def token_of(s):
    big = s < 224
    second = ((s >= 112) & (s < 224)) | (s >= 272)
    u = jnp.where(big, s - jnp.where(s >= 112, 112, 0), s - jnp.where(s >= 272, 272, 224))
    low = jnp.where(second, 0, 3)
    wide = big & (u < 72)
    u2 = jnp.where(big, u - 72, u)
    lev_w = (u >= 36).astype(jnp.int32)
    m_w = u - 36 * lev_w
    row_w = (m_w >= 12).astype(jnp.int32) + (m_w >= 24).astype(jnp.int32)
    col_w = 6 + m_w - 12 * row_w
    lev_n = (u2 >= 18).astype(jnp.int32)
    m_n = u2 - 18 * lev_n
    row_n = (m_n >= 6).astype(jnp.int32) + (m_n >= 12).astype(jnp.int32)
    col_n = jnp.where(big, 18, 0) + m_n - 6 * row_n
    lev = jnp.where(wide, lev_w, lev_n)
    row = jnp.where(wide, row_w, row_n) + low
    col = jnp.where(wide, col_w, col_n)
    empty = u >= jnp.where(big, 108, 36)
    return jnp.where(empty, -1, lev * 144 + row * 24 + col)


def packed_of(w):
    at = jnp.where(w < 72, w, w + 40)
    at = jnp.where(w >= 144, w - 72, at)
    at = jnp.where(w >= 180, w + 44, at)
    at = jnp.where(w >= 216, w - 32, at)
    return jnp.where(w >= 252, w + 20, at)


def iota(shape, dim):
    return lax.broadcasted_iota(jnp.int32, shape, dim)


def ones_at(same):
    return jnp.where(same, 1.0, 0.0).astype(BF16)


def pack_matrix():
    return ones_at(token_of(iota((PACKED, 1), 0)) == iota((PACKED, NT), 1))


def unpack_matrix():
    return ones_at(token_of(iota((1, PACKED), 1)) == iota((NT, PACKED), 0))


def window_matrix():
    return ones_at(packed_of(iota((NT, 1), 0)) == iota((NT, PACKED), 1))


def unwindow_matrix():
    return ones_at(packed_of(iota((1, NT), 1)) == iota((PACKED, NT), 0))


def normalize(values):
    centre = values - jnp.mean(values, axis=-1, keepdims=True)
    inv_std = lax.rsqrt(jnp.mean(centre * centre, axis=-1, keepdims=True) + epsilon)
    return centre * inv_std, inv_std


def norm_back(upstream, normed, inv_std):
    mean_up = jnp.mean(upstream, axis=-1, keepdims=True)
    mean_dot = jnp.mean(upstream * normed, axis=-1, keepdims=True)
    return inv_std * (upstream - mean_up - normed * mean_dot)


def head_stack(value):
    lane = iota((144, 128), 1)
    zero = jnp.zeros_like(value)
    return jnp.concatenate([jnp.where((lane >> 5) == j, value, zero) for j in range(4)], axis=0)


def head_merge(value):
    lane = iota((144, 128), 1) >> 5
    out = value[432:576]
    for j in range(3):
        out = jnp.where(lane == j, value[144 * j : 144 * j + 144], out)
    return out


OWN, SIB = slice(0, NT), slice(NT, 2 * NT)


def block_kernel(
    x_hbm, c_hbm, wqkv_hbm, wproj_hbm, wfc1_hbm, wfc2_hbm,
    out_hbm, gin_hbm, wg_ref,
    early, late, orders_ref, wqkv, wproj, wfc1, wfc2,
    packs, arrived, maps_p, maps_w, act, gh, n1b, n2b, cot, ctx, gr, gm,
    lhs_n1, lhs_n2, lhs_cot, lhs_ctx, qkv, probs, bias, gctx, f32s, cols, ends,
    send_sems, recv_sems, local_sems,
):
    place = Place()
    copies = Copies(send_sems, recv_sems)
    met = greet(place)
    loads = [
        pltpu.make_async_copy(src, dst, local_sems.at[i])
        for i, (src, dst) in enumerate(
            (
                (x_hbm, ends.at[0]),
                (c_hbm, ends.at[1]),
                (wqkv_hbm, wqkv),
                (wproj_hbm, wproj),
                (wfc1_hbm, wfc1),
                (wfc2_hbm, wfc2),
            )
        )
    ]
    for load in loads:
        load.start()
    X, N1, N2 = 0, 1, 2
    R1, R2 = 0, 1

    def share(ref, at=0, count=None):
        here = pl.ds(at, ref.shape[1] if count is None else count)
        return copies.send(ref.at[pl.ds(0, NT), here], ref.at[pl.ds(NT, NT), here], place.shifted("core"))

    early = [
        Part(place, copies, i, width, scr, emit, wg_ref) for i, (width, scr, emit) in enumerate(zip(EARLY, early, EARLY_OUT))
    ]
    late = [
        Part(place, copies, i, width, scr, emit, wg_ref) for i, (width, scr, emit) in enumerate(zip(LATE, late, LATE_OUT))
    ]

    maps_p[0] = pack_matrix()
    for i in range(2):
        loads[i].wait()
        packs[i] = dot(maps_p[0], ends[i]).astype(BF16)
    maps_w[0] = window_matrix()
    maps_p[1] = unwindow_matrix()
    maps_w[1] = unpack_matrix()
    for part, order in enumerate(ORDERS):
        orders_ref[part] = row_order(place, order)
    apart = ((iota((144, 144), 0) >= 72) != (iota((144, 144), 1) >= 72)) & (place.lat == 15)
    bias[...] = jnp.where(apart, neg_fill, 0.0)
    met()
    halos = []
    for i in range(2):
        if i:
            for copy in halos[0]:
                copies.left(copy)
        halos.append(
            [
                copies.send(
                    packs.at[i, pl.ds(at, count)],
                    arrived.at[i, pl.ds(at, count)],
                    place.neighbour(16 - a if a else 0, 16 - b if b else 0),
                )
                for at, count, a, b in SECTIONS
            ]
        )
        arrived[i, 0:112] = packs[i, 0:112]

    def return_home(slot, value):
        packs[slot] = dot(maps_p[1], value).astype(BF16)
        sent = [
            copies.send(
                packs.at[slot, pl.ds(at, count)],
                arrived.at[slot, pl.ds(at, count)],
                place.neighbour(a, b),
            )
            for at, count, a, b in SECTIONS
        ]
        arrived[slot, 0:112] = packs[slot, 0:112]
        return sent

    def arrive_home(slot, sent, ref):
        for copy in sent:
            copy.wait_recv()
        ends[slot] = dot(maps_w[1], arrived[slot]).astype(BF16)
        store = pltpu.make_async_copy(ends.at[slot], ref, local_sems.at[4 + slot])
        store.start()
        return store

    for copy in halos[0]:
        copy.wait_recv()
    x = dot(maps_w[0], arrived[0])
    f32s[X] = x
    normed, inv_std = normalize(x)
    f32s[N1] = normed
    cols[R1] = inv_std
    n1b[OWN] = normed.astype(BF16)
    shared_n1 = share(n1b)
    loads[2].wait()
    for i in range(3):
        part = dot(n1b[OWN], wqkv[:, 512 * i : 512 * i + 512])
        if i == 0:
            part = part * 32 ** (-0.5)
        qkv[:, 512 * i : 512 * i + 512] = part.astype(BF16)

    def group(w, g):
        rows = slice(144 * w, 144 * w + 144)
        return rows, [slice(512 * j + 128 * g, 512 * j + 128 * g + 128) for j in range(3)]

    for w in range(2):
        for g in range(4):
            rows, (lq, lk, lv) = group(w, g)
            scores = dot(head_stack(qkv[rows, lq]), qkv[rows, lk], 1, 1)
            scores = scores + jnp.concatenate([bias[...]] * 4, axis=0)
            raised = jnp.exp(scores - jnp.max(scores, axis=-1, keepdims=True))
            p = raised * (1.0 / jnp.sum(raised, axis=-1, keepdims=True))
            probs[4 * w + g] = p
            ctx[rows, lq] = head_merge(dot(p.astype(BF16), qkv[rows, lv])).astype(BF16)

    shared_ctx = share(ctx)
    loads[3].wait()
    branch = dot(ctx[OWN], wproj[...]).astype(BF16)
    residual = (f32s[X] + branch.astype(F32)).astype(BF16)
    resid32 = residual.astype(F32)
    f32s[X] = resid32
    normed, inv_std = normalize(resid32)
    f32s[N2] = normed
    cols[R2] = inv_std
    n2b[OWN] = normed.astype(BF16)
    shared_n2 = share(n2b)

    for copy in halos[1]:
        copy.wait_recv()
    cot[OWN] = dot(maps_w[0], arrived[1]).astype(BF16)
    shared_cot = share(cot)
    loads[4].wait()
    loads[5].wait()
    shared_ff = []

    def forward_tile(t):
        tile = slice(512 * t, 512 * t + 512)
        hidden = dot(n2b[OWN], wfc1[:, tile])
        upper = 0.5 * (1.0 + lax.erf(hidden * inv_root_two))
        act[OWN, tile] = (hidden * upper).astype(BF16)
        slope = upper + hidden * inv_root_tau * jnp.exp(-0.5 * hidden * hidden)
        gh[OWN, tile] = (dot(cot[OWN], wfc2[tile, :], 1, 1) * slope).astype(BF16)
        shared_ff.append((share(act, 512 * t, 512), share(gh, 512 * t, 512)))

    def quarter(t):
        for copy in shared_ff[t]:
            copy.wait_recv()
        for part, lhs, rhs in ((0, lhs_n2, gh), (1, lhs_cot, act)):
            early[part].multiply(lhs, rhs, 512 * t, 512 * t, 512)
            early[part].send_first(512 * t, 512)

    forward_tile(0)
    forward_tile(1)
    shared_n2.wait_recv()
    shared_cot.wait_recv()
    lhs_n2[...] = dot(orders_ref[0], n2b[...], 1, 1).astype(BF16)
    lhs_cot[...] = dot(orders_ref[1], cot[...], 1, 1).astype(BF16)
    quarter(0)
    forward_tile(2)
    quarter(1)
    forward_tile(3)
    quarter(2)
    grad_n2 = dot(gh[OWN], wfc1[...], 1, 1)
    grad_resid = (cot[OWN].astype(F32) + norm_back(grad_n2, f32s[N2], cols[R2])).astype(BF16)
    gr[OWN] = grad_resid
    shared_gr = share(gr)
    quarter(3)
    block_out = (f32s[X] + dot(act[OWN], wfc2[...])).astype(BF16)
    out_sent = return_home(2, block_out)
    gctx[...] = dot(gr[OWN], wproj[...], 1, 1).astype(BF16)
    shared_ctx.wait_recv()
    lhs_ctx[...] = dot(orders_ref[2], ctx[...], 1, 1).astype(BF16)
    shared_gr.wait_recv()
    early[2].multiply(lhs_ctx, gr, 0, 0, 512)
    early[2].send_first(0, 512)

    shared_n1.wait_recv()
    for i in range(2):
        lhs_n1[i] = dot(orders_ref[i], n1b[...], 1, 1).astype(BF16)

    def late_half(h, shared):
        for copy in shared:
            copy.wait_recv()
        for i in range(2):
            late[i].multiply(lhs_n1.at[i], gm, 512 * i + 256 * h, 384 * h, 256)
            late[i].multiply(lhs_n1.at[i], gm, 1024 + 256 * h + 128 * i, 384 * h + 256, 128)
            late[i].send_first(384 * h, 384)

    shared_gm = []
    for g in range(4):
        for w in range(2):
            rows, (lq, lk, lv) = group(w, g)
            grad = head_stack(gctx[rows, lq])
            p = probs[4 * w + g]
            grad_p = dot(grad, qkv[rows, lv], 1, 1)
            grad_s = (p * (grad_p - jnp.sum(grad_p * p, axis=-1, keepdims=True))).astype(BF16)
            gm[rows, lv] = dot(p.astype(BF16), grad, 0, 0).astype(BF16)
            gm[rows, lq] = (head_merge(dot(grad_s, qkv[rows, lk])) * 32 ** (-0.5)).astype(BF16)
            gm[rows, lk] = dot(grad_s, head_stack(qkv[rows, lq]), 0, 0).astype(BF16)
        if g == 1:
            shared_gm.append([share(gm, 512 * j, 256) for j in range(3)])
        if g == 2:
            late_half(0, shared_gm[0])
        if g >= 2:
            shared_gm.append([share(gm, 512 * j + 128 * g, 128) for j in range(3)])

    grad_n1 = dot(gm[OWN], wqkv[...], 1, 1).astype(BF16)
    late_half(1, shared_gm[1] + shared_gm[2])
    for part in early:
        part.second_step()
    grad_in = gr[OWN].astype(F32) + norm_back(grad_n1.astype(F32), f32s[N1], cols[R1])
    in_sent = return_home(3, grad_in.astype(BF16))
    out_stored = arrive_home(2, out_sent, out_hbm)
    for part in late:
        part.second_step()
    for part in early:
        part.third_step()
    gin_stored = arrive_home(3, in_sent, gin_hbm)
    for part in late:
        part.third_step()
    for part in early:
        part.finish()
    for part in late:
        part.finish()
    out_stored.wait()
    gin_stored.wait()
    copies.drain()


def hand_over(*refs):
    count = len(refs) // 2
    for i in range(count):
        refs[count + i][...] = refs[i][...]


def on_device(tokens, cotangent, w_qkv, w_proj, w_fc1, w_fc2):
    vmem = pl.BlockSpec(memory_space=pltpu.VMEM)
    hbm = pl.BlockSpec(memory_space=pl.ANY)
    both = 2 * NT
    out, gin, wg = pl.pallas_call(
        block_kernel,
        out_shape=(
            jax.ShapeDtypeStruct((NT, D), BF16),
            jax.ShapeDtypeStruct((NT, D), BF16),
            jax.ShapeDtypeStruct((96, 128), F32),
        ),
        in_specs=[hbm] * 6,
        out_specs=(hbm, hbm, vmem),
        scratch_shapes=[
            [part_scratch(i, w) for i, w in enumerate(EARLY)],
            [part_scratch(i, w) for i, w in enumerate(LATE)],
            pltpu.VMEM((3, 256, D), BF16),
            pltpu.VMEM((D, 3 * D), BF16),
            pltpu.VMEM((D, D), BF16),
            pltpu.VMEM((D, 4 * D), BF16),
            pltpu.VMEM((4 * D, D), BF16),
            pltpu.VMEM((4, PACKED, D), BF16),
            pltpu.VMEM((4, PACKED, D), BF16),
            pltpu.VMEM((2, PACKED, NT), BF16),
            pltpu.VMEM((2, NT, PACKED), BF16),
            pltpu.VMEM((both, 4 * D), BF16),
            pltpu.VMEM((both, 4 * D), BF16),
            pltpu.VMEM((both, D), BF16),
            pltpu.VMEM((both, D), BF16),
            pltpu.VMEM((both, D), BF16),
            pltpu.VMEM((both, D), BF16),
            pltpu.VMEM((both, D), BF16),
            pltpu.VMEM((both, 3 * D), BF16),
            pltpu.VMEM((3, 256, both), BF16),
            pltpu.VMEM((256, both), BF16),
            pltpu.VMEM((256, both), BF16),
            pltpu.VMEM((256, both), BF16),
            pltpu.VMEM((NT, 3 * D), BF16),
            pltpu.VMEM((8, 576, 144), F32),
            pltpu.VMEM((144, 144), F32),
            pltpu.VMEM((NT, D), BF16),
            pltpu.VMEM((3, NT, D), F32),
            pltpu.VMEM((2, NT, 1), F32),
            pltpu.VMEM((4, NT, D), BF16),
            pltpu.SemaphoreType.DMA((128,)),
            pltpu.SemaphoreType.DMA((128,)),
            pltpu.SemaphoreType.DMA((8,)),
        ],
        compiler_params=pltpu.CompilerParams(
            collective_id=0, has_side_effects=True, vmem_limit_bytes=60 * 1024 * 1024
        ),
    )(tokens.reshape(NT, D), cotangent.reshape(NT, D), w_qkv, w_proj, w_fc1, w_fc2)
    out, gin, wg = pl.pallas_call(
        hand_over,
        out_shape=tuple(jax.ShapeDtypeStruct(v.shape, v.dtype) for v in (out, gin, wg)),
        in_specs=[vmem] * 3,
        out_specs=(vmem,) * 3,
    )(out, gin, wg)
    return out.reshape(tokens.shape), gin.reshape(tokens.shape), wg


def solution(mesh):
    return jax.shard_map(
        on_device,
        mesh=mesh,
        in_specs=(P(None, "lat", "lon", None), P(None, "lat", "lon", None), P(), P(), P(), P()),
        out_specs=(
            P(None, "lat", "lon", None),
            P(None, "lat", "lon", None),
            P(("lat", "lon"), None),
        ),
        check_vma=False,
    )
```

```python
import jax
import jax.numpy as jnp
from jax import lax
from jax.experimental import pallas as pl
from jax.experimental.pallas import tpu as pltpu
from jax.sharding import PartitionSpec as P

MESH = pl.DeviceIdType.MESH
H = 16
D = 512
NT = 288
F32 = jnp.float32
BF16 = jnp.bfloat16

epsilon = 1e-05
neg_fill = -1e30
inv_root_two = 0.7071067811865476
inv_root_tau = 0.3989422804014327
grad_scale = 73728 ** (-0.5)


class Place:
    def __init__(self):
        lat, lon = lax.axis_index("lat"), lax.axis_index("lon")
        self.lat, self.lon = lat, lon
        self.core = lax.rem(lat, 2)
        self.x = lax.rem(lax.div(lat, 2), 4)
        self.y = lax.div(lat, 8) * 2 + lax.rem(lon, 2)
        self.z = lax.div(lon, 2)

    def shifted(self, axis=None, by=0):
        x, y, z, core = self.x, self.y, self.z, self.core
        if axis == "x":
            x = lax.rem(x + by, 4)
        elif axis == "y":
            y = lax.rem(y + by, 4)
        elif axis == "z":
            z = lax.rem(z + by, 8)
        elif axis == "core":
            core = 1 - core
        return (lax.div(y, 2) * 8 + x * 2 + core, z * 2 + lax.rem(y, 2))

    def neighbour(self, by_lat, by_lon):
        return (lax.rem(self.lat + by_lat, 16), lax.rem(self.lon + by_lon, 16))


SIZES = {"x": 4, "y": 4, "z": 8}
ORDERS = (("x", "y", "z"), ("y", "x", "z"), ("z", "x", "y"))


def row_order(place, order):
    p = lax.broadcasted_iota(jnp.int32, (256, 1), 0)
    r = p & 1
    rest = p >> 1
    off = {}
    for axis in reversed(order):
        bits = 3 if axis == "z" else 2
        off[axis] = rest & (SIZES[axis] - 1)
        rest = rest >> bits
    x = (off["x"] + place.x) & 3
    y = (off["y"] + place.y) & 3
    z = (off["z"] + place.z) & 7
    row = ((((((y >> 1) * 4 + x) * 2 + place.core) * 8 + z) * 2 + (y & 1)) * 2) + r
    columns = lax.broadcasted_iota(jnp.int32, (256, D), 1)
    return jnp.where(columns == row, 1.0, 0.0).astype(BF16)


def dot(a, b, ca=1, cb=0):
    return lax.dot_general(a, b, (((ca,), (cb,)), ((), ())), preferred_element_type=F32)


class Copies:
    def __init__(self, send_sems, recv_sems):
        self.send_sems, self.recv_sems, self.used, self.started = send_sems, recv_sems, 0, []

    def send(self, src, dst, target):
        k = self.used
        self.used += 1
        copy = pltpu.make_async_remote_copy(
            src_ref=src,
            dst_ref=dst,
            send_sem=self.send_sems.at[k],
            recv_sem=self.recv_sems.at[k],
            device_id=target,
            device_id_type=MESH,
        )
        copy.start()
        self.started.append(copy)
        return copy

    def left(self, copy):
        copy.wait_send()
        self.started.remove(copy)

    def drain(self):
        for copy in self.started:
            copy.wait_send()


class Part:
    def __init__(self, place, copies, part, width, scr, emit, out_ref):
        self.place, self.copies, self.scr, self.width = place, copies, scr, width
        self.first, self.second, self.third = ORDERS[part]
        self.n1, self.n2, self.n3 = (SIZES[a] for a in ORDERS[part])
        self.rows1 = 256 // self.n1
        self.rows2 = self.rows1 // self.n2
        self.emit, self.out_ref = emit, out_ref
        self.pending, self.relays, self.spans = [], [], []

    def multiply(self, lhs, rhs, src, at, count):
        value = dot(lhs[...], rhs[:, src : src + count])
        self.scr["own"][:, at : at + count] = value[: self.rows1]
        self.scr["send1"][:, at : at + count] = value[self.rows1 :].astype(BF16)

    def send_ring(self, at, count):
        r, half = self.rows1, count // 2
        lo, hi, kept = pl.ds(at, half), pl.ds(at + half, half), pl.ds(at // 2, half)
        plus, minus = self.place.shifted(self.first, 1), self.place.shifted(self.first, 3)
        near, opposite, far = pl.ds(0, r), pl.ds(r, r), pl.ds(2 * r, r)
        out, into, relay = self.scr["send1"], self.scr["recv1"], self.scr["relay"]
        first = self.copies.send(out.at[opposite, lo], relay.at[near, kept], plus)
        second = self.copies.send(out.at[opposite, hi], relay.at[opposite, kept], minus)
        self.pending.append(self.copies.send(out.at[near, hi], into.at[near, hi], plus))
        self.pending.append(self.copies.send(out.at[far, lo], into.at[far, lo], minus))
        self.relays.append((first, (near, lo, near, kept), plus))
        self.relays.append((second, (far, hi, opposite, kept), minus))
        self.spans.append((at, count, (0, 2)))

    def relay(self):
        out, into, relay = self.scr["send1"], self.scr["recv1"], self.scr["relay"]
        for copy, (rows, span, from_rows, kept), target in self.relays[:2]:
            copy.wait_recv()
            out[rows, span] = (out[rows, span].astype(F32) + relay[from_rows, kept].astype(F32)).astype(BF16)
            self.pending.append(self.copies.send(out.at[rows, span], into.at[rows, span], target))
        self.relays = self.relays[2:]

    def send_first(self, at, count):
        self.spans.append((at, count, range(self.n1 - 1)))
        r = self.rows1
        for j in range(1, self.n1):
            here = (pl.ds((j - 1) * r, r), pl.ds(at, count))
            self.pending.append(
                self.copies.send(
                    self.scr["send1"].at[here], self.scr["recv1"].at[here], self.place.shifted(self.first, j)
                )
            )

    def arrive(self):
        for copy in self.pending:
            copy.wait_recv()
        self.pending = []

    def second_step(self):
        self.arrive()
        scr, r1, r = self.scr, self.rows1, self.rows2
        fine = r % 16 == 0
        for at, count, slots in self.spans:
            span = slice(at, at + count)
            if not fine:
                whole = scr["own"][:, span]
                for i in slots:
                    whole = whole + scr["recv1"][i * r1 : i * r1 + r1, span].astype(F32)
            for j in range(self.n2):
                rows = slice(j * r, j * r + r)
                if fine:
                    total = scr["own"][rows, span]
                    for i in slots:
                        total = total + scr["recv1"][i * r1 + j * r : i * r1 + j * r + r, span].astype(F32)
                else:
                    total = whole[rows]
                if j == 0:
                    scr["own"][rows, span] = total
                else:
                    scr["send2"][(j - 1) * r : j * r, span] = total.astype(scr["send2"].dtype)
        for j in (2, 1, 3):
            here = pl.ds((j - 1) * r, r)
            self.pending.append(
                self.copies.send(scr["send2"].at[here], scr["recv2"].at[here], self.place.shifted(self.second, j))
            )

    def third_step(self):
        self.arrive()
        scr, r = self.scr, self.rows2
        total = scr["own"][0:r]
        for i in range(self.n2 - 1):
            total = total + scr["recv2"][i * r : i * r + r].astype(F32)
        slots = scr["wide3"].shape[0] // (2 * self.n3)
        for c in range(self.width // 128):
            scr["wide3"][pl.ds(c, 2 * self.n3, stride=slots), :] = total[:, c * 128 : (c + 1) * 128]
        each = 2 * slots
        scr["send3"][...] = scr["wide3"][each:].astype(BF16)
        for j in range(1, self.n3):
            here = pl.ds((j - 1) * each, each)
            self.pending.append(
                self.copies.send(scr["send3"].at[here], scr["recv3"].at[here], self.place.shifted(self.third, j))
            )

    def finish(self):
        self.arrive()
        scr = self.scr
        slots = scr["wide3"].shape[0] // (2 * self.n3)
        each = 2 * slots
        total = scr["wide3"][0:each]
        for i in range(self.n3 - 1):
            total = total + scr["recv3"][i * each : (i + 1) * each].astype(F32)
        total = total * grad_scale
        for r in range(2):
            for local, whole, count in self.emit:
                self.out_ref[r * 48 + whole : r * 48 + whole + count, :] = total[
                    r * slots + local : r * slots + local + count, :
                ]


def part_scratch(part, width):
    n1, n2, n3 = (SIZES[a] for a in ORDERS[part])
    r1 = 256 // n1
    r2 = r1 // n2
    slots = -(-(width // 128) // 8) * 8
    mid = BF16 if r2 >= 16 else F32
    return dict(
        own=pltpu.VMEM((r1, width), F32),
        send1=pltpu.VMEM((256 - r1, width), BF16),
        recv1=pltpu.VMEM((256 - r1, width), BF16),
        relay=pltpu.VMEM((2 * r1, width // 2), BF16),
        send2=pltpu.VMEM((r1 - r2, width), mid),
        recv2=pltpu.VMEM((r1 - r2, width), mid),
        wide3=pltpu.VMEM((2 * n3 * slots, 128), F32),
        send3=pltpu.VMEM((2 * (n3 - 1) * slots, 128), BF16),
        recv3=pltpu.VMEM((2 * (n3 - 1) * slots, 128), BF16),
    )


EARLY = (2048, 2048, 512)
LATE = (768, 768)
EARLY_OUT = (((0, 16, 16),), ((0, 32, 16),), ((0, 12, 4),))
LATE_OUT = (((0, 0, 2), (2, 8, 1), (3, 2, 1), (4, 10, 1), (5, 3, 1)), ((0, 4, 2), (2, 9, 1), (3, 6, 2), (5, 11, 1)))


def greet(place):
    barrier = pltpu.get_barrier_semaphore()
    peers = [place.shifted("core")]
    for axis in ("x", "y", "z"):
        peers += [place.shifted(axis, by) for by in range(1, SIZES[axis])]
    for by in (1, 15):
        peers += [place.neighbour(by, 0), place.neighbour(0, by), place.neighbour(by, by)]
    for peer in peers:
        pl.semaphore_signal(barrier, inc=1, device_id=peer, device_id_type=MESH)
    return lambda: pl.semaphore_wait(barrier, len(peers))


PACKED = 320
SECTIONS = ((112, 112, 1, 0), (224, 48, 0, 1), (272, 48, 1, 1))


def token_of(s):
    big = s < 224
    second = ((s >= 112) & (s < 224)) | (s >= 272)
    u = jnp.where(big, s - jnp.where(s >= 112, 112, 0), s - jnp.where(s >= 272, 272, 224))
    low = jnp.where(second, 0, 3)
    wide = big & (u < 72)
    u2 = jnp.where(big, u - 72, u)
    lev_w = (u >= 36).astype(jnp.int32)
    m_w = u - 36 * lev_w
    row_w = (m_w >= 12).astype(jnp.int32) + (m_w >= 24).astype(jnp.int32)
    col_w = 6 + m_w - 12 * row_w
    lev_n = (u2 >= 18).astype(jnp.int32)
    m_n = u2 - 18 * lev_n
    row_n = (m_n >= 6).astype(jnp.int32) + (m_n >= 12).astype(jnp.int32)
    col_n = jnp.where(big, 18, 0) + m_n - 6 * row_n
    lev = jnp.where(wide, lev_w, lev_n)
    row = jnp.where(wide, row_w, row_n) + low
    col = jnp.where(wide, col_w, col_n)
    empty = u >= jnp.where(big, 108, 36)
    return jnp.where(empty, -1, lev * 144 + row * 24 + col)


def packed_of(w):
    at = jnp.where(w < 72, w, w + 40)
    at = jnp.where(w >= 144, w - 72, at)
    at = jnp.where(w >= 180, w + 44, at)
    at = jnp.where(w >= 216, w - 32, at)
    return jnp.where(w >= 252, w + 20, at)


def iota(shape, dim):
    return lax.broadcasted_iota(jnp.int32, shape, dim)


def ones_at(same):
    return jnp.where(same, 1.0, 0.0).astype(BF16)


def pack_matrix():
    return ones_at(token_of(iota((PACKED, 1), 0)) == iota((PACKED, NT), 1))


def unpack_matrix():
    return ones_at(token_of(iota((1, PACKED), 1)) == iota((NT, PACKED), 0))


def window_matrix():
    return ones_at(packed_of(iota((NT, 1), 0)) == iota((NT, PACKED), 1))


def unwindow_matrix():
    return ones_at(packed_of(iota((1, NT), 1)) == iota((PACKED, NT), 0))


def normalize(values):
    centre = values - jnp.mean(values, axis=-1, keepdims=True)
    inv_std = lax.rsqrt(jnp.mean(centre * centre, axis=-1, keepdims=True) + epsilon)
    return centre * inv_std, inv_std


def norm_back(upstream, normed, inv_std):
    mean_up = jnp.mean(upstream, axis=-1, keepdims=True)
    mean_dot = jnp.mean(upstream * normed, axis=-1, keepdims=True)
    return inv_std * (upstream - mean_up - normed * mean_dot)


def head_stack(value):
    lane = iota((144, 128), 1)
    zero = jnp.zeros_like(value)
    return jnp.concatenate([jnp.where((lane >> 5) == j, value, zero) for j in range(4)], axis=0)


def head_merge(value):
    lane = iota((144, 128), 1) >> 5
    out = value[432:576]
    for j in range(3):
        out = jnp.where(lane == j, value[144 * j : 144 * j + 144], out)
    return out


OWN, SIB = slice(0, NT), slice(NT, 2 * NT)


def block_kernel(
    x_hbm, c_hbm, wqkv_hbm, wproj_hbm, wfc1_hbm, wfc2_hbm,
    out_hbm, gin_hbm, wg_ref,
    early, late, orders_ref, wqkv, wproj, wfc1, wfc2,
    packs, arrived, maps_p, maps_w, act, gh, n1b, n2b, cot, ctx, gr, gm,
    lhs_n1, lhs_n2, lhs_cot, lhs_ctx, qkv, probs, bias, gctx, f32s, cols, ends,
    send_sems, recv_sems, local_sems,
):
    place = Place()
    copies = Copies(send_sems, recv_sems)
    met = greet(place)
    loads = [
        pltpu.make_async_copy(src, dst, local_sems.at[i])
        for i, (src, dst) in enumerate(
            (
                (x_hbm, ends.at[0]),
                (c_hbm, ends.at[1]),
                (wqkv_hbm, wqkv),
                (wproj_hbm, wproj),
                (wfc1_hbm, wfc1),
                (wfc2_hbm, wfc2),
            )
        )
    ]
    for load in loads:
        load.start()
    X, N1, N2 = 0, 1, 2
    R1, R2 = 0, 1

    def share(ref, at=0, count=None):
        here = pl.ds(at, ref.shape[1] if count is None else count)
        return copies.send(ref.at[pl.ds(0, NT), here], ref.at[pl.ds(NT, NT), here], place.shifted("core"))

    early = [
        Part(place, copies, i, width, scr, emit, wg_ref) for i, (width, scr, emit) in enumerate(zip(EARLY, early, EARLY_OUT))
    ]
    late = [
        Part(place, copies, i, width, scr, emit, wg_ref) for i, (width, scr, emit) in enumerate(zip(LATE, late, LATE_OUT))
    ]

    maps_p[0] = pack_matrix()
    for i in range(2):
        loads[i].wait()
        packs[i] = dot(maps_p[0], ends[i]).astype(BF16)
    maps_w[0] = window_matrix()
    maps_p[1] = unwindow_matrix()
    maps_w[1] = unpack_matrix()
    for part, order in enumerate(ORDERS):
        orders_ref[part] = row_order(place, order)
    lane = iota((144, 576), 1)
    high = lane < 0
    for j in range(4):
        high = high | ((lane >= 144 * j + 72) & (lane < 144 * j + 144))
    apart = ((iota((144, 576), 0) >= 72) != high) & (place.lat == 15)
    bias[...] = jnp.where(apart, neg_fill, 0.0)
    met()
    halos = []
    for i in range(2):
        if i:
            for copy in halos[0]:
                copies.left(copy)
        halos.append(
            [
                copies.send(
                    packs.at[i, pl.ds(at, count)],
                    arrived.at[i, pl.ds(at, count)],
                    place.neighbour(16 - a if a else 0, 16 - b if b else 0),
                )
                for at, count, a, b in SECTIONS
            ]
        )
        arrived[i, 0:112] = packs[i, 0:112]

    def return_home(slot, value):
        packs[slot] = dot(maps_p[1], value).astype(BF16)
        sent = [
            copies.send(
                packs.at[slot, pl.ds(at, count)],
                arrived.at[slot, pl.ds(at, count)],
                place.neighbour(a, b),
            )
            for at, count, a, b in SECTIONS
        ]
        arrived[slot, 0:112] = packs[slot, 0:112]
        return sent

    def arrive_home(slot, sent, ref):
        for copy in sent:
            copy.wait_recv()
        ends[slot] = dot(maps_w[1], arrived[slot]).astype(BF16)
        store = pltpu.make_async_copy(ends.at[slot], ref, local_sems.at[4 + slot])
        store.start()
        return store

    for copy in halos[0]:
        copy.wait_recv()
    x = dot(maps_w[0], arrived[0])
    f32s[X] = x
    normed, inv_std = normalize(x)
    f32s[N1] = normed
    cols[R1] = inv_std
    n1b[OWN] = normed.astype(BF16)
    shared_n1 = share(n1b)
    loads[2].wait()
    for i in range(3):
        part = dot(n1b[OWN], wqkv[:, 512 * i : 512 * i + 512])
        if i == 0:
            part = part * 32 ** (-0.5)
        qkv[:, 512 * i : 512 * i + 512] = part.astype(BF16)

    def group(w, g):
        rows = slice(144 * w, 144 * w + 144)
        return rows, [slice(512 * j + 128 * g, 512 * j + 128 * g + 128) for j in range(3)]

    for w in range(2):
        for g in range(4):
            rows, (lq, lk, lv) = group(w, g)
            scores = dot(qkv[rows, lk], head_stack(qkv[rows, lq]), 1, 1) + bias[...]
            raised = jnp.exp(scores - jnp.max(scores, axis=0, keepdims=True))
            p = raised * (1.0 / jnp.sum(raised, axis=0, keepdims=True))
            probs[4 * w + g] = p
            ctx[rows, lq] = head_merge(dot(p.astype(BF16), qkv[rows, lv], 0, 0)).astype(BF16)

    shared_ctx = share(ctx)
    for copy in halos[1]:
        copy.wait_recv()
    cot[OWN] = dot(maps_w[0], arrived[1]).astype(BF16)
    shared_cot = share(cot)
    loads[3].wait()
    branch = dot(ctx[OWN], wproj[...]).astype(BF16)
    residual = (f32s[X] + branch.astype(F32)).astype(BF16)
    resid32 = residual.astype(F32)
    f32s[X] = resid32
    normed, inv_std = normalize(resid32)
    f32s[N2] = normed
    cols[R2] = inv_std
    n2b[OWN] = normed.astype(BF16)
    shared_n2 = share(n2b)

    loads[4].wait()
    loads[5].wait()
    shared_ff = []

    def forward_tile(t):
        tile = slice(512 * t, 512 * t + 512)
        hidden = dot(n2b[OWN], wfc1[:, tile])
        upper = 0.5 * (1.0 + lax.erf(hidden * inv_root_two))
        act[OWN, tile] = (hidden * upper).astype(BF16)
        slope = upper + hidden * inv_root_tau * jnp.exp(-0.5 * hidden * hidden)
        gh[OWN, tile] = (dot(cot[OWN], wfc2[tile, :], 1, 1) * slope).astype(BF16)
        shared_ff.append((share(act, 512 * t, 512), share(gh, 512 * t, 512)))

    def quarter(t):
        for copy in shared_ff[t]:
            copy.wait_recv()
        for part, lhs, rhs in ((0, lhs_n2, gh), (1, lhs_cot, act)):
            early[part].multiply(lhs, rhs, 512 * t, 512 * t, 512)
            early[part].send_ring(512 * t, 512)

    for t in range(4):
        forward_tile(t)
    shared_n2.wait_recv()
    lhs_n2[...] = dot(orders_ref[0], n2b[...], 1, 1).astype(BF16)
    shared_cot.wait_recv()
    lhs_cot[...] = dot(orders_ref[1], cot[...], 1, 1).astype(BF16)
    quarter(0)
    shared_ctx.wait_recv()
    lhs_ctx[...] = dot(orders_ref[2], ctx[...], 1, 1).astype(BF16)
    quarter(1)
    grad_n2 = dot(gh[OWN], wfc1[...], 1, 1)
    grad_resid = (cot[OWN].astype(F32) + norm_back(grad_n2, f32s[N2], cols[R2])).astype(BF16)
    gr[OWN] = grad_resid
    shared_gr = share(gr)
    quarter(2)
    gctx[...] = dot(gr[OWN], wproj[...], 1, 1).astype(BF16)
    quarter(3)
    block_out = (f32s[X] + dot(act[OWN], wfc2[...])).astype(BF16)
    out_sent = return_home(2, block_out)

    def relay():
        for part in early[:2]:
            part.relay()

    relay()
    shared_gr.wait_recv()
    early[2].multiply(lhs_ctx, gr, 0, 0, 512)
    early[2].send_first(0, 512)
    shared_n1.wait_recv()
    for i in range(2):
        lhs_n1[i] = dot(orders_ref[i], n1b[...], 1, 1).astype(BF16)
    relay()

    pieces = (
        (((0, 0, 256), (1024, 256, 128)), ((512, 0, 256), (1152, 256, 128))),
        (((256, 384, 128), (1280, 512, 128)), ((768, 384, 128),)),
        (((384, 640, 128),), ((896, 512, 128), (1408, 640, 128))),
    )

    def late_piece(h):
        for copy in shared_gm[h]:
            copy.wait_recv()
        for part, moves in zip(late, pieces[h]):
            for src, at, count in moves:
                part.multiply(lhs_n1.at[late.index(part)], gm, src, at, count)
            part.send_first(moves[0][1], sum(count for _, _, count in moves))

    shared_gm = []
    for g in range(4):
        for w in range(2):
            rows, (lq, lk, lv) = group(w, g)
            grad = head_stack(gctx[rows, lq])
            p = probs[4 * w + g]
            grad_p = dot(qkv[rows, lv], grad, 1, 1)
            grad_s = (p * (grad_p - jnp.sum(grad_p * p, axis=0, keepdims=True))).astype(BF16)
            gm[rows, lv] = dot(p.astype(BF16), grad).astype(BF16)
            gm[rows, lq] = (head_merge(dot(grad_s, qkv[rows, lk], 0, 0)) * 32 ** (-0.5)).astype(BF16)
            gm[rows, lk] = dot(grad_s, head_stack(qkv[rows, lq])).astype(BF16)
        if g < 2:
            relay()
        if g == 1:
            shared_gm.append([share(gm, 512 * j, 256) for j in range(3)])
        if g == 2:
            late_piece(0)
        if g >= 2:
            shared_gm.append([share(gm, 512 * j + 128 * g, 128) for j in range(3)])

    late_piece(1)
    grad_n1 = dot(gm[OWN], wqkv[...], 1, 1).astype(BF16)
    late_piece(2)
    for part in early[:2]:
        part.second_step()
    grad_in = gr[OWN].astype(F32) + norm_back(grad_n1.astype(F32), f32s[N1], cols[R1])
    in_sent = return_home(3, grad_in.astype(BF16))
    out_stored = arrive_home(2, out_sent, out_hbm)
    for part in late:
        part.second_step()
    early[2].second_step()
    for part in early[:2]:
        part.third_step()
    gin_stored = arrive_home(3, in_sent, gin_hbm)
    for part in late:
        part.third_step()
    early[2].third_step()
    for part in early:
        part.finish()
    for part in late:
        part.finish()
    out_stored.wait()
    gin_stored.wait()
    copies.drain()


def hand_over(*refs):
    count = len(refs) // 2
    for i in range(count):
        refs[count + i][...] = refs[i][...]


def on_device(tokens, cotangent, w_qkv, w_proj, w_fc1, w_fc2):
    vmem = pl.BlockSpec(memory_space=pltpu.VMEM)
    hbm = pl.BlockSpec(memory_space=pl.ANY)
    both = 2 * NT
    out, gin, wg = pl.pallas_call(
        block_kernel,
        out_shape=(
            jax.ShapeDtypeStruct((NT, D), BF16),
            jax.ShapeDtypeStruct((NT, D), BF16),
            jax.ShapeDtypeStruct((96, 128), F32),
        ),
        in_specs=[hbm] * 6,
        out_specs=(hbm, hbm, vmem),
        scratch_shapes=[
            [part_scratch(i, w) for i, w in enumerate(EARLY)],
            [part_scratch(i, w) for i, w in enumerate(LATE)],
            pltpu.VMEM((3, 256, D), BF16),
            pltpu.VMEM((D, 3 * D), BF16),
            pltpu.VMEM((D, D), BF16),
            pltpu.VMEM((D, 4 * D), BF16),
            pltpu.VMEM((4 * D, D), BF16),
            pltpu.VMEM((4, PACKED, D), BF16),
            pltpu.VMEM((4, PACKED, D), BF16),
            pltpu.VMEM((2, PACKED, NT), BF16),
            pltpu.VMEM((2, NT, PACKED), BF16),
            pltpu.VMEM((both, 4 * D), BF16),
            pltpu.VMEM((both, 4 * D), BF16),
            pltpu.VMEM((both, D), BF16),
            pltpu.VMEM((both, D), BF16),
            pltpu.VMEM((both, D), BF16),
            pltpu.VMEM((both, D), BF16),
            pltpu.VMEM((both, D), BF16),
            pltpu.VMEM((both, 3 * D), BF16),
            pltpu.VMEM((3, 256, both), BF16),
            pltpu.VMEM((256, both), BF16),
            pltpu.VMEM((256, both), BF16),
            pltpu.VMEM((256, both), BF16),
            pltpu.VMEM((NT, 3 * D), BF16),
            pltpu.VMEM((8, 144, 576), F32),
            pltpu.VMEM((144, 576), F32),
            pltpu.VMEM((NT, D), BF16),
            pltpu.VMEM((3, NT, D), F32),
            pltpu.VMEM((2, NT, 1), F32),
            pltpu.VMEM((4, NT, D), BF16),
            pltpu.SemaphoreType.DMA((192,)),
            pltpu.SemaphoreType.DMA((192,)),
            pltpu.SemaphoreType.DMA((8,)),
        ],
        compiler_params=pltpu.CompilerParams(
            collective_id=0, has_side_effects=True, vmem_limit_bytes=60 * 1024 * 1024
        ),
    )(tokens.reshape(NT, D), cotangent.reshape(NT, D), w_qkv, w_proj, w_fc1, w_fc2)
    out, gin, wg = pl.pallas_call(
        hand_over,
        out_shape=tuple(jax.ShapeDtypeStruct(v.shape, v.dtype) for v in (out, gin, wg)),
        in_specs=[vmem] * 3,
        out_specs=(vmem,) * 3,
    )(out, gin, wg)
    return out.reshape(tokens.shape), gin.reshape(tokens.shape), wg


def solution(mesh):
    return jax.shard_map(
        on_device,
        mesh=mesh,
        in_specs=(P(None, "lat", "lon", None), P(None, "lat", "lon", None), P(), P(), P(), P()),
        out_specs=(
            P(None, "lat", "lon", None),
            P(None, "lat", "lon", None),
            P(("lat", "lon"), None),
        ),
        check_vma=False,
    )
```

```python
import jax
import jax.numpy as jnp
from jax import lax
from jax.experimental import pallas as pl
from jax.experimental.pallas import tpu as pltpu
from jax.sharding import PartitionSpec as P

MESH = pl.DeviceIdType.MESH
H = 16
D = 512
NT = 288
F32 = jnp.float32
BF16 = jnp.bfloat16

epsilon = 1e-05
neg_fill = -1e30
inv_root_two = 0.7071067811865476
inv_root_tau = 0.3989422804014327
grad_scale = 73728 ** (-0.5)


class Place:
    def __init__(self):
        lat, lon = lax.axis_index("lat"), lax.axis_index("lon")
        self.lat, self.lon = lat, lon
        self.core = lax.rem(lat, 2)
        self.x = lax.rem(lax.div(lat, 2), 4)
        self.y = lax.div(lat, 8) * 2 + lax.rem(lon, 2)
        self.z = lax.div(lon, 2)

    def shifted(self, axis=None, by=0):
        x, y, z, core = self.x, self.y, self.z, self.core
        if axis == "x":
            x = lax.rem(x + by, 4)
        elif axis == "y":
            y = lax.rem(y + by, 4)
        elif axis == "z":
            z = lax.rem(z + by, 8)
        elif axis == "core":
            core = 1 - core
        return (lax.div(y, 2) * 8 + x * 2 + core, z * 2 + lax.rem(y, 2))

    def neighbour(self, by_lat, by_lon):
        return (lax.rem(self.lat + by_lat, 16), lax.rem(self.lon + by_lon, 16))


SIZES = {"x": 4, "y": 4, "z": 8}
ORDERS = (("x", "y", "z"), ("y", "x", "z"), ("z", "x", "y"))


def row_order(place, order):
    p = lax.broadcasted_iota(jnp.int32, (256, 1), 0)
    r = p & 1
    rest = p >> 1
    off = {}
    for axis in reversed(order):
        bits = 3 if axis == "z" else 2
        off[axis] = rest & (SIZES[axis] - 1)
        rest = rest >> bits
    x = (off["x"] + place.x) & 3
    y = (off["y"] + place.y) & 3
    z = (off["z"] + place.z) & 7
    row = ((((((y >> 1) * 4 + x) * 2 + place.core) * 8 + z) * 2 + (y & 1)) * 2) + r
    columns = lax.broadcasted_iota(jnp.int32, (256, D), 1)
    return jnp.where(columns == row, 1.0, 0.0).astype(BF16)


def dot(a, b, ca=1, cb=0):
    return lax.dot_general(a, b, (((ca,), (cb,)), ((), ())), preferred_element_type=F32)


class Copies:
    def __init__(self, send_sems, recv_sems):
        self.send_sems, self.recv_sems, self.used, self.started = send_sems, recv_sems, 0, []

    def send(self, src, dst, target):
        k = self.used
        self.used += 1
        copy = pltpu.make_async_remote_copy(
            src_ref=src,
            dst_ref=dst,
            send_sem=self.send_sems.at[k],
            recv_sem=self.recv_sems.at[k],
            device_id=target,
            device_id_type=MESH,
        )
        copy.start()
        self.started.append(copy)
        return copy

    def left(self, copy):
        copy.wait_send()
        self.started.remove(copy)

    def drain(self):
        for copy in self.started:
            copy.wait_send()


class Part:
    def __init__(self, place, copies, part, width, scr, emit, out_ref):
        self.place, self.copies, self.scr, self.width = place, copies, scr, width
        self.first, self.second, self.third = ORDERS[part]
        self.n1, self.n2, self.n3 = (SIZES[a] for a in ORDERS[part])
        self.rows1 = 256 // self.n1
        self.rows2 = self.rows1 // self.n2
        self.emit, self.out_ref = emit, out_ref
        self.pending, self.relays, self.spans = [], [], []

    def multiply(self, lhs, rhs, src, at, count):
        value = dot(lhs[...], rhs[:, src : src + count])
        self.scr["own"][:, at : at + count] = value[: self.rows1]
        self.scr["send1"][:, at : at + count] = value[self.rows1 :].astype(BF16)

    def send_ring(self, at, count):
        r, half = self.rows1, count // 2
        lo, hi, kept = pl.ds(at, half), pl.ds(at + half, half), pl.ds(at // 2, half)
        plus, minus = self.place.shifted(self.first, 1), self.place.shifted(self.first, 3)
        near, opposite, far = pl.ds(0, r), pl.ds(r, r), pl.ds(2 * r, r)
        out, into, relay = self.scr["send1"], self.scr["recv1"], self.scr["relay"]
        first = self.copies.send(out.at[opposite, lo], relay.at[near, kept], plus)
        second = self.copies.send(out.at[opposite, hi], relay.at[opposite, kept], minus)
        self.pending.append(self.copies.send(out.at[near, hi], into.at[near, hi], plus))
        self.pending.append(self.copies.send(out.at[far, lo], into.at[far, lo], minus))
        self.relays.append((first, (near, lo, near, kept), plus))
        self.relays.append((second, (far, hi, opposite, kept), minus))
        self.spans.append((at, count, (0, 2)))

    def relay(self):
        out, into, relay = self.scr["send1"], self.scr["recv1"], self.scr["relay"]
        for copy, (rows, span, from_rows, kept), target in self.relays[:2]:
            copy.wait_recv()
            out[rows, span] = (out[rows, span].astype(F32) + relay[from_rows, kept].astype(F32)).astype(BF16)
            self.pending.append(self.copies.send(out.at[rows, span], into.at[rows, span], target))
        self.relays = self.relays[2:]

    def send_first(self, at, count):
        self.spans.append((at, count, range(self.n1 - 1)))
        r = self.rows1
        for j in range(1, self.n1):
            here = (pl.ds((j - 1) * r, r), pl.ds(at, count))
            self.pending.append(
                self.copies.send(
                    self.scr["send1"].at[here], self.scr["recv1"].at[here], self.place.shifted(self.first, j)
                )
            )

    def arrive(self):
        for copy in self.pending:
            copy.wait_recv()
        self.pending = []

    def second_step(self):
        self.arrive()
        scr, r1, r = self.scr, self.rows1, self.rows2
        fine = r % 16 == 0
        for at, count, slots in self.spans:
            span = slice(at, at + count)
            if not fine:
                whole = scr["own"][:, span]
                for i in slots:
                    whole = whole + scr["recv1"][i * r1 : i * r1 + r1, span].astype(F32)
            for j in range(self.n2):
                rows = slice(j * r, j * r + r)
                if fine:
                    total = scr["own"][rows, span]
                    for i in slots:
                        total = total + scr["recv1"][i * r1 + j * r : i * r1 + j * r + r, span].astype(F32)
                else:
                    total = whole[rows]
                if j == 0:
                    scr["own"][rows, span] = total
                else:
                    scr["send2"][(j - 1) * r : j * r, span] = total.astype(scr["send2"].dtype)
        for j in (2, 1, 3):
            here = pl.ds((j - 1) * r, r)
            self.pending.append(
                self.copies.send(scr["send2"].at[here], scr["recv2"].at[here], self.place.shifted(self.second, j))
            )

    def third_step(self):
        self.arrive()
        scr, r = self.scr, self.rows2
        total = scr["own"][0:r]
        for i in range(self.n2 - 1):
            total = total + scr["recv2"][i * r : i * r + r].astype(F32)
        slots = scr["wide3"].shape[0] // (2 * self.n3)
        for c in range(self.width // 128):
            scr["wide3"][pl.ds(c, 2 * self.n3, stride=slots), :] = total[:, c * 128 : (c + 1) * 128]
        each = 2 * slots
        scr["send3"][...] = scr["wide3"][each:].astype(BF16)
        for j in range(1, self.n3):
            here = pl.ds((j - 1) * each, each)
            self.pending.append(
                self.copies.send(scr["send3"].at[here], scr["recv3"].at[here], self.place.shifted(self.third, j))
            )

    def finish(self):
        self.arrive()
        scr = self.scr
        slots = scr["wide3"].shape[0] // (2 * self.n3)
        each = 2 * slots
        total = scr["wide3"][0:each]
        for i in range(self.n3 - 1):
            total = total + scr["recv3"][i * each : (i + 1) * each].astype(F32)
        total = total * grad_scale
        for r in range(2):
            for local, whole, count in self.emit:
                self.out_ref[r * 48 + whole : r * 48 + whole + count, :] = total[
                    r * slots + local : r * slots + local + count, :
                ]


def part_scratch(part, width):
    n1, n2, n3 = (SIZES[a] for a in ORDERS[part])
    r1 = 256 // n1
    r2 = r1 // n2
    slots = -(-(width // 128) // 8) * 8
    mid = BF16 if r2 >= 16 else F32
    return dict(
        own=pltpu.VMEM((r1, width), F32),
        send1=pltpu.VMEM((256 - r1, width), BF16),
        recv1=pltpu.VMEM((256 - r1, width), BF16),
        relay=pltpu.VMEM((2 * r1, width // 2), BF16),
        send2=pltpu.VMEM((r1 - r2, width), mid),
        recv2=pltpu.VMEM((r1 - r2, width), mid),
        wide3=pltpu.VMEM((2 * n3 * slots, 128), F32),
        send3=pltpu.VMEM((2 * (n3 - 1) * slots, 128), BF16),
        recv3=pltpu.VMEM((2 * (n3 - 1) * slots, 128), BF16),
    )


EARLY = (1536, 2048, 1024)
LATE = (896, 640)
EARLY_OUT = (((0, 20, 12),), ((0, 32, 16),), ((0, 16, 4), (4, 12, 4)))
LATE_OUT = (((0, 0, 2), (2, 8, 1), (3, 2, 1), (4, 10, 1), (5, 3, 1), (6, 11, 1)), ((0, 4, 2), (2, 9, 1), (3, 6, 2)))


def greet(place):
    barrier = pltpu.get_barrier_semaphore()
    peers = [place.shifted("core")]
    for axis in ("x", "y", "z"):
        peers += [place.shifted(axis, by) for by in range(1, SIZES[axis])]
    for by in (1, 15):
        peers += [place.neighbour(by, 0), place.neighbour(0, by), place.neighbour(by, by)]
    for peer in peers:
        pl.semaphore_signal(barrier, inc=1, device_id=peer, device_id_type=MESH)
    return lambda: pl.semaphore_wait(barrier, len(peers))


PACKED = 320
SECTIONS = ((112, 112, 1, 0), (224, 48, 0, 1), (272, 48, 1, 1))


def token_of(s):
    big = s < 224
    second = ((s >= 112) & (s < 224)) | (s >= 272)
    u = jnp.where(big, s - jnp.where(s >= 112, 112, 0), s - jnp.where(s >= 272, 272, 224))
    low = jnp.where(second, 0, 3)
    wide = big & (u < 72)
    u2 = jnp.where(big, u - 72, u)
    lev_w = (u >= 36).astype(jnp.int32)
    m_w = u - 36 * lev_w
    row_w = (m_w >= 12).astype(jnp.int32) + (m_w >= 24).astype(jnp.int32)
    col_w = 6 + m_w - 12 * row_w
    lev_n = (u2 >= 18).astype(jnp.int32)
    m_n = u2 - 18 * lev_n
    row_n = (m_n >= 6).astype(jnp.int32) + (m_n >= 12).astype(jnp.int32)
    col_n = jnp.where(big, 18, 0) + m_n - 6 * row_n
    lev = jnp.where(wide, lev_w, lev_n)
    row = jnp.where(wide, row_w, row_n) + low
    col = jnp.where(wide, col_w, col_n)
    empty = u >= jnp.where(big, 108, 36)
    return jnp.where(empty, -1, lev * 144 + row * 24 + col)


def packed_of(w):
    at = jnp.where(w < 72, w, w + 40)
    at = jnp.where(w >= 144, w - 72, at)
    at = jnp.where(w >= 180, w + 44, at)
    at = jnp.where(w >= 216, w - 32, at)
    return jnp.where(w >= 252, w + 20, at)


def iota(shape, dim):
    return lax.broadcasted_iota(jnp.int32, shape, dim)


def ones_at(same):
    return jnp.where(same, 1.0, 0.0).astype(BF16)


def pack_matrix():
    return ones_at(token_of(iota((PACKED, 1), 0)) == iota((PACKED, NT), 1))


def unpack_matrix():
    return ones_at(token_of(iota((1, PACKED), 1)) == iota((NT, PACKED), 0))


def window_matrix():
    return ones_at(packed_of(iota((NT, 1), 0)) == iota((NT, PACKED), 1))


def unwindow_matrix():
    return ones_at(packed_of(iota((1, NT), 1)) == iota((PACKED, NT), 0))


def normalize(values):
    centre = values - jnp.mean(values, axis=-1, keepdims=True)
    inv_std = lax.rsqrt(jnp.mean(centre * centre, axis=-1, keepdims=True) + epsilon)
    return centre * inv_std, inv_std


def norm_back(upstream, normed, inv_std):
    mean_up = jnp.mean(upstream, axis=-1, keepdims=True)
    mean_dot = jnp.mean(upstream * normed, axis=-1, keepdims=True)
    return inv_std * (upstream - mean_up - normed * mean_dot)


def head_stack(value):
    lane = iota((144, 128), 1)
    zero = jnp.zeros_like(value)
    return jnp.concatenate([jnp.where((lane >> 5) == j, value, zero) for j in range(4)], axis=0)


def head_merge(value):
    lane = iota((144, 128), 1) >> 5
    out = value[432:576]
    for j in range(3):
        out = jnp.where(lane == j, value[144 * j : 144 * j + 144], out)
    return out


OWN, SIB = slice(0, NT), slice(NT, 2 * NT)


def block_kernel(
    x_hbm, c_hbm, wqkv_hbm, wproj_hbm, wfc1_hbm, wfc2_hbm,
    out_hbm, gin_hbm, wg_ref,
    early, late, orders_ref, wqkv, wproj, wfc1, wfc2,
    packs, arrived, maps_p, maps_w, act, gh, n1b, n2b, cot, ctx, gr, gm,
    lhs_n1, lhs_n2, lhs_n2c, lhs_cot, lhs_ctx, qkv, probs, bias, gctx, f32s, cols, ends,
    send_sems, recv_sems, local_sems,
):
    place = Place()
    copies = Copies(send_sems, recv_sems)
    met = greet(place)
    loads = [
        pltpu.make_async_copy(src, dst, local_sems.at[i])
        for i, (src, dst) in enumerate(
            (
                (x_hbm, ends.at[0]),
                (c_hbm, ends.at[1]),
                (wqkv_hbm, wqkv),
                (wproj_hbm, wproj),
                (wfc1_hbm, wfc1),
                (wfc2_hbm, wfc2),
            )
        )
    ]
    for load in loads:
        load.start()
    X, N1, N2 = 0, 1, 2
    R1, R2 = 0, 1

    def share(ref, at=0, count=None):
        here = pl.ds(at, ref.shape[1] if count is None else count)
        return copies.send(ref.at[pl.ds(0, NT), here], ref.at[pl.ds(NT, NT), here], place.shifted("core"))

    early = [
        Part(place, copies, i, width, scr, emit, wg_ref) for i, (width, scr, emit) in enumerate(zip(EARLY, early, EARLY_OUT))
    ]
    late = [
        Part(place, copies, i, width, scr, emit, wg_ref) for i, (width, scr, emit) in enumerate(zip(LATE, late, LATE_OUT))
    ]

    maps_p[0] = pack_matrix()
    for i in range(2):
        loads[i].wait()
        packs[i] = dot(maps_p[0], ends[i]).astype(BF16)
    maps_w[0] = window_matrix()
    maps_p[1] = unwindow_matrix()
    maps_w[1] = unpack_matrix()
    for part, order in enumerate(ORDERS):
        orders_ref[part] = row_order(place, order)
    lane = iota((144, 576), 1)
    high = lane < 0
    for j in range(4):
        high = high | ((lane >= 144 * j + 72) & (lane < 144 * j + 144))
    apart = ((iota((144, 576), 0) >= 72) != high) & (place.lat == 15)
    bias[...] = jnp.where(apart, neg_fill, 0.0)
    met()
    halos = []
    for i in range(2):
        if i:
            for copy in halos[0]:
                copies.left(copy)
        halos.append(
            [
                copies.send(
                    packs.at[i, pl.ds(at, count)],
                    arrived.at[i, pl.ds(at, count)],
                    place.neighbour(16 - a if a else 0, 16 - b if b else 0),
                )
                for at, count, a, b in SECTIONS
            ]
        )
        arrived[i, 0:112] = packs[i, 0:112]

    def return_home(slot, value):
        packs[slot] = dot(maps_p[1], value).astype(BF16)
        sent = [
            copies.send(
                packs.at[slot, pl.ds(at, count)],
                arrived.at[slot, pl.ds(at, count)],
                place.neighbour(a, b),
            )
            for at, count, a, b in SECTIONS
        ]
        arrived[slot, 0:112] = packs[slot, 0:112]
        return sent

    def arrive_home(slot, sent, ref):
        for copy in sent:
            copy.wait_recv()
        ends[slot] = dot(maps_w[1], arrived[slot]).astype(BF16)
        store = pltpu.make_async_copy(ends.at[slot], ref, local_sems.at[4 + slot])
        store.start()
        return store

    for copy in halos[0]:
        copy.wait_recv()
    x = dot(maps_w[0], arrived[0])
    f32s[X] = x
    normed, inv_std = normalize(x)
    f32s[N1] = normed
    cols[R1] = inv_std
    n1b[OWN] = normed.astype(BF16)
    shared_n1 = share(n1b)
    loads[2].wait()
    for i in range(3):
        part = dot(n1b[OWN], wqkv[:, 512 * i : 512 * i + 512])
        if i == 0:
            part = part * 32 ** (-0.5)
        qkv[:, 512 * i : 512 * i + 512] = part.astype(BF16)

    def group(w, g):
        rows = slice(144 * w, 144 * w + 144)
        return rows, [slice(512 * j + 128 * g, 512 * j + 128 * g + 128) for j in range(3)]

    for w in range(2):
        for g in range(4):
            rows, (lq, lk, lv) = group(w, g)
            scores = dot(qkv[rows, lk], head_stack(qkv[rows, lq]), 1, 1) + bias[...]
            raised = jnp.exp(scores - jnp.max(scores, axis=0, keepdims=True))
            p = raised * (1.0 / jnp.sum(raised, axis=0, keepdims=True))
            probs[4 * w + g] = p
            ctx[rows, lq] = head_merge(dot(p.astype(BF16), qkv[rows, lv], 0, 0)).astype(BF16)

    shared_ctx = share(ctx)
    for copy in halos[1]:
        copy.wait_recv()
    cot[OWN] = dot(maps_w[0], arrived[1]).astype(BF16)
    shared_cot = share(cot)
    loads[3].wait()
    branch = dot(ctx[OWN], wproj[...]).astype(BF16)
    residual = (f32s[X] + branch.astype(F32)).astype(BF16)
    resid32 = residual.astype(F32)
    f32s[X] = resid32
    normed, inv_std = normalize(resid32)
    f32s[N2] = normed
    cols[R2] = inv_std
    n2b[OWN] = normed.astype(BF16)
    shared_n2 = share(n2b)

    loads[4].wait()
    loads[5].wait()
    shared_ff = []

    def forward_tile(t):
        tile = slice(512 * t, 512 * t + 512)
        hidden = dot(n2b[OWN], wfc1[:, tile])
        upper = 0.5 * (1.0 + lax.erf(hidden * inv_root_two))
        act[OWN, tile] = (hidden * upper).astype(BF16)
        slope = upper + hidden * inv_root_tau * jnp.exp(-0.5 * hidden * hidden)
        gh[OWN, tile] = (dot(cot[OWN], wfc2[tile, :], 1, 1) * slope).astype(BF16)
        shared_ff.append((share(act, 512 * t, 512), share(gh, 512 * t, 512)))

    def quarter(t):
        for copy in shared_ff[t]:
            copy.wait_recv()
        if t == 0:
            early[2].multiply(lhs_n2c, gh, 0, 0, 512)
            early[2].send_first(0, 512)
        else:
            early[0].multiply(lhs_n2, gh, 512 * t, 512 * (t - 1), 512)
            early[0].send_ring(512 * (t - 1), 512)
        early[1].multiply(lhs_cot, act, 512 * t, 512 * t, 512)
        early[1].send_ring(512 * t, 512)

    for t in range(4):
        forward_tile(t)
    shared_n2.wait_recv()
    lhs_n2c[...] = dot(orders_ref[2], n2b[...], 1, 1).astype(BF16)
    shared_cot.wait_recv()
    lhs_cot[...] = dot(orders_ref[1], cot[...], 1, 1).astype(BF16)
    quarter(0)
    lhs_n2[...] = dot(orders_ref[0], n2b[...], 1, 1).astype(BF16)
    quarter(1)
    shared_ctx.wait_recv()
    lhs_ctx[...] = dot(orders_ref[2], ctx[...], 1, 1).astype(BF16)
    grad_n2 = dot(gh[OWN], wfc1[...], 1, 1)
    grad_resid = (cot[OWN].astype(F32) + norm_back(grad_n2, f32s[N2], cols[R2])).astype(BF16)
    gr[OWN] = grad_resid
    shared_gr = share(gr)
    quarter(2)
    gctx[...] = dot(gr[OWN], wproj[...], 1, 1).astype(BF16)
    quarter(3)
    block_out = (f32s[X] + dot(act[OWN], wfc2[...])).astype(BF16)
    out_sent = return_home(2, block_out)

    def relay(t):
        if t:
            early[0].relay()
        early[1].relay()

    relay(0)
    shared_gr.wait_recv()
    early[2].multiply(lhs_ctx, gr, 0, 512, 512)
    early[2].send_first(512, 512)
    shared_n1.wait_recv()
    for i in range(2):
        lhs_n1[i] = dot(orders_ref[i], n1b[...], 1, 1).astype(BF16)
    relay(1)

    pieces = (
        (((0, 0, 256), (1024, 256, 128)), ((512, 0, 256), (1152, 256, 128))),
        (((256, 384, 128), (1280, 512, 128)), ((768, 384, 128),)),
        (((384, 640, 128), (1408, 768, 128)), ((896, 512, 128),)),
    )

    def late_piece(h):
        for copy in shared_gm[h]:
            copy.wait_recv()
        for part, moves in zip(late, pieces[h]):
            for src, at, count in moves:
                part.multiply(lhs_n1.at[late.index(part)], gm, src, at, count)
            part.send_first(moves[0][1], sum(count for _, _, count in moves))

    shared_gm = []
    for g in range(4):
        for w in range(2):
            rows, (lq, lk, lv) = group(w, g)
            grad = head_stack(gctx[rows, lq])
            p = probs[4 * w + g]
            grad_p = dot(qkv[rows, lv], grad, 1, 1)
            grad_s = (p * (grad_p - jnp.sum(grad_p * p, axis=0, keepdims=True))).astype(BF16)
            gm[rows, lv] = dot(p.astype(BF16), grad).astype(BF16)
            gm[rows, lq] = (head_merge(dot(grad_s, qkv[rows, lk], 0, 0)) * 32 ** (-0.5)).astype(BF16)
            gm[rows, lk] = dot(grad_s, head_stack(qkv[rows, lq])).astype(BF16)
        if g < 2:
            relay(2 + g)
        if g == 1:
            shared_gm.append([share(gm, 512 * j, 256) for j in range(3)])
        if g == 2:
            late_piece(0)
        if g >= 2:
            shared_gm.append([share(gm, 512 * j + 128 * g, 128) for j in range(3)])

    late_piece(1)
    grad_n1 = dot(gm[OWN], wqkv[...], 1, 1).astype(BF16)
    late_piece(2)
    for part in early[:2]:
        part.second_step()
    grad_in = gr[OWN].astype(F32) + norm_back(grad_n1.astype(F32), f32s[N1], cols[R1])
    in_sent = return_home(3, grad_in.astype(BF16))
    out_stored = arrive_home(2, out_sent, out_hbm)
    for part in late:
        part.second_step()
    early[2].second_step()
    for part in early[:2]:
        part.third_step()
    gin_stored = arrive_home(3, in_sent, gin_hbm)
    for part in late:
        part.third_step()
    early[2].third_step()
    copies.drain()
    for part in early:
        part.finish()
    for part in late:
        part.finish()
    out_stored.wait()
    gin_stored.wait()


def hand_over(*refs):
    count = len(refs) // 2
    for i in range(count):
        refs[count + i][...] = refs[i][...]


def on_device(tokens, cotangent, w_qkv, w_proj, w_fc1, w_fc2):
    vmem = pl.BlockSpec(memory_space=pltpu.VMEM)
    hbm = pl.BlockSpec(memory_space=pl.ANY)
    both = 2 * NT
    out, gin, wg = pl.pallas_call(
        block_kernel,
        out_shape=(
            jax.ShapeDtypeStruct((NT, D), BF16),
            jax.ShapeDtypeStruct((NT, D), BF16),
            jax.ShapeDtypeStruct((96, 128), F32),
        ),
        in_specs=[hbm] * 6,
        out_specs=(hbm, hbm, vmem),
        scratch_shapes=[
            [part_scratch(i, w) for i, w in enumerate(EARLY)],
            [part_scratch(i, w) for i, w in enumerate(LATE)],
            pltpu.VMEM((3, 256, D), BF16),
            pltpu.VMEM((D, 3 * D), BF16),
            pltpu.VMEM((D, D), BF16),
            pltpu.VMEM((D, 4 * D), BF16),
            pltpu.VMEM((4 * D, D), BF16),
            pltpu.VMEM((4, PACKED, D), BF16),
            pltpu.VMEM((4, PACKED, D), BF16),
            pltpu.VMEM((2, PACKED, NT), BF16),
            pltpu.VMEM((2, NT, PACKED), BF16),
            pltpu.VMEM((both, 4 * D), BF16),
            pltpu.VMEM((both, 4 * D), BF16),
            pltpu.VMEM((both, D), BF16),
            pltpu.VMEM((both, D), BF16),
            pltpu.VMEM((both, D), BF16),
            pltpu.VMEM((both, D), BF16),
            pltpu.VMEM((both, D), BF16),
            pltpu.VMEM((both, 3 * D), BF16),
            pltpu.VMEM((3, 256, both), BF16),
            pltpu.VMEM((256, both), BF16),
            pltpu.VMEM((256, both), BF16),
            pltpu.VMEM((256, both), BF16),
            pltpu.VMEM((256, both), BF16),
            pltpu.VMEM((NT, 3 * D), BF16),
            pltpu.VMEM((8, 144, 576), F32),
            pltpu.VMEM((144, 576), F32),
            pltpu.VMEM((NT, D), BF16),
            pltpu.VMEM((3, NT, D), F32),
            pltpu.VMEM((2, NT, 1), F32),
            pltpu.VMEM((4, NT, D), BF16),
            pltpu.SemaphoreType.DMA((192,)),
            pltpu.SemaphoreType.DMA((192,)),
            pltpu.SemaphoreType.DMA((8,)),
        ],
        compiler_params=pltpu.CompilerParams(
            collective_id=0, has_side_effects=True, vmem_limit_bytes=60 * 1024 * 1024
        ),
    )(tokens.reshape(NT, D), cotangent.reshape(NT, D), w_qkv, w_proj, w_fc1, w_fc2)
    out, gin, wg = pl.pallas_call(
        hand_over,
        out_shape=tuple(jax.ShapeDtypeStruct(v.shape, v.dtype) for v in (out, gin, wg)),
        in_specs=[vmem] * 3,
        out_specs=(vmem,) * 3,
    )(out, gin, wg)
    return out.reshape(tokens.shape), gin.reshape(tokens.shape), wg


def solution(mesh):
    return jax.shard_map(
        on_device,
        mesh=mesh,
        in_specs=(P(None, "lat", "lon", None), P(None, "lat", "lon", None), P(), P(), P(), P()),
        out_specs=(
            P(None, "lat", "lon", None),
            P(None, "lat", "lon", None),
            P(("lat", "lon"), None),
        ),
        check_vma=False,
    )
```

```python
import jax
import jax.numpy as jnp
from jax import lax
from jax.experimental import pallas as pl
from jax.experimental.pallas import tpu as pltpu
from jax.sharding import PartitionSpec as P

MESH = pl.DeviceIdType.MESH
H = 16
D = 512
NT = 288
F32 = jnp.float32
BF16 = jnp.bfloat16

epsilon = 1e-05
neg_fill = -1e30
inv_root_two = 0.7071067811865476
inv_root_tau = 0.3989422804014327
grad_scale = 73728 ** (-0.5)


class Place:
    def __init__(self):
        lat, lon = lax.axis_index("lat"), lax.axis_index("lon")
        self.lat, self.lon = lat, lon
        self.core = lax.rem(lat, 2)
        self.x = lax.rem(lax.div(lat, 2), 4)
        self.y = lax.div(lat, 8) * 2 + lax.rem(lon, 2)
        self.z = lax.div(lon, 2)

    def shifted(self, axis=None, by=0):
        x, y, z, core = self.x, self.y, self.z, self.core
        if axis == "x":
            x = lax.rem(x + by, 4)
        elif axis == "y":
            y = lax.rem(y + by, 4)
        elif axis == "z":
            z = lax.rem(z + by, 8)
        elif axis == "core":
            core = 1 - core
        return (lax.div(y, 2) * 8 + x * 2 + core, z * 2 + lax.rem(y, 2))

    def neighbour(self, by_lat, by_lon):
        return (lax.rem(self.lat + by_lat, 16), lax.rem(self.lon + by_lon, 16))


SIZES = {"x": 4, "y": 4, "z": 8}
ORDERS = (("x", "y", "z"), ("y", "x", "z"), ("z", "x", "y"))


def row_order(place, order):
    p = lax.broadcasted_iota(jnp.int32, (256, 1), 0)
    r = p & 1
    rest = p >> 1
    off = {}
    for axis in reversed(order):
        bits = 3 if axis == "z" else 2
        off[axis] = rest & (SIZES[axis] - 1)
        rest = rest >> bits
    x = (off["x"] + place.x) & 3
    y = (off["y"] + place.y) & 3
    z = (off["z"] + place.z) & 7
    row = ((((((y >> 1) * 4 + x) * 2 + place.core) * 8 + z) * 2 + (y & 1)) * 2) + r
    columns = lax.broadcasted_iota(jnp.int32, (256, D), 1)
    return jnp.where(columns == row, 1.0, 0.0).astype(BF16)


def dot(a, b, ca=1, cb=0):
    return lax.dot_general(a, b, (((ca,), (cb,)), ((), ())), preferred_element_type=F32)


class Copies:
    def __init__(self, send_sems, recv_sems):
        self.send_sems, self.recv_sems, self.used, self.started = send_sems, recv_sems, 0, []

    def send(self, src, dst, target):
        k = self.used
        self.used += 1
        copy = pltpu.make_async_remote_copy(
            src_ref=src,
            dst_ref=dst,
            send_sem=self.send_sems.at[k],
            recv_sem=self.recv_sems.at[k],
            device_id=target,
            device_id_type=MESH,
        )
        copy.start()
        self.started.append(copy)
        return copy

    def left(self, copy):
        copy.wait_send()
        self.started.remove(copy)

    def drain(self):
        for copy in self.started:
            copy.wait_send()


class Part:
    def __init__(self, place, copies, part, width, scr, emit, out_ref):
        self.place, self.copies, self.scr, self.width = place, copies, scr, width
        self.first, self.second, self.third = ORDERS[part]
        self.n1, self.n2, self.n3 = (SIZES[a] for a in ORDERS[part])
        self.rows1 = 256 // self.n1
        self.rows2 = self.rows1 // self.n2
        self.emit, self.out_ref = emit, out_ref
        self.pending, self.relays, self.spans = [], [], []

    def multiply(self, lhs, rhs, src, at, count):
        value = dot(lhs[...], rhs[:, src : src + count])
        self.scr["own"][:, at : at + count] = value[: self.rows1]
        self.scr["send1"][:, at : at + count] = value[self.rows1 :].astype(BF16)

    def send_ring(self, at, count):
        r, half = self.rows1, count // 2
        lo, hi, kept = pl.ds(at, half), pl.ds(at + half, half), pl.ds(at // 2, half)
        plus, minus = self.place.shifted(self.first, 1), self.place.shifted(self.first, 3)
        near, opposite, far = pl.ds(0, r), pl.ds(r, r), pl.ds(2 * r, r)
        out, into, relay = self.scr["send1"], self.scr["recv1"], self.scr["relay"]
        first = self.copies.send(out.at[opposite, lo], relay.at[near, kept], plus)
        second = self.copies.send(out.at[opposite, hi], relay.at[opposite, kept], minus)
        self.pending.append(self.copies.send(out.at[near, hi], into.at[near, hi], plus))
        self.pending.append(self.copies.send(out.at[far, lo], into.at[far, lo], minus))
        self.relays.append((first, (near, lo, near, kept), plus))
        self.relays.append((second, (far, hi, opposite, kept), minus))
        self.spans.append((at, count, (0, 2)))

    def relay(self):
        out, into, relay = self.scr["send1"], self.scr["recv1"], self.scr["relay"]
        for copy, (rows, span, from_rows, kept), target in self.relays[:2]:
            copy.wait_recv()
            out[rows, span] = (out[rows, span].astype(F32) + relay[from_rows, kept].astype(F32)).astype(BF16)
            self.pending.append(self.copies.send(out.at[rows, span], into.at[rows, span], target))
        self.relays = self.relays[2:]

    def send_first(self, at, count):
        self.spans.append((at, count, range(self.n1 - 1)))
        r = self.rows1
        for j in range(1, self.n1):
            here = (pl.ds((j - 1) * r, r), pl.ds(at, count))
            self.pending.append(
                self.copies.send(
                    self.scr["send1"].at[here], self.scr["recv1"].at[here], self.place.shifted(self.first, j)
                )
            )

    def arrive(self):
        for copy in self.pending:
            copy.wait_recv()
        self.pending = []

    def second_step(self):
        self.arrive()
        scr, r1, r = self.scr, self.rows1, self.rows2
        fine = r % 16 == 0
        for at, count, slots in self.spans:
            span = slice(at, at + count)
            if not fine:
                whole = scr["own"][:, span]
                for i in slots:
                    whole = whole + scr["recv1"][i * r1 : i * r1 + r1, span].astype(F32)
            for j in range(self.n2):
                rows = slice(j * r, j * r + r)
                if fine:
                    total = scr["own"][rows, span]
                    for i in slots:
                        total = total + scr["recv1"][i * r1 + j * r : i * r1 + j * r + r, span].astype(F32)
                else:
                    total = whole[rows]
                if j == 0:
                    scr["own"][rows, span] = total
                else:
                    scr["send2"][(j - 1) * r : j * r, span] = total.astype(scr["send2"].dtype)
        for j in (2, 1, 3):
            here = pl.ds((j - 1) * r, r)
            self.pending.append(
                self.copies.send(scr["send2"].at[here], scr["recv2"].at[here], self.place.shifted(self.second, j))
            )

    def third_step(self):
        self.arrive()
        scr, r = self.scr, self.rows2
        total = scr["own"][0:r]
        for i in range(self.n2 - 1):
            total = total + scr["recv2"][i * r : i * r + r].astype(F32)
        slots = scr["wide3"].shape[0] // (2 * self.n3)
        for c in range(self.width // 128):
            scr["wide3"][pl.ds(c, 2 * self.n3, stride=slots), :] = total[:, c * 128 : (c + 1) * 128]
        each = 2 * slots
        scr["send3"][...] = scr["wide3"][each:].astype(BF16)
        for j in range(1, self.n3):
            here = pl.ds((j - 1) * each, each)
            self.pending.append(
                self.copies.send(scr["send3"].at[here], scr["recv3"].at[here], self.place.shifted(self.third, j))
            )

    def finish(self):
        self.arrive()
        scr = self.scr
        slots = scr["wide3"].shape[0] // (2 * self.n3)
        each = 2 * slots
        total = scr["wide3"][0:each]
        for i in range(self.n3 - 1):
            total = total + scr["recv3"][i * each : (i + 1) * each].astype(F32)
        total = total * grad_scale
        for r in range(2):
            for local, whole, count in self.emit:
                self.out_ref[r * 48 + whole : r * 48 + whole + count, :] = total[
                    r * slots + local : r * slots + local + count, :
                ]


def part_scratch(part, width):
    n1, n2, n3 = (SIZES[a] for a in ORDERS[part])
    r1 = 256 // n1
    r2 = r1 // n2
    slots = -(-(width // 128) // 8) * 8
    mid = BF16 if r2 >= 16 else F32
    return dict(
        own=pltpu.VMEM((r1, width), F32),
        send1=pltpu.VMEM((256 - r1, width), BF16),
        recv1=pltpu.VMEM((256 - r1, width), BF16),
        relay=pltpu.VMEM((2 * r1, width // 2), BF16),
        send2=pltpu.VMEM((r1 - r2, width), mid),
        recv2=pltpu.VMEM((r1 - r2, width), mid),
        wide3=pltpu.VMEM((2 * n3 * slots, 128), F32),
        send3=pltpu.VMEM((2 * (n3 - 1) * slots, 128), BF16),
        recv3=pltpu.VMEM((2 * (n3 - 1) * slots, 128), BF16),
    )


EARLY = (2048, 2048, 512)
LATE = (768, 768)
EARLY_OUT = (((0, 16, 16),), ((0, 32, 16),), ((0, 12, 4),))
LATE_OUT = (((0, 0, 2), (2, 8, 1), (3, 2, 1), (4, 10, 1), (5, 3, 1)), ((0, 4, 2), (2, 9, 1), (3, 6, 2), (5, 11, 1)))


def greet(place):
    barrier = pltpu.get_barrier_semaphore()
    peers = [place.shifted("core")]
    for axis in ("x", "y", "z"):
        peers += [place.shifted(axis, by) for by in range(1, SIZES[axis])]
    for by in (1, 15):
        peers += [place.neighbour(by, 0), place.neighbour(0, by), place.neighbour(by, by)]
    for peer in peers:
        pl.semaphore_signal(barrier, inc=1, device_id=peer, device_id_type=MESH)
    return lambda: pl.semaphore_wait(barrier, len(peers))


PACKED = 320
SECTIONS = ((112, 112, 1, 0), (224, 48, 0, 1), (272, 48, 1, 1))


def token_of(s):
    big = s < 224
    second = ((s >= 112) & (s < 224)) | (s >= 272)
    u = jnp.where(big, s - jnp.where(s >= 112, 112, 0), s - jnp.where(s >= 272, 272, 224))
    low = jnp.where(second, 0, 3)
    wide = big & (u < 72)
    u2 = jnp.where(big, u - 72, u)
    lev_w = (u >= 36).astype(jnp.int32)
    m_w = u - 36 * lev_w
    row_w = (m_w >= 12).astype(jnp.int32) + (m_w >= 24).astype(jnp.int32)
    col_w = 6 + m_w - 12 * row_w
    lev_n = (u2 >= 18).astype(jnp.int32)
    m_n = u2 - 18 * lev_n
    row_n = (m_n >= 6).astype(jnp.int32) + (m_n >= 12).astype(jnp.int32)
    col_n = jnp.where(big, 18, 0) + m_n - 6 * row_n
    lev = jnp.where(wide, lev_w, lev_n)
    row = jnp.where(wide, row_w, row_n) + low
    col = jnp.where(wide, col_w, col_n)
    empty = u >= jnp.where(big, 108, 36)
    return jnp.where(empty, -1, lev * 144 + row * 24 + col)


def packed_of(w):
    at = jnp.where(w < 72, w, w + 40)
    at = jnp.where(w >= 144, w - 72, at)
    at = jnp.where(w >= 180, w + 44, at)
    at = jnp.where(w >= 216, w - 32, at)
    return jnp.where(w >= 252, w + 20, at)


def iota(shape, dim):
    return lax.broadcasted_iota(jnp.int32, shape, dim)


def ones_at(same):
    return jnp.where(same, 1.0, 0.0).astype(BF16)


def pack_matrix():
    return ones_at(token_of(iota((PACKED, 1), 0)) == iota((PACKED, NT), 1))


def unpack_matrix():
    return ones_at(token_of(iota((1, PACKED), 1)) == iota((NT, PACKED), 0))


def window_matrix():
    return ones_at(packed_of(iota((NT, 1), 0)) == iota((NT, PACKED), 1))


def unwindow_matrix():
    return ones_at(packed_of(iota((1, NT), 1)) == iota((PACKED, NT), 0))


def normalize(values):
    centre = values - jnp.mean(values, axis=-1, keepdims=True)
    inv_std = lax.rsqrt(jnp.mean(centre * centre, axis=-1, keepdims=True) + epsilon)
    return centre * inv_std, inv_std


def norm_back(upstream, normed, inv_std):
    mean_up = jnp.mean(upstream, axis=-1, keepdims=True)
    mean_dot = jnp.mean(upstream * normed, axis=-1, keepdims=True)
    return inv_std * (upstream - mean_up - normed * mean_dot)


def head_stack(value):
    lane = iota((144, 128), 1)
    zero = jnp.zeros_like(value)
    return jnp.concatenate([jnp.where((lane >> 5) == j, value, zero) for j in range(4)], axis=0)


def head_merge(value):
    lane = iota((144, 128), 1) >> 5
    out = value[432:576]
    for j in range(3):
        out = jnp.where(lane == j, value[144 * j : 144 * j + 144], out)
    return out


OWN, SIB = slice(0, NT), slice(NT, 2 * NT)


def block_kernel(
    x_hbm, c_hbm, wqkv_hbm, wproj_hbm, wfc1_hbm, wfc2_hbm,
    out_hbm, gin_hbm, wg_ref,
    early, late, orders_ref, wqkv, wproj, wfc1, wfc2,
    packs, arrived, maps_p, maps_w, act, gh, n1b, n2b, cot, ctx, gr, gm,
    lhs_n1, lhs_n2, lhs_cot, lhs_ctx, qkv, probs, bias, gctx, f32s, cols, ends,
    send_sems, recv_sems, local_sems,
):
    place = Place()
    copies = Copies(send_sems, recv_sems)
    met = greet(place)
    loads = [
        pltpu.make_async_copy(src, dst, local_sems.at[i])
        for i, (src, dst) in enumerate(
            (
                (x_hbm, ends.at[0]),
                (c_hbm, ends.at[1]),
                (wqkv_hbm, wqkv),
                (wproj_hbm, wproj),
                (wfc1_hbm, wfc1),
                (wfc2_hbm, wfc2),
            )
        )
    ]
    for load in loads:
        load.start()
    X, N1, N2 = 0, 1, 2
    R1, R2 = 0, 1

    def share(ref, at=0, count=None):
        here = pl.ds(at, ref.shape[1] if count is None else count)
        return copies.send(ref.at[pl.ds(0, NT), here], ref.at[pl.ds(NT, NT), here], place.shifted("core"))

    early = [
        Part(place, copies, i, width, scr, emit, wg_ref) for i, (width, scr, emit) in enumerate(zip(EARLY, early, EARLY_OUT))
    ]
    late = [
        Part(place, copies, i, width, scr, emit, wg_ref) for i, (width, scr, emit) in enumerate(zip(LATE, late, LATE_OUT))
    ]

    maps_p[0] = pack_matrix()
    for i in range(2):
        loads[i].wait()
        packs[i] = dot(maps_p[0], ends[i]).astype(BF16)
    maps_w[0] = window_matrix()
    maps_p[1] = unwindow_matrix()
    maps_w[1] = unpack_matrix()
    for part, order in enumerate(ORDERS):
        orders_ref[part] = row_order(place, order)
    lane = iota((144, 576), 1)
    high = lane < 0
    for j in range(4):
        high = high | ((lane >= 144 * j + 72) & (lane < 144 * j + 144))
    apart = ((iota((144, 576), 0) >= 72) != high) & (place.lat == 15)
    bias[...] = jnp.where(apart, neg_fill, 0.0)
    met()
    halos = []
    for i in range(2):
        if i:
            for copy in halos[0]:
                copies.left(copy)
        halos.append(
            [
                copies.send(
                    packs.at[i, pl.ds(at, count)],
                    arrived.at[i, pl.ds(at, count)],
                    place.neighbour(16 - a if a else 0, 16 - b if b else 0),
                )
                for at, count, a, b in SECTIONS
            ]
        )
        arrived[i, 0:112] = packs[i, 0:112]

    def return_home(slot, value):
        packs[slot] = dot(maps_p[1], value).astype(BF16)
        sent = [
            copies.send(
                packs.at[slot, pl.ds(at, count)],
                arrived.at[slot, pl.ds(at, count)],
                place.neighbour(a, b),
            )
            for at, count, a, b in SECTIONS
        ]
        arrived[slot, 0:112] = packs[slot, 0:112]
        return sent

    def arrive_home(slot, sent, ref):
        for copy in sent:
            copy.wait_recv()
        ends[slot] = dot(maps_w[1], arrived[slot]).astype(BF16)
        store = pltpu.make_async_copy(ends.at[slot], ref, local_sems.at[4 + slot])
        store.start()
        return store

    for copy in halos[0]:
        copy.wait_recv()
    x = dot(maps_w[0], arrived[0])
    f32s[X] = x
    normed, inv_std = normalize(x)
    f32s[N1] = normed
    cols[R1] = inv_std
    n1b[OWN] = normed.astype(BF16)
    shared_n1 = share(n1b)
    loads[2].wait()
    for i in range(3):
        part = dot(n1b[OWN], wqkv[:, 512 * i : 512 * i + 512])
        if i == 0:
            part = part * 32 ** (-0.5)
        qkv[:, 512 * i : 512 * i + 512] = part.astype(BF16)

    def group(w, g):
        rows = slice(144 * w, 144 * w + 144)
        return rows, [slice(512 * j + 128 * g, 512 * j + 128 * g + 128) for j in range(3)]

    for w in range(2):
        for g in range(4):
            rows, (lq, lk, lv) = group(w, g)
            scores = dot(qkv[rows, lk], head_stack(qkv[rows, lq]), 1, 1) + bias[...]
            raised = jnp.exp(scores - jnp.max(scores, axis=0, keepdims=True))
            p = raised * (1.0 / jnp.sum(raised, axis=0, keepdims=True))
            probs[4 * w + g] = p
            ctx[rows, lq] = head_merge(dot(p.astype(BF16), qkv[rows, lv], 0, 0)).astype(BF16)

    shared_ctx = share(ctx)
    for copy in halos[1]:
        copy.wait_recv()
    cot[OWN] = dot(maps_w[0], arrived[1]).astype(BF16)
    shared_cot = share(cot)
    loads[3].wait()
    branch = dot(ctx[OWN], wproj[...]).astype(BF16)
    residual = (f32s[X] + branch.astype(F32)).astype(BF16)
    resid32 = residual.astype(F32)
    f32s[X] = resid32
    normed, inv_std = normalize(resid32)
    f32s[N2] = normed
    cols[R2] = inv_std
    n2b[OWN] = normed.astype(BF16)
    shared_n2 = share(n2b)

    loads[4].wait()
    loads[5].wait()
    shared_ff = []

    def forward_tile(t):
        tile = slice(512 * t, 512 * t + 512)
        hidden = dot(n2b[OWN], wfc1[:, tile])
        upper = 0.5 * (1.0 + lax.erf(hidden * inv_root_two))
        act[OWN, tile] = (hidden * upper).astype(BF16)
        slope = upper + hidden * inv_root_tau * jnp.exp(-0.5 * hidden * hidden)
        gh[OWN, tile] = (dot(cot[OWN], wfc2[tile, :], 1, 1) * slope).astype(BF16)
        shared_ff.append((share(act, 512 * t, 512), share(gh, 512 * t, 512)))

    def quarter(t):
        for copy in shared_ff[t]:
            copy.wait_recv()
        for part, lhs, rhs in ((0, lhs_n2, gh), (1, lhs_cot, act)):
            early[part].multiply(lhs, rhs, 512 * t, 512 * t, 512)
            early[part].send_ring(512 * t, 512)

    for t in range(4):
        forward_tile(t)
    shared_n2.wait_recv()
    lhs_n2[...] = dot(orders_ref[0], n2b[...], 1, 1).astype(BF16)
    shared_cot.wait_recv()
    lhs_cot[...] = dot(orders_ref[1], cot[...], 1, 1).astype(BF16)
    quarter(0)
    shared_ctx.wait_recv()
    lhs_ctx[...] = dot(orders_ref[2], ctx[...], 1, 1).astype(BF16)
    quarter(1)
    grad_n2 = dot(gh[OWN], wfc1[...], 1, 1)
    grad_resid = (cot[OWN].astype(F32) + norm_back(grad_n2, f32s[N2], cols[R2])).astype(BF16)
    gr[OWN] = grad_resid
    shared_gr = share(gr)
    quarter(2)
    gctx[...] = dot(gr[OWN], wproj[...], 1, 1).astype(BF16)
    quarter(3)
    block_out = (f32s[X] + dot(act[OWN], wfc2[...])).astype(BF16)
    out_sent = return_home(2, block_out)

    def relay():
        for part in early[:2]:
            part.relay()

    relay()
    shared_gr.wait_recv()
    early[2].multiply(lhs_ctx, gr, 0, 0, 512)
    early[2].send_first(0, 512)
    shared_n1.wait_recv()
    for i in range(2):
        lhs_n1[i] = dot(orders_ref[i], n1b[...], 1, 1).astype(BF16)
    relay()

    pieces = (
        (((0, 0, 256), (1024, 256, 128)), ((512, 0, 256), (1152, 256, 128))),
        (((256, 384, 128), (1280, 512, 128)), ((768, 384, 128),)),
        (((384, 640, 128),), ((896, 512, 128), (1408, 640, 128))),
    )

    def late_piece(h):
        for copy in shared_gm[h]:
            copy.wait_recv()
        for part, moves in zip(late, pieces[h]):
            for src, at, count in moves:
                part.multiply(lhs_n1.at[late.index(part)], gm, src, at, count)
            part.send_first(moves[0][1], sum(count for _, _, count in moves))

    shared_gm = []
    for g in range(4):
        for w in range(2):
            rows, (lq, lk, lv) = group(w, g)
            grad = head_stack(gctx[rows, lq])
            p = probs[4 * w + g]
            grad_p = dot(qkv[rows, lv], grad, 1, 1)
            grad_s = (p * (grad_p - jnp.sum(grad_p * p, axis=0, keepdims=True))).astype(BF16)
            gm[rows, lv] = dot(p.astype(BF16), grad).astype(BF16)
            gm[rows, lq] = (head_merge(dot(grad_s, qkv[rows, lk], 0, 0)) * 32 ** (-0.5)).astype(BF16)
            gm[rows, lk] = dot(grad_s, head_stack(qkv[rows, lq])).astype(BF16)
        if g < 2:
            relay()
        if g == 1:
            shared_gm.append([share(gm, 512 * j, 256) for j in range(3)])
        if g == 2:
            late_piece(0)
        if g >= 2:
            shared_gm.append([share(gm, 512 * j + 128 * g, 128) for j in range(3)])

    late_piece(1)
    grad_n1 = dot(gm[OWN], wqkv[...], 1, 1).astype(BF16)
    late_piece(2)
    for part in early[:2]:
        part.second_step()
    grad_in = gr[OWN].astype(F32) + norm_back(grad_n1.astype(F32), f32s[N1], cols[R1])
    out_stored = arrive_home(2, out_sent, out_hbm)
    for part in late:
        part.second_step()
    in_sent = return_home(3, grad_in.astype(BF16))
    early[2].second_step()
    for part in early[:2]:
        part.third_step()
    for part in late:
        part.third_step()
    early[2].third_step()
    gin_stored = arrive_home(3, in_sent, gin_hbm)
    copies.drain()
    for part in early:
        part.finish()
    for part in late:
        part.finish()
    out_stored.wait()
    gin_stored.wait()


def hand_over(*refs):
    count = len(refs) // 2
    for i in range(count):
        refs[count + i][...] = refs[i][...]


def on_device(tokens, cotangent, w_qkv, w_proj, w_fc1, w_fc2):
    vmem = pl.BlockSpec(memory_space=pltpu.VMEM)
    hbm = pl.BlockSpec(memory_space=pl.ANY)
    both = 2 * NT
    out, gin, wg = pl.pallas_call(
        block_kernel,
        out_shape=(
            jax.ShapeDtypeStruct((NT, D), BF16),
            jax.ShapeDtypeStruct((NT, D), BF16),
            jax.ShapeDtypeStruct((96, 128), F32),
        ),
        in_specs=[hbm] * 6,
        out_specs=(hbm, hbm, vmem),
        scratch_shapes=[
            [part_scratch(i, w) for i, w in enumerate(EARLY)],
            [part_scratch(i, w) for i, w in enumerate(LATE)],
            pltpu.VMEM((3, 256, D), BF16),
            pltpu.VMEM((D, 3 * D), BF16),
            pltpu.VMEM((D, D), BF16),
            pltpu.VMEM((D, 4 * D), BF16),
            pltpu.VMEM((4 * D, D), BF16),
            pltpu.VMEM((4, PACKED, D), BF16),
            pltpu.VMEM((4, PACKED, D), BF16),
            pltpu.VMEM((2, PACKED, NT), BF16),
            pltpu.VMEM((2, NT, PACKED), BF16),
            pltpu.VMEM((both, 4 * D), BF16),
            pltpu.VMEM((both, 4 * D), BF16),
            pltpu.VMEM((both, D), BF16),
            pltpu.VMEM((both, D), BF16),
            pltpu.VMEM((both, D), BF16),
            pltpu.VMEM((both, D), BF16),
            pltpu.VMEM((both, D), BF16),
            pltpu.VMEM((both, 3 * D), BF16),
            pltpu.VMEM((3, 256, both), BF16),
            pltpu.VMEM((256, both), BF16),
            pltpu.VMEM((256, both), BF16),
            pltpu.VMEM((256, both), BF16),
            pltpu.VMEM((NT, 3 * D), BF16),
            pltpu.VMEM((8, 144, 576), F32),
            pltpu.VMEM((144, 576), F32),
            pltpu.VMEM((NT, D), BF16),
            pltpu.VMEM((3, NT, D), F32),
            pltpu.VMEM((2, NT, 1), F32),
            pltpu.VMEM((4, NT, D), BF16),
            pltpu.SemaphoreType.DMA((192,)),
            pltpu.SemaphoreType.DMA((192,)),
            pltpu.SemaphoreType.DMA((8,)),
        ],
        compiler_params=pltpu.CompilerParams(
            collective_id=0, has_side_effects=True, vmem_limit_bytes=60 * 1024 * 1024
        ),
    )(tokens.reshape(NT, D), cotangent.reshape(NT, D), w_qkv, w_proj, w_fc1, w_fc2)
    out, gin, wg = pl.pallas_call(
        hand_over,
        out_shape=tuple(jax.ShapeDtypeStruct(v.shape, v.dtype) for v in (out, gin, wg)),
        in_specs=[vmem] * 3,
        out_specs=(vmem,) * 3,
    )(out, gin, wg)
    return out.reshape(tokens.shape), gin.reshape(tokens.shape), wg


def solution(mesh):
    return jax.shard_map(
        on_device,
        mesh=mesh,
        in_specs=(P(None, "lat", "lon", None), P(None, "lat", "lon", None), P(), P(), P(), P()),
        out_specs=(
            P(None, "lat", "lon", None),
            P(None, "lat", "lon", None),
            P(("lat", "lon"), None),
        ),
        check_vma=False,
    )
```

```python
import jax
import jax.numpy as jnp
from jax import lax
from jax.experimental import pallas as pl
from jax.experimental.pallas import tpu as pltpu
from jax.sharding import PartitionSpec as P

MESH = pl.DeviceIdType.MESH
H = 16
D = 512
NT = 288
F32 = jnp.float32
BF16 = jnp.bfloat16

epsilon = 1e-05
neg_fill = -1e30
inv_root_two = 0.7071067811865476
inv_root_tau = 0.3989422804014327
grad_scale = 73728 ** (-0.5)


class Place:
    def __init__(self):
        lat, lon = lax.axis_index("lat"), lax.axis_index("lon")
        self.lat, self.lon = lat, lon
        self.core = lax.rem(lat, 2)
        self.x = lax.rem(lax.div(lat, 2), 4)
        self.y = lax.div(lat, 8) * 2 + lax.rem(lon, 2)
        self.z = lax.div(lon, 2)

    def shifted(self, axis=None, by=0):
        x, y, z, core = self.x, self.y, self.z, self.core
        if axis == "x":
            x = lax.rem(x + by, 4)
        elif axis == "y":
            y = lax.rem(y + by, 4)
        elif axis == "z":
            z = lax.rem(z + by, 8)
        elif axis == "core":
            core = 1 - core
        return (lax.div(y, 2) * 8 + x * 2 + core, z * 2 + lax.rem(y, 2))

    def neighbour(self, by_lat, by_lon):
        return (lax.rem(self.lat + by_lat, 16), lax.rem(self.lon + by_lon, 16))


SIZES = {"x": 4, "y": 4, "z": 8}
ORDERS = (("x", "y", "z"), ("y", "x", "z"), ("z", "x", "y"))


def row_order(place, order):
    p = lax.broadcasted_iota(jnp.int32, (256, 1), 0)
    r = p & 1
    rest = p >> 1
    off = {}
    for axis in reversed(order):
        bits = 3 if axis == "z" else 2
        off[axis] = rest & (SIZES[axis] - 1)
        rest = rest >> bits
    x = (off["x"] + place.x) & 3
    y = (off["y"] + place.y) & 3
    z = (off["z"] + place.z) & 7
    row = ((((((y >> 1) * 4 + x) * 2 + place.core) * 8 + z) * 2 + (y & 1)) * 2) + r
    columns = lax.broadcasted_iota(jnp.int32, (256, D), 1)
    return jnp.where(columns == row, 1.0, 0.0).astype(BF16)


def dot(a, b, ca=1, cb=0):
    return lax.dot_general(a, b, (((ca,), (cb,)), ((), ())), preferred_element_type=F32)


class Copies:
    def __init__(self, send_sems, recv_sems):
        self.send_sems, self.recv_sems, self.used, self.started = send_sems, recv_sems, 0, []

    def send(self, src, dst, target):
        k = self.used
        self.used += 1
        copy = pltpu.make_async_remote_copy(
            src_ref=src,
            dst_ref=dst,
            send_sem=self.send_sems.at[k],
            recv_sem=self.recv_sems.at[k],
            device_id=target,
            device_id_type=MESH,
        )
        copy.start()
        self.started.append(copy)
        return copy

    def left(self, copy):
        copy.wait_send()
        self.started.remove(copy)

    def drain(self):
        for copy in self.started:
            copy.wait_send()


class Part:
    def __init__(self, place, copies, part, width, scr, emit, out_ref):
        self.place, self.copies, self.scr, self.width = place, copies, scr, width
        self.first, self.second, self.third = ORDERS[part]
        self.n1, self.n2, self.n3 = (SIZES[a] for a in ORDERS[part])
        self.rows1 = 256 // self.n1
        self.rows2 = self.rows1 // self.n2
        self.emit, self.out_ref = emit, out_ref
        self.pending, self.relays, self.spans = [], [], []

    def multiply(self, lhs, rhs, src, at, count):
        value = dot(lhs[...], rhs[:, src : src + count])
        self.scr["own"][:, at : at + count] = value[: self.rows1]
        self.scr["send1"][:, at : at + count] = value[self.rows1 :].astype(BF16)

    def send_ring(self, at, count):
        r, half = self.rows1, count // 2
        lo, hi, kept = pl.ds(at, half), pl.ds(at + half, half), pl.ds(at // 2, half)
        plus, minus = self.place.shifted(self.first, 1), self.place.shifted(self.first, 3)
        near, opposite, far = pl.ds(0, r), pl.ds(r, r), pl.ds(2 * r, r)
        out, into, relay = self.scr["send1"], self.scr["recv1"], self.scr["relay"]
        first = self.copies.send(out.at[opposite, lo], relay.at[near, kept], plus)
        second = self.copies.send(out.at[opposite, hi], relay.at[opposite, kept], minus)
        self.pending.append(self.copies.send(out.at[near, hi], into.at[near, hi], plus))
        self.pending.append(self.copies.send(out.at[far, lo], into.at[far, lo], minus))
        self.relays.append((first, (near, lo, near, kept), plus))
        self.relays.append((second, (far, hi, opposite, kept), minus))
        self.spans.append((at, count, (0, 2)))

    def relay(self):
        out, into, relay = self.scr["send1"], self.scr["recv1"], self.scr["relay"]
        for copy, (rows, span, from_rows, kept), target in self.relays[:2]:
            copy.wait_recv()
            out[rows, span] = (out[rows, span].astype(F32) + relay[from_rows, kept].astype(F32)).astype(BF16)
            self.pending.append(self.copies.send(out.at[rows, span], into.at[rows, span], target))
        self.relays = self.relays[2:]

    def send_first(self, at, count):
        self.spans.append((at, count, range(self.n1 - 1)))
        r = self.rows1
        for j in range(1, self.n1):
            here = (pl.ds((j - 1) * r, r), pl.ds(at, count))
            self.pending.append(
                self.copies.send(
                    self.scr["send1"].at[here], self.scr["recv1"].at[here], self.place.shifted(self.first, j)
                )
            )

    def arrive(self):
        for copy in self.pending:
            copy.wait_recv()
        self.pending = []

    def second_step(self):
        self.arrive()
        scr, r1, r = self.scr, self.rows1, self.rows2
        fine = r % 16 == 0
        for at, count, slots in self.spans:
            span = slice(at, at + count)
            if not fine:
                whole = scr["own"][:, span]
                for i in slots:
                    whole = whole + scr["recv1"][i * r1 : i * r1 + r1, span].astype(F32)
            for j in range(self.n2):
                rows = slice(j * r, j * r + r)
                if fine:
                    total = scr["own"][rows, span]
                    for i in slots:
                        total = total + scr["recv1"][i * r1 + j * r : i * r1 + j * r + r, span].astype(F32)
                else:
                    total = whole[rows]
                if j == 0:
                    scr["own"][rows, span] = total
                else:
                    scr["send2"][(j - 1) * r : j * r, span] = total.astype(scr["send2"].dtype)
        for j in (2, 1, 3):
            here = pl.ds((j - 1) * r, r)
            self.pending.append(
                self.copies.send(scr["send2"].at[here], scr["recv2"].at[here], self.place.shifted(self.second, j))
            )

    def third_step(self):
        self.arrive()
        scr, r = self.scr, self.rows2
        total = scr["own"][0:r]
        for i in range(self.n2 - 1):
            total = total + scr["recv2"][i * r : i * r + r].astype(F32)
        slots = scr["wide3"].shape[0] // (2 * self.n3)
        for c in range(self.width // 128):
            scr["wide3"][pl.ds(c, 2 * self.n3, stride=slots), :] = total[:, c * 128 : (c + 1) * 128]
        each = 2 * slots
        scr["send3"][...] = scr["wide3"][each:].astype(BF16)
        for j in range(1, self.n3):
            here = pl.ds((j - 1) * each, each)
            self.pending.append(
                self.copies.send(scr["send3"].at[here], scr["recv3"].at[here], self.place.shifted(self.third, j))
            )

    def finish(self):
        self.arrive()
        scr = self.scr
        slots = scr["wide3"].shape[0] // (2 * self.n3)
        each = 2 * slots
        total = scr["wide3"][0:each]
        for i in range(self.n3 - 1):
            total = total + scr["recv3"][i * each : (i + 1) * each].astype(F32)
        total = total * grad_scale
        for r in range(2):
            for local, whole, count in self.emit:
                self.out_ref[r * 48 + whole : r * 48 + whole + count, :] = total[
                    r * slots + local : r * slots + local + count, :
                ]


def part_scratch(part, width):
    n1, n2, n3 = (SIZES[a] for a in ORDERS[part])
    r1 = 256 // n1
    r2 = r1 // n2
    slots = -(-(width // 128) // 8) * 8
    mid = BF16 if r2 >= 16 else F32
    return dict(
        own=pltpu.VMEM((r1, width), F32),
        send1=pltpu.VMEM((256 - r1, width), BF16),
        recv1=pltpu.VMEM((256 - r1, width), BF16),
        relay=pltpu.VMEM((2 * r1, width // 2), BF16),
        send2=pltpu.VMEM((r1 - r2, width), mid),
        recv2=pltpu.VMEM((r1 - r2, width), mid),
        wide3=pltpu.VMEM((2 * n3 * slots, 128), F32),
        send3=pltpu.VMEM((2 * (n3 - 1) * slots, 128), BF16),
        recv3=pltpu.VMEM((2 * (n3 - 1) * slots, 128), BF16),
    )


EARLY = (2048, 2048, 512)
LATE = (768, 768)
EARLY_OUT = (((0, 16, 16),), ((0, 32, 16),), ((0, 12, 4),))
LATE_OUT = (((0, 0, 2), (2, 8, 1), (3, 2, 1), (4, 10, 1), (5, 3, 1)), ((0, 4, 2), (2, 9, 1), (3, 6, 2), (5, 11, 1)))


def greet(place):
    barrier = pltpu.get_barrier_semaphore()
    peers = [place.shifted("core")]
    for axis in ("x", "y", "z"):
        peers += [place.shifted(axis, by) for by in range(1, SIZES[axis])]
    for by in (1, 15):
        peers += [place.neighbour(by, 0), place.neighbour(0, by), place.neighbour(by, by)]
    for peer in peers:
        pl.semaphore_signal(barrier, inc=1, device_id=peer, device_id_type=MESH)
    return lambda: pl.semaphore_wait(barrier, len(peers))


PACKED = 320
SECTIONS = ((112, 112, 1, 0), (224, 48, 0, 1), (272, 48, 1, 1))


def token_of(s):
    big = s < 224
    second = ((s >= 112) & (s < 224)) | (s >= 272)
    u = jnp.where(big, s - jnp.where(s >= 112, 112, 0), s - jnp.where(s >= 272, 272, 224))
    low = jnp.where(second, 0, 3)
    wide = big & (u < 72)
    u2 = jnp.where(big, u - 72, u)
    lev_w = (u >= 36).astype(jnp.int32)
    m_w = u - 36 * lev_w
    row_w = (m_w >= 12).astype(jnp.int32) + (m_w >= 24).astype(jnp.int32)
    col_w = 6 + m_w - 12 * row_w
    lev_n = (u2 >= 18).astype(jnp.int32)
    m_n = u2 - 18 * lev_n
    row_n = (m_n >= 6).astype(jnp.int32) + (m_n >= 12).astype(jnp.int32)
    col_n = jnp.where(big, 18, 0) + m_n - 6 * row_n
    lev = jnp.where(wide, lev_w, lev_n)
    row = jnp.where(wide, row_w, row_n) + low
    col = jnp.where(wide, col_w, col_n)
    empty = u >= jnp.where(big, 108, 36)
    return jnp.where(empty, -1, lev * 144 + row * 24 + col)


def packed_of(w):
    at = jnp.where(w < 72, w, w + 40)
    at = jnp.where(w >= 144, w - 72, at)
    at = jnp.where(w >= 180, w + 44, at)
    at = jnp.where(w >= 216, w - 32, at)
    return jnp.where(w >= 252, w + 20, at)


def iota(shape, dim):
    return lax.broadcasted_iota(jnp.int32, shape, dim)


def ones_at(same):
    return jnp.where(same, 1.0, 0.0).astype(BF16)


def pack_matrix():
    return ones_at(token_of(iota((PACKED, 1), 0)) == iota((PACKED, NT), 1))


def unpack_matrix():
    return ones_at(token_of(iota((1, PACKED), 1)) == iota((NT, PACKED), 0))


def window_matrix():
    return ones_at(packed_of(iota((NT, 1), 0)) == iota((NT, PACKED), 1))


def unwindow_matrix():
    return ones_at(packed_of(iota((1, NT), 1)) == iota((PACKED, NT), 0))


def normalize(values):
    centre = values - jnp.mean(values, axis=-1, keepdims=True)
    inv_std = lax.rsqrt(jnp.mean(centre * centre, axis=-1, keepdims=True) + epsilon)
    return centre * inv_std, inv_std


def norm_back(upstream, normed, inv_std):
    mean_up = jnp.mean(upstream, axis=-1, keepdims=True)
    mean_dot = jnp.mean(upstream * normed, axis=-1, keepdims=True)
    return inv_std * (upstream - mean_up - normed * mean_dot)


def head_stack(value):
    lane = iota((144, 128), 1)
    zero = jnp.zeros_like(value)
    return jnp.concatenate([jnp.where((lane >> 5) == j, value, zero) for j in range(4)], axis=0)


def head_merge(value):
    lane = iota((144, 128), 1) >> 5
    out = value[432:576]
    for j in range(3):
        out = jnp.where(lane == j, value[144 * j : 144 * j + 144], out)
    return out


OWN, SIB = slice(0, NT), slice(NT, 2 * NT)


def block_kernel(
    x_hbm, c_hbm, wqkv_hbm, wproj_hbm, wfc1_hbm, wfc2_hbm,
    out_hbm, gin_hbm, wg_ref,
    early, late, orders_ref, wqkv, wproj, wfc1, wfc2,
    packs, arrived, maps_p, maps_w, act, gh, n1b, n2b, cot, ctx, gr, gm,
    lhs_n1, lhs_n2, lhs_cot, lhs_ctx, qkv, probs, bias, gctx, f32s, cols, ends,
    send_sems, recv_sems, local_sems,
):
    place = Place()
    copies = Copies(send_sems, recv_sems)
    met = greet(place)
    loads = [
        pltpu.make_async_copy(src, dst, local_sems.at[i])
        for i, (src, dst) in enumerate(
            (
                (x_hbm, ends.at[0]),
                (c_hbm, ends.at[1]),
                (wqkv_hbm, wqkv),
                (wproj_hbm, wproj),
                (wfc1_hbm, wfc1),
                (wfc2_hbm, wfc2),
            )
        )
    ]
    for load in loads:
        load.start()
    X, N1, N2 = 0, 1, 2
    R1, R2 = 0, 1

    def share(ref, at=0, count=None):
        here = pl.ds(at, ref.shape[1] if count is None else count)
        return copies.send(ref.at[pl.ds(0, NT), here], ref.at[pl.ds(NT, NT), here], place.shifted("core"))

    early = [
        Part(place, copies, i, width, scr, emit, wg_ref) for i, (width, scr, emit) in enumerate(zip(EARLY, early, EARLY_OUT))
    ]
    late = [
        Part(place, copies, i, width, scr, emit, wg_ref) for i, (width, scr, emit) in enumerate(zip(LATE, late, LATE_OUT))
    ]

    maps_p[0] = pack_matrix()
    for i in range(2):
        loads[i].wait()
        packs[i] = dot(maps_p[0], ends[i]).astype(BF16)
    maps_w[0] = window_matrix()
    maps_p[1] = unwindow_matrix()
    maps_w[1] = unpack_matrix()
    for part, order in enumerate(ORDERS):
        orders_ref[part] = row_order(place, order)
    lane = iota((144, 576), 1)
    high = lane < 0
    for j in range(4):
        high = high | ((lane >= 144 * j + 72) & (lane < 144 * j + 144))
    apart = ((iota((144, 576), 0) >= 72) != high) & (place.lat == 15)
    bias[...] = jnp.where(apart, neg_fill, 0.0)
    met()
    halos = []
    for i in range(2):
        if i:
            for copy in halos[0]:
                copies.left(copy)
        halos.append(
            [
                copies.send(
                    packs.at[i, pl.ds(at, count)],
                    arrived.at[i, pl.ds(at, count)],
                    place.neighbour(16 - a if a else 0, 16 - b if b else 0),
                )
                for at, count, a, b in SECTIONS
            ]
        )
        arrived[i, 0:112] = packs[i, 0:112]

    def return_home(slot, value):
        packs[slot] = dot(maps_p[1], value).astype(BF16)
        sent = [
            copies.send(
                packs.at[slot, pl.ds(at, count)],
                arrived.at[slot, pl.ds(at, count)],
                place.neighbour(a, b),
            )
            for at, count, a, b in SECTIONS
        ]
        arrived[slot, 0:112] = packs[slot, 0:112]
        return sent

    def arrive_home(slot, sent, ref):
        for copy in sent:
            copy.wait_recv()
        ends[slot] = dot(maps_w[1], arrived[slot]).astype(BF16)
        store = pltpu.make_async_copy(ends.at[slot], ref, local_sems.at[4 + slot])
        store.start()
        return store

    for copy in halos[0]:
        copy.wait_recv()
    x = dot(maps_w[0], arrived[0])
    f32s[X] = x
    normed, inv_std = normalize(x)
    f32s[N1] = normed
    cols[R1] = inv_std
    n1b[OWN] = normed.astype(BF16)
    shared_n1 = share(n1b)
    loads[2].wait()
    for i in range(3):
        part = dot(n1b[OWN], wqkv[:, 512 * i : 512 * i + 512])
        if i == 0:
            part = part * 32 ** (-0.5)
        qkv[:, 512 * i : 512 * i + 512] = part.astype(BF16)

    def group(w, g):
        rows = slice(144 * w, 144 * w + 144)
        return rows, [slice(512 * j + 128 * g, 512 * j + 128 * g + 128) for j in range(3)]

    for w in range(2):
        for g in range(4):
            rows, (lq, lk, lv) = group(w, g)
            scores = dot(qkv[rows, lk], head_stack(qkv[rows, lq]), 1, 1) + bias[...]
            raised = jnp.exp(scores - jnp.max(scores, axis=0, keepdims=True))
            p = raised * (1.0 / jnp.sum(raised, axis=0, keepdims=True))
            probs[4 * w + g] = p
            ctx[rows, lq] = head_merge(dot(p.astype(BF16), qkv[rows, lv], 0, 0)).astype(BF16)

    shared_ctx = share(ctx)
    for copy in halos[1]:
        copy.wait_recv()
    cot[OWN] = dot(maps_w[0], arrived[1]).astype(BF16)
    shared_cot = share(cot)
    loads[3].wait()
    branch = dot(ctx[OWN], wproj[...]).astype(BF16)
    residual = (f32s[X] + branch.astype(F32)).astype(BF16)
    resid32 = residual.astype(F32)
    f32s[X] = resid32
    normed, inv_std = normalize(resid32)
    f32s[N2] = normed
    cols[R2] = inv_std
    n2b[OWN] = normed.astype(BF16)
    shared_n2 = share(n2b)

    loads[4].wait()
    loads[5].wait()
    shared_ff = []

    def forward_tile(t):
        tile = slice(512 * t, 512 * t + 512)
        hidden = dot(n2b[OWN], wfc1[:, tile])
        upper = 0.5 * (1.0 + lax.erf(hidden * inv_root_two))
        act[OWN, tile] = (hidden * upper).astype(BF16)
        slope = upper + hidden * inv_root_tau * jnp.exp(-0.5 * hidden * hidden)
        gh[OWN, tile] = (dot(cot[OWN], wfc2[tile, :], 1, 1) * slope).astype(BF16)
        shared_ff.append((share(act, 512 * t, 512), share(gh, 512 * t, 512)))

    def quarter(t):
        for copy in shared_ff[t]:
            copy.wait_recv()
        for part, lhs, rhs in ((0, lhs_n2, gh), (1, lhs_cot, act)):
            early[part].multiply(lhs, rhs, 512 * t, 512 * t, 512)
            early[part].send_ring(512 * t, 512)

    for t in range(4):
        forward_tile(t)
    shared_n2.wait_recv()
    lhs_n2[...] = dot(orders_ref[0], n2b[...], 1, 1).astype(BF16)
    shared_cot.wait_recv()
    lhs_cot[...] = dot(orders_ref[1], cot[...], 1, 1).astype(BF16)
    quarter(0)
    shared_ctx.wait_recv()
    lhs_ctx[...] = dot(orders_ref[2], ctx[...], 1, 1).astype(BF16)
    quarter(1)
    grad_n2 = dot(gh[OWN], wfc1[...], 1, 1)
    grad_resid = (cot[OWN].astype(F32) + norm_back(grad_n2, f32s[N2], cols[R2])).astype(BF16)
    gr[OWN] = grad_resid
    shared_gr = share(gr)
    quarter(2)
    gctx[...] = dot(gr[OWN], wproj[...], 1, 1).astype(BF16)
    quarter(3)
    block_out = (f32s[X] + dot(act[OWN], wfc2[...])).astype(BF16)
    out_sent = return_home(2, block_out)

    def relay():
        for part in early[:2]:
            part.relay()

    relay()
    shared_gr.wait_recv()
    early[2].multiply(lhs_ctx, gr, 0, 0, 512)
    early[2].send_first(0, 512)
    shared_n1.wait_recv()
    for i in range(2):
        lhs_n1[i] = dot(orders_ref[i], n1b[...], 1, 1).astype(BF16)
    relay()

    pieces = (
        (((0, 0, 256), (1024, 256, 128)), ((512, 0, 256), (1152, 256, 128))),
        (((256, 384, 128), (1280, 512, 128)), ((768, 384, 128),)),
        (((384, 640, 128),), ((896, 512, 128), (1408, 640, 128))),
    )

    def late_piece(h):
        for copy in shared_gm[h]:
            copy.wait_recv()
        for part, moves in zip(late, pieces[h]):
            for src, at, count in moves:
                part.multiply(lhs_n1.at[late.index(part)], gm, src, at, count)
            part.send_first(moves[0][1], sum(count for _, _, count in moves))

    shared_gm = []
    for g in range(4):
        for w in range(2):
            rows, (lq, lk, lv) = group(w, g)
            grad = head_stack(gctx[rows, lq])
            p = probs[4 * w + g]
            grad_p = dot(qkv[rows, lv], grad, 1, 1)
            grad_s = (p * (grad_p - jnp.sum(grad_p * p, axis=0, keepdims=True))).astype(BF16)
            gm[rows, lv] = dot(p.astype(BF16), grad).astype(BF16)
            gm[rows, lq] = (head_merge(dot(grad_s, qkv[rows, lk], 0, 0)) * 32 ** (-0.5)).astype(BF16)
            gm[rows, lk] = dot(grad_s, head_stack(qkv[rows, lq])).astype(BF16)
        if g < 2:
            relay()
        if g == 1:
            shared_gm.append([share(gm, 512 * j, 256) for j in range(3)])
        if g == 2:
            late_piece(0)
        if g >= 2:
            shared_gm.append([share(gm, 512 * j + 128 * g, 128) for j in range(3)])

    late_piece(1)
    grad_n1 = dot(gm[OWN], wqkv[...], 1, 1).astype(BF16)
    late_piece(2)
    for part in early[:2]:
        part.second_step()
    grad_in = gr[OWN].astype(F32) + norm_back(grad_n1.astype(F32), f32s[N1], cols[R1])
    for part in late:
        part.second_step()
    in_sent = return_home(3, grad_in.astype(BF16))
    early[2].second_step()
    for part in early[:2]:
        part.third_step()
    for part in late:
        part.third_step()
    early[2].third_step()
    out_stored = arrive_home(2, out_sent, out_hbm)
    gin_stored = arrive_home(3, in_sent, gin_hbm)
    copies.drain()
    for part in early:
        part.finish()
    for part in late:
        part.finish()
    out_stored.wait()
    gin_stored.wait()


def hand_over(*refs):
    count = len(refs) // 2
    for i in range(count):
        refs[count + i][...] = refs[i][...]


def on_device(tokens, cotangent, w_qkv, w_proj, w_fc1, w_fc2):
    vmem = pl.BlockSpec(memory_space=pltpu.VMEM)
    hbm = pl.BlockSpec(memory_space=pl.ANY)
    both = 2 * NT
    out, gin, wg = pl.pallas_call(
        block_kernel,
        out_shape=(
            jax.ShapeDtypeStruct((NT, D), BF16),
            jax.ShapeDtypeStruct((NT, D), BF16),
            jax.ShapeDtypeStruct((96, 128), F32),
        ),
        in_specs=[hbm] * 6,
        out_specs=(hbm, hbm, vmem),
        scratch_shapes=[
            [part_scratch(i, w) for i, w in enumerate(EARLY)],
            [part_scratch(i, w) for i, w in enumerate(LATE)],
            pltpu.VMEM((3, 256, D), BF16),
            pltpu.VMEM((D, 3 * D), BF16),
            pltpu.VMEM((D, D), BF16),
            pltpu.VMEM((D, 4 * D), BF16),
            pltpu.VMEM((4 * D, D), BF16),
            pltpu.VMEM((4, PACKED, D), BF16),
            pltpu.VMEM((4, PACKED, D), BF16),
            pltpu.VMEM((2, PACKED, NT), BF16),
            pltpu.VMEM((2, NT, PACKED), BF16),
            pltpu.VMEM((both, 4 * D), BF16),
            pltpu.VMEM((both, 4 * D), BF16),
            pltpu.VMEM((both, D), BF16),
            pltpu.VMEM((both, D), BF16),
            pltpu.VMEM((both, D), BF16),
            pltpu.VMEM((both, D), BF16),
            pltpu.VMEM((both, D), BF16),
            pltpu.VMEM((both, 3 * D), BF16),
            pltpu.VMEM((3, 256, both), BF16),
            pltpu.VMEM((256, both), BF16),
            pltpu.VMEM((256, both), BF16),
            pltpu.VMEM((256, both), BF16),
            pltpu.VMEM((NT, 3 * D), BF16),
            pltpu.VMEM((8, 144, 576), F32),
            pltpu.VMEM((144, 576), F32),
            pltpu.VMEM((NT, D), BF16),
            pltpu.VMEM((3, NT, D), F32),
            pltpu.VMEM((2, NT, 1), F32),
            pltpu.VMEM((4, NT, D), BF16),
            pltpu.SemaphoreType.DMA((192,)),
            pltpu.SemaphoreType.DMA((192,)),
            pltpu.SemaphoreType.DMA((8,)),
        ],
        compiler_params=pltpu.CompilerParams(
            collective_id=0, has_side_effects=True, vmem_limit_bytes=60 * 1024 * 1024
        ),
    )(tokens.reshape(NT, D), cotangent.reshape(NT, D), w_qkv, w_proj, w_fc1, w_fc2)
    out, gin, wg = pl.pallas_call(
        hand_over,
        out_shape=tuple(jax.ShapeDtypeStruct(v.shape, v.dtype) for v in (out, gin, wg)),
        in_specs=[vmem] * 3,
        out_specs=(vmem,) * 3,
    )(out, gin, wg)
    return out.reshape(tokens.shape), gin.reshape(tokens.shape), wg


def solution(mesh):
    return jax.shard_map(
        on_device,
        mesh=mesh,
        in_specs=(P(None, "lat", "lon", None), P(None, "lat", "lon", None), P(), P(), P(), P()),
        out_specs=(
            P(None, "lat", "lon", None),
            P(None, "lat", "lon", None),
            P(("lat", "lon"), None),
        ),
        check_vma=False,
    )
```
